32 devices in a mesh: dp: 4 (over y, x), seq: 8 (over z, core).
Axes of the slice: x: 2, y: 2, z: 4, core: 2. Of those that a mesh axis runs over, the one named last changes fastest.
Arguments:
- inputs: bfloat16 [2, 4, 2048, 768], P(None, 'dp', 'seq'), may hold values from -6 to 6
- offsets: int32 [2, 4, 2048], P(None, 'dp', 'seq'), may hold values from 0 to 2045, as said below
- w_query: bfloat16 [768, 768], P(('dp', 'seq')), may hold values from -0.21875 to 0.21875
- w_kv: bfloat16 [768, 128], P(('dp', 'seq')), may hold values from -0.21875 to 0.21875
- w_out: bfloat16 [768, 768], P(('dp', 'seq')), may hold values from -0.875 to 0.875
- w_up: bfloat16 [768, 3072], P(('dp', 'seq')), may hold values from -0.21875 to 0.21875
- w_down: bfloat16 [3072, 768], P(('dp', 'seq')), may hold values from -0.109375 to 0.109375
- b_up: bfloat16 [3072], P(('dp', 'seq')), may hold values from -1.5 to 1.5
- vectors: bfloat16 [7, 768], P(None, ('dp', 'seq')), may hold values from -1.5 to 1.5
- b_kv: bfloat16 [128], replicated, may hold values from -2.5 to 2.5
- cotangent: bfloat16 [2, 4, 2048, 768], P(None, 'dp', 'seq'), may hold values from -6 to 6
Outputs:
- out: bfloat16 [2, 4, 2048, 768], P(None, 'dp', 'seq')
- grad_inputs: float32 [2, 4, 2048, 768], P(None, 'dp', 'seq')
- grad_w_query: float32 [768, 768], P(('dp', 'seq'))
- grad_w_kv: float32 [768, 128], P(('dp', 'seq'))
- grad_w_out: float32 [768, 768], P(('dp', 'seq'))
- grad_w_up: float32 [768, 3072], P(('dp', 'seq'))
- grad_w_down: float32 [3072, 768], P(('dp', 'seq'))
- grad_b_up: float32 [3072], P(('dp', 'seq'))
- grad_vectors: float32 [7, 768], P(None, ('dp', 'seq'))
- grad_b_kv: float32 [128], replicated
The draws below stay inside these ranges and needn't reach their ends.
Inputs may be any that keep to these rules, and one draw needn't show every extreme that they name: Each sequence holds three documents end to end; offsets count 0, 1, 2, ... within each document; the first and the last document have 1 to 128 positions, and in some sequence of every draw both have exactly one.
All inputs are finite; a program needn't handle non-finite values.
Results may differ from the reference program's by a relative error of at most 0.011.
Values may be sent and summed in bfloat16 or wider, within the bound.
A program may use at most 128 MiB of HBM per device.

```python
import math
import jax
import jax.numpy as jnp
from jax import lax

D = 768
H = 12
HD = 64
FF = 3072
ROT = 16
MB = 2
SEQLEN = 2048
ROWS = 256
SEQS = 4


def draw_offsets(key, part):
    key = jax.random.fold_in(key, 1)
    first_key, last_key, pick_key = jax.random.split(key, 3)
    leading = jax.random.randint(first_key, (MB, SEQS, 1), 1, ROWS // 2 + 1, dtype=jnp.int32)
    trailing = jax.random.randint(last_key, (MB, SEQS, 1), 1, ROWS // 2 + 1, dtype=jnp.int32)
    chosen = jax.random.randint(pick_key, (), 0, MB * SEQS, dtype=jnp.int32)
    numbers = jnp.arange(MB * SEQS, dtype=jnp.int32).reshape(MB, SEQS, 1)
    leading = jnp.where(numbers == chosen, 1, leading).astype(jnp.int32)
    trailing = jnp.where(numbers == chosen, 1, trailing).astype(jnp.int32)
    places = jnp.arange(SEQLEN, dtype=jnp.int32)[None, None, :]
    middle_end = SEQLEN - trailing
    return jnp.where(places < leading, places, jnp.where(places < middle_end, places - leading, places - middle_end)).astype(jnp.int32)


def draw_vectors(key, part):
    key = jax.random.fold_in(key, 2)
    gain_key, shift_key = jax.random.split(key)
    gains = jax.random.uniform(gain_key, (7, D), jnp.float32, 0.5, 1.5)
    shifts = jnp.clip(0.3 * jax.random.normal(shift_key, (7, D), jnp.float32), -1.5, 1.5)
    row_numbers = jnp.arange(7)
    gain_rows = (row_numbers == 0) | (row_numbers == 2)
    return jnp.where(gain_rows[:, None], gains, shifts).astype(jnp.bfloat16)


def steps_of(rng, dims, cuts, least, largest):
    def one(dim, parts):
        heights = jax.random.uniform(jax.random.fold_in(jax.random.fold_in(rng, 6), dim), (parts,), jnp.float32, least / len(cuts), largest / len(cuts))
        return jnp.repeat(jnp.exp(heights), dims[dim] // parts).reshape((-1,) + (1,) * (len(dims) - dim - 1))

    loudness = one(*cuts[0])
    for cut in cuts[1:]:
        loudness = loudness * one(*cut)
    return loudness


def scatter_about(key, extent, scale, reach, pieces=(), kind=jnp.bfloat16):
    loudness = steps_of(key, extent, pieces, -0.22, 0.18) if pieces else 1.0
    values = jax.random.normal(key, extent, jnp.float32) * scale * loudness
    return jnp.minimum(jnp.maximum(values, -reach), reach).astype(kind)


def setup_inputs(seed: int = 0) -> dict:
    key_of = jax.random.split(jax.random.key(seed), 12)
    return {
        "inputs": scatter_about(key_of[0], (MB, SEQS, SEQLEN, D), 1.0, 6.0, ((1, 4), (2, 8))),
        "offsets": draw_offsets(jax.random.fold_in(key_of[11], 71), 0),
        "w_query": scatter_about(key_of[2], (D, D), D ** -0.5, 0.21875, ((0, 32),)),
        "w_kv": scatter_about(key_of[3], (D, 2 * HD), D ** -0.5, 0.21875, ((0, 32),)),
        "w_out": scatter_about(key_of[4], (D, D), (D // 16) ** -0.5, 0.875, ((0, 32),)),
        "w_up": scatter_about(key_of[5], (D, FF), D ** -0.5, 0.21875, ((0, 32),)),
        "w_down": scatter_about(key_of[6], (FF, D), FF ** -0.5, 0.109375, ((0, 32),)),
        "b_up": scatter_about(key_of[7], (FF,), 0.3, 1.5, ((0, 32),)),
        "vectors": draw_vectors(jax.random.fold_in(key_of[11], 71), 0),
        "b_kv": scatter_about(key_of[9], (2 * HD,), 0.5, 2.5),
        "cotangent": scatter_about(key_of[10], (MB, SEQS, SEQLEN, D), 1.0, 6.0, ((1, 4), (2, 8))),
    }


@jax.custom_vjp
def low(v):
    return lax.optimization_barrier(v.astype(jnp.bfloat16)).astype(jnp.float32)

@jax.custom_vjp
def low_back(v):
    return v

def low_keep(v):
    return (low(v), None)

def low_pass(kept, grad):
    return (grad,)

def back_keep(v):
    return (v, None)

def back_low(kept, grad):
    return (low(grad),)
low.defvjp(low_keep, low_pass)
low_back.defvjp(back_keep, back_low)
epsilon = 1e-05
masked_score = -1e+30
highest = lax.Precision.HIGHEST

def product(left, right):
    return jnp.dot(left, right, precision=highest)

def layer_norm(values, gain_row, shift_row):
    average = lax.optimization_barrier(jnp.mean(values, axis=-1, keepdims=True))
    centered = values - average
    return centered * lax.rsqrt(lax.optimization_barrier(jnp.mean(centered * centered, axis=-1, keepdims=True)) + epsilon) * gain_row + shift_row

def rotate(values, cosine, sine_part):
    half_rot = ROT // 2
    first_part = values[..., :half_rot]
    second = values[..., half_rot:ROT]
    return jnp.concatenate([first_part * cosine - second * sine_part, second * cosine + first_part * sine_part, values[..., ROT:]], axis=-1)

def sequence_layer(weight_set, values_in, row_offsets):
    w_query, w_kv, w_out, w_up, w_down, b_up, vectors, b_kv = weight_set
    half_rot = ROT // 2
    frequency = jnp.power(10000.0, -jnp.arange(half_rot, dtype=jnp.float32) * (2.0 / ROT))
    angle = (row_offsets.astype(jnp.float32) * 0.25)[:, None] * frequency[None, :]
    cosine = jnp.cos(angle)
    sine_part = jnp.sin(angle)
    normed1 = low(layer_norm(values_in, vectors[0], vectors[1]))
    query_pre = low_back(product(normed1, w_query) + vectors[4])
    kv_pre = low_back(product(normed1, w_kv) + b_kv)
    queries = low(rotate(query_pre.reshape(SEQLEN, H, HD), cosine[:, None, :], sine_part[:, None, :]))
    shared = low(jnp.concatenate([rotate(kv_pre[:, :HD], cosine, sine_part), kv_pre[:, HD:]], axis=1))
    query_block = math.gcd(SEQLEN, 512)
    block_count = SEQLEN // query_block
    columns = jnp.arange(SEQLEN, dtype=jnp.int32)

    def attend(block_args):
        block_queries, block_offsets, block_rows = block_args
        scores = jnp.einsum('rhd,kd->hrk', block_queries, shared[:, :HD], precision=highest) * 0.125
        scores = low_back(scores)
        allowed = (columns[None, :] <= block_rows[:, None]) & (block_rows[:, None] - columns[None, :] <= block_offsets[:, None])
        scores = jnp.where(allowed[None], scores, masked_score)
        highest_score = lax.optimization_barrier(jnp.max(scores, axis=-1, keepdims=True))
        exponent_terms = jnp.exp(scores - highest_score)
        soft_weights = low(exponent_terms / lax.optimization_barrier(jnp.sum(exponent_terms, axis=-1, keepdims=True)))
        return jnp.einsum('hrk,kd->rhd', soft_weights, shared[:, HD:], precision=highest)
    attended = lax.map(jax.checkpoint(attend), (queries.reshape(block_count, query_block, H, HD), row_offsets.reshape(block_count, query_block), columns.reshape(block_count, query_block)))
    attended = low(low_back(attended.reshape(SEQLEN, D)))
    attn_out = product(attended, w_out) + vectors[5]
    normed2 = low(layer_norm(values_in, vectors[2], vectors[3]))
    hidden = low_back(product(normed2, w_up) + b_up)
    activated = low(jax.nn.gelu(hidden, approximate=False))
    mlp_out = product(activated, w_down) + vectors[6]
    return values_in + attn_out + mlp_out

def reference(inputs, offsets, w_query, w_kv, w_out, w_up, w_down, b_up, vectors, b_kv, cotangent):
    weight_set = (w_query.astype(jnp.float32), w_kv.astype(jnp.float32), w_out.astype(jnp.float32), w_up.astype(jnp.float32), w_down.astype(jnp.float32), b_up.astype(jnp.float32), vectors.astype(jnp.float32), b_kv.astype(jnp.float32))
    seq_count = MB * SEQS
    flat_inputs = inputs.astype(jnp.float32).reshape(seq_count, SEQLEN, D)
    flat_offsets = offsets.reshape(seq_count, SEQLEN)

    def forward(weights_in, values):
        return lax.map(lambda pair: sequence_layer(weights_in, pair[0], pair[1]), (values, flat_offsets))
    result, pullback = jax.vjp(forward, weight_set, flat_inputs)
    grad_weights, grad_values = pullback(cotangent.astype(jnp.float32).reshape(seq_count, SEQLEN, D))
    full_shape = (MB, SEQS, SEQLEN, D)
    return (result.reshape(full_shape).astype(jnp.bfloat16), grad_values.reshape(full_shape), grad_weights[0], grad_weights[1], grad_weights[2], grad_weights[3], grad_weights[4], grad_weights[5], grad_weights[6], grad_weights[7])
```

```python
import functools
import math

import jax
import jax.numpy as jnp
from jax import lax
from jax.experimental import pallas as pl
from jax.experimental.pallas import tpu as pltpu
from jax.sharding import PartitionSpec as P

H = 12
HD = 64
ROT = 16


epsilon = 1e-05
root_half = 0.7071067811865476
density_scale = 0.3989422804014327
masked_score = -1e30


def normalize(values):
    average = jnp.mean(values, axis=-1, keepdims=True)
    centered = values - average
    inverse = lax.rsqrt(jnp.mean(centered * centered, axis=-1, keepdims=True) + epsilon)
    return (centered * inverse, inverse)


def norm_back(grad_out, normed, inverse, gain_row):
    scaled = grad_out * gain_row
    first_mean = jnp.mean(scaled, axis=-1, keepdims=True)
    second_mean = jnp.mean(scaled * normed, axis=-1, keepdims=True)
    return inverse * (scaled - first_mean - normed * second_mean)


def rotate(values, cosine, sine_part):
    half_rot = ROT // 2
    first_part = values[..., :half_rot]
    second = values[..., half_rot:ROT]
    return jnp.concatenate(
        [
            first_part * cosine - second * sine_part,
            second * cosine + first_part * sine_part,
            values[..., ROT:],
        ],
        axis=-1,
    )


def gelu_slope(hidden):
    return 0.5 * (1.0 + lax.erf(hidden * root_half)) + hidden * density_scale * jnp.exp(
        -0.5 * hidden * hidden
    )


def tree_add(left_tree, right_tree):
    return tuple((left_item + right_item for left_item, right_item in zip(left_tree, right_tree)))


def plain_on_device(inputs, offsets, w_query, w_kv, w_out, w_up, w_down, b_up, vectors, b_kv, cotangent):
    micro_count = inputs.shape[0]
    local_rows = inputs.shape[2]
    model_width = inputs.shape[3]
    seqlen = local_rows * lax.axis_size("seq")
    key_block = math.gcd(seqlen, 512)
    first_row = lax.axis_index("seq") * local_rows
    blocks_used = (first_row + local_rows + key_block - 1) // key_block
    row_ids = first_row + jnp.arange(local_rows, dtype=jnp.int32)
    half_rot = ROT // 2
    frequency = jnp.power(10000.0, -jnp.arange(half_rot, dtype=jnp.float32) * (2.0 / ROT))
    kv_bias = b_kv.astype(jnp.float32)
    results = []
    input_grads = []
    totals = None
    kv_bias_total = jnp.zeros(b_kv.shape, jnp.float32)
    for micro_index in range(micro_count):
        values_in = inputs[micro_index, 0].astype(jnp.float32)
        row_offsets = offsets[micro_index, 0]
        upstream = cotangent[micro_index, 0]
        upstream_f = upstream.astype(jnp.float32)
        angle = (row_offsets.astype(jnp.float32) * 0.25)[:, None] * frequency[None, :]
        cosine = jnp.cos(angle)
        sine_part = jnp.sin(angle)
        gathered = (
            lax.all_gather(w_query, ("dp", "seq"), axis=0, tiled=True),
            lax.all_gather(w_kv, ("dp", "seq"), axis=0, tiled=True),
            lax.all_gather(w_out, ("dp", "seq"), axis=0, tiled=True),
            lax.all_gather(w_up, ("dp", "seq"), axis=0, tiled=True),
            lax.all_gather(w_down, ("dp", "seq"), axis=0, tiled=True),
            lax.all_gather(b_up, ("dp", "seq"), axis=0, tiled=True),
            lax.all_gather(vectors, ("dp", "seq"), axis=1, tiled=True),
        )
        query_full, kv_full, out_full, up_full, down_full, up_bias, vector_full = gathered
        vector_f = vector_full.astype(jnp.float32)
        normed1, inverse1 = normalize(values_in)
        hidden1 = (normed1 * vector_f[0] + vector_f[1]).astype(jnp.bfloat16)
        query_pre = jnp.dot(hidden1, query_full, preferred_element_type=jnp.float32) + vector_f[4]
        kv_pre = jnp.dot(hidden1, kv_full, preferred_element_type=jnp.float32) + kv_bias
        queries = rotate(
            query_pre.reshape(local_rows, H, HD), cosine[:, None, :], sine_part[:, None, :]
        ).astype(jnp.bfloat16)
        shared_local = jnp.concatenate(
            [rotate(kv_pre[:, :HD], cosine, sine_part), kv_pre[:, HD:]], axis=1
        ).astype(jnp.bfloat16)
        shared = lax.all_gather(shared_local, "seq", axis=0, tiled=True)

        def block_scores(number):
            start_row = number * key_block
            key_piece = lax.dynamic_slice_in_dim(shared, start_row, key_block, 0)
            columns = start_row + jnp.arange(key_block, dtype=jnp.int32)
            allowed = (columns[None, :] <= row_ids[:, None]) & (
                row_ids[:, None] - columns[None, :] <= row_offsets[:, None]
            )
            scores = (
                jnp.einsum(
                    "rhd,kd->hrk", queries, key_piece[:, :HD], preferred_element_type=jnp.float32
                )
                * 0.125
            )
            return (jnp.where(allowed[None], scores, masked_score), key_piece)

        def max_step(number, state_pair):
            running_top, denominator = state_pair
            scores, key_piece = block_scores(number)
            new_top = jnp.maximum(running_top, jnp.max(scores, axis=-1))
            denominator = denominator * jnp.exp(running_top - new_top) + jnp.sum(
                jnp.exp(scores - new_top[..., None]), axis=-1
            )
            return (new_top, denominator)

        start_top = jnp.full((H, local_rows), masked_score, jnp.float32)
        running_top, denominator = lax.fori_loop(
            0, blocks_used, max_step, (start_top, jnp.zeros((H, local_rows), jnp.float32))
        )
        log_total = running_top + jnp.log(denominator)

        def value_step(number, accumulated):
            scores, key_piece = block_scores(number)
            soft_weights = jnp.exp(scores - log_total[..., None]).astype(jnp.bfloat16)
            return accumulated + jnp.einsum(
                "hrk,kd->rhd", soft_weights, key_piece[:, HD:], preferred_element_type=jnp.float32
            )

        attended_f = lax.fori_loop(
            0, blocks_used, value_step, jnp.zeros((local_rows, H, HD), jnp.float32)
        )
        attended = attended_f.reshape(local_rows, model_width).astype(jnp.bfloat16)
        attn_out = jnp.dot(attended, out_full, preferred_element_type=jnp.float32) + vector_f[5]
        normed2, inverse2 = normalize(values_in)
        hidden2 = (normed2 * vector_f[2] + vector_f[3]).astype(jnp.bfloat16)
        hidden_up = jnp.dot(hidden2, up_full, preferred_element_type=jnp.float32) + up_bias.astype(
            jnp.float32
        )
        activated = jax.nn.gelu(hidden_up, approximate=False).astype(jnp.bfloat16)
        mlp_out = jnp.dot(activated, down_full, preferred_element_type=jnp.float32) + vector_f[6]
        results.append((values_in + attn_out + mlp_out).astype(jnp.bfloat16))
        regathered = (
            lax.all_gather(w_query, ("dp", "seq"), axis=0, tiled=True),
            lax.all_gather(w_kv, ("dp", "seq"), axis=0, tiled=True),
            lax.all_gather(w_out, ("dp", "seq"), axis=0, tiled=True),
            lax.all_gather(w_up, ("dp", "seq"), axis=0, tiled=True),
            lax.all_gather(w_down, ("dp", "seq"), axis=0, tiled=True),
            lax.all_gather(b_up, ("dp", "seq"), axis=0, tiled=True),
            lax.all_gather(vectors, ("dp", "seq"), axis=1, tiled=True),
        )
        query_back, kv_back, out_back, up_back, down_back, up_bias_back, vector_back = regathered
        vector_back_f = vector_back.astype(jnp.float32)
        grad_w_down = jnp.einsum(
            "rf,rd->fd", activated, upstream, preferred_element_type=jnp.float32
        )
        d_act = jnp.einsum("rd,fd->rf", upstream, down_back, preferred_element_type=jnp.float32)
        d_hidden = (d_act * gelu_slope(hidden_up)).astype(jnp.bfloat16)
        grad_w_up = jnp.einsum("rd,rf->df", hidden2, d_hidden, preferred_element_type=jnp.float32)
        grad_b_up = jnp.sum(d_hidden.astype(jnp.float32), axis=0)
        d_normed2 = jnp.einsum("rf,df->rd", d_hidden, up_back, preferred_element_type=jnp.float32)
        grad_w_out = jnp.einsum("rd,re->de", attended, upstream, preferred_element_type=jnp.float32)
        d_attended = (
            jnp.einsum("re,de->rd", upstream, out_back, preferred_element_type=jnp.float32)
            .astype(jnp.bfloat16)
            .reshape(local_rows, H, HD)
        )

        def delta_step(number, accumulated):
            scores, key_piece = block_scores(number)
            soft_probs = jnp.exp(scores - log_total[..., None])
            d_probs = jnp.einsum(
                "rhd,kd->hrk", d_attended, key_piece[:, HD:], preferred_element_type=jnp.float32
            )
            return accumulated + jnp.sum(soft_probs * d_probs, axis=-1)

        delta = lax.fori_loop(0, blocks_used, delta_step, jnp.zeros((H, local_rows), jnp.float32))

        def grad_step(number, state_pair):
            d_query_rot, d_shared_all = state_pair
            start_row = number * key_block
            scores, key_piece = block_scores(number)
            soft_probs = jnp.exp(scores - log_total[..., None])
            d_probs = jnp.einsum(
                "rhd,kd->hrk", d_attended, key_piece[:, HD:], preferred_element_type=jnp.float32
            )
            d_scores = (soft_probs * (d_probs - delta[..., None])).astype(jnp.bfloat16)
            d_query_rot = (
                d_query_rot
                + jnp.einsum(
                    "hrk,kd->rhd", d_scores, key_piece[:, :HD], preferred_element_type=jnp.float32
                )
                * 0.125
            )
            d_keys = (
                jnp.einsum("hrk,rhd->kd", d_scores, queries, preferred_element_type=jnp.float32)
                * 0.125
            )
            d_values = jnp.einsum(
                "hrk,rhd->kd",
                soft_probs.astype(jnp.bfloat16),
                d_attended,
                preferred_element_type=jnp.float32,
            )
            current = lax.dynamic_slice_in_dim(d_shared_all, start_row, key_block, 0)
            d_shared_all = lax.dynamic_update_slice_in_dim(
                d_shared_all, current + jnp.concatenate([d_keys, d_values], axis=1), start_row, 0
            )
            return (d_query_rot, d_shared_all)

        d_query_rot, d_shared_all = lax.fori_loop(
            0,
            blocks_used,
            grad_step,
            (jnp.zeros((local_rows, H, HD), jnp.float32), jnp.zeros((seqlen, 2 * HD), jnp.float32)),
        )
        d_shared_mine = lax.psum_scatter(
            d_shared_all.astype(jnp.bfloat16), "seq", scatter_dimension=0, tiled=True
        ).astype(jnp.float32)
        d_shared = jnp.concatenate(
            [rotate(d_shared_mine[:, :HD], cosine, -sine_part), d_shared_mine[:, HD:]], axis=1
        ).astype(jnp.bfloat16)
        d_queries = (
            rotate(d_query_rot, cosine[:, None, :], -sine_part[:, None, :])
            .reshape(local_rows, model_width)
            .astype(jnp.bfloat16)
        )
        grad_w_query = jnp.einsum(
            "rd,re->de", hidden1, d_queries, preferred_element_type=jnp.float32
        )
        grad_w_kv = jnp.einsum("rd,rc->dc", hidden1, d_shared, preferred_element_type=jnp.float32)
        kv_bias_total = kv_bias_total + jnp.sum(d_shared.astype(jnp.float32), axis=0)
        d_normed1 = jnp.einsum(
            "re,de->rd", d_queries, query_back, preferred_element_type=jnp.float32
        ) + jnp.einsum("rc,dc->rd", d_shared, kv_back, preferred_element_type=jnp.float32)
        upstream_sum = jnp.sum(upstream_f, axis=0)
        grad_vectors = jnp.stack(
            [
                jnp.sum(d_normed1 * normed1, axis=0),
                jnp.sum(d_normed1, axis=0),
                jnp.sum(d_normed2 * normed2, axis=0),
                jnp.sum(d_normed2, axis=0),
                jnp.sum(d_queries.astype(jnp.float32), axis=0),
                upstream_sum,
                upstream_sum,
            ]
        )
        input_grads.append(
            upstream_f
            + norm_back(d_normed1, normed1, inverse1, vector_back_f[0])
            + norm_back(d_normed2, normed2, inverse2, vector_back_f[2])
        )
        shares = (
            lax.psum_scatter(grad_w_query, ("dp", "seq"), scatter_dimension=0, tiled=True),
            lax.psum_scatter(grad_w_kv, ("dp", "seq"), scatter_dimension=0, tiled=True),
            lax.psum_scatter(grad_w_out, ("dp", "seq"), scatter_dimension=0, tiled=True),
            lax.psum_scatter(grad_w_up, ("dp", "seq"), scatter_dimension=0, tiled=True),
            lax.psum_scatter(grad_w_down, ("dp", "seq"), scatter_dimension=0, tiled=True),
            lax.psum_scatter(grad_b_up, ("dp", "seq"), scatter_dimension=0, tiled=True),
            lax.psum_scatter(grad_vectors, ("dp", "seq"), scatter_dimension=1, tiled=True),
        )
        totals = shares if totals is None else tree_add(totals, shares)
    kv_bias_grad = lax.psum(kv_bias_total, ("dp", "seq"))
    return (
        jnp.stack(results)[:, None],
        jnp.stack(input_grads)[:, None],
        totals[0],
        totals[1],
        totals[2],
        totals[3],
        totals[4],
        totals[5],
        totals[6],
        kv_bias_grad,
    )


MESH = pl.DeviceIdType.MESH
NT = (((1,), (1,)), ((), ()))
VM = pl.BlockSpec(memory_space=pltpu.VMEM)
HBM = pl.BlockSpec(memory_space=pl.ANY)
GROUP = 4
KEYS = 512
MINI = 256
scale_log2 = 0.125 * 1.4426950408889634


def dot(left, right):
    return jnp.dot(left, right, preferred_element_type=jnp.float32)


def dot_nt(left, right):
    return lax.dot_general(left, right, NT, preferred_element_type=jnp.float32)


def bf(values):
    return values.astype(jnp.bfloat16)


def f32(values):
    return values.astype(jnp.float32)


def rotate_rows(block, cosine, sine_part):
    half_rot = ROT // 2
    first, second = block[:half_rot], block[half_rot:ROT]
    return jnp.concatenate(
        [first * cosine - second * sine_part, second * cosine + first * sine_part, block[ROT:]],
        axis=0,
    )


def here():
    return lax.axis_index("dp"), lax.axis_index("seq")


def greet(targets):
    barrier = pltpu.get_barrier_semaphore()
    for target in targets:
        pl.semaphore_signal(barrier, inc=1, device_id=target, device_id_type=MESH)
    pl.semaphore_wait(barrier, len(targets))


def remote(source, target, send, recv, device):
    return pltpu.make_async_remote_copy(
        src_ref=source,
        dst_ref=target,
        send_sem=send,
        recv_sem=recv,
        device_id=device,
        device_id_type=MESH,
    )


class Gather:
    def __init__(self, shard, slabs, halves, send, recv):
        self.shard, self.slabs, self.halves, self.send, self.recv = shard, slabs, halves, send, recv
        self.dp, self.seq = here()
        self.sent = []

    def index(self, dp_flip, z_flip, core_flip=0):
        return (self.dp ^ dp_flip) * 8 + (self.seq ^ (2 * z_flip + core_flip))

    def part(self, slab, half):
        rows, columns = half
        return self.slabs.at[slab, rows, columns]

    def start(self, number, source, target, device):
        copy = remote(source, target, self.send.at[number], self.recv.at[number], device)
        copy.start()
        self.sent.append(copy)

    def arrived(self, number, target):
        remote(target, target, self.send.at[number], self.recv.at[number], (self.dp, self.seq ^ 1)).wait_recv()

    def own(self):
        mine = self.slabs.at[self.index(0, 0)]
        for flip in (1, 2, 3):
            self.start(flip - 1, self.shard, mine, (self.dp, self.seq ^ (2 * flip)))
        self.start(3, self.shard, mine, (self.dp ^ 1, self.seq))
        self.start(7, self.shard, mine, (self.dp ^ 2, self.seq))
        self.start(19, self.shard, mine, (self.dp, self.seq ^ 1))

    def from_z(self, flip):
        piece = self.slabs.at[self.index(0, flip)]
        self.arrived(flip - 1, piece)
        self.start(3 + flip, piece, piece, (self.dp ^ 1, self.seq))
        self.start(7 + flip, piece, piece, (self.dp ^ 2, self.seq))
        self.start(19 + flip, piece, piece, (self.dp, self.seq ^ 1))

    def from_xy(self, flip):
        for axis, half in ((1, 0), (2, 1)):
            number = 3 if axis == 1 else 7
            slab = self.index(axis, flip)
            piece = self.slabs.at[slab]
            self.arrived(number + flip, piece)
            cut = self.part(slab, self.halves[half])
            self.start(11 + 4 * half + flip, cut, cut, (self.dp ^ (3 - axis), self.seq))
            self.start((23 if axis == 1 else 27) + flip, piece, piece, (self.dp, self.seq ^ 1))

    def from_diagonal(self, flip):
        slab = self.index(3, flip)
        for half in (0, 1):
            self.arrived(11 + 4 * half + flip, self.part(slab, self.halves[half]))
        piece = self.slabs.at[slab]
        self.start(31 + flip, piece, piece, (self.dp, self.seq ^ 1))

    def from_core(self):
        for number, dp_flip in ((19, 0), (23, 1), (27, 2), (31, 3)):
            for flip in range(4):
                self.arrived(number + flip, self.slabs.at[self.index(dp_flip, flip, 1)])

    def finish(self):
        for copy in self.sent:
            copy.wait_send()


def attend(
    micro, steps, row0, begin_ref, q_t, do_t, kv_ref, kv_t, att_t, dq_t, dkv, pair, scaled, score_ref, weight_ref, tick
):
    cols = slice(micro * MINI, (micro + 1) * MINI)
    begin = begin_ref[0:1, cols]
    row_ids = row0 + lax.broadcasted_iota(jnp.int32, (1, MINI), 1)
    for group in range(H // GROUP):
        heads = [slice((group * GROUP + n) * HD, (group * GROUP + n + 1) * HD) for n in range(GROUP)]
        for n, head in enumerate(heads):
            pair[n, :HD, :MINI] = q_t[head, cols]
            pair[n, HD:, MINI:] = do_t[head, cols]

        def score_step(step, tops):
            keys = pl.ds(pl.multiple_of(step * KEYS, KEYS), KEYS)
            block = kv_ref[micro, keys, :]
            ids = step * KEYS + lax.broadcasted_iota(jnp.int32, (KEYS, 1), 0)
            allowed = (ids <= row_ids) & (ids >= begin)
            found = []
            for n in range(GROUP):
                both = dot(block, pair[n])
                scores = jnp.where(allowed, both[:, :MINI] * scale_log2, masked_score)
                score_ref[n, keys, :MINI] = scores
                score_ref[n, keys, MINI:] = both[:, MINI:]
                found.append(jnp.maximum(tops[n], jnp.max(scores.reshape(KEYS // 8, 8, MINI), axis=0)))
            return tuple(found)

        tops = lax.fori_loop(
            0, steps, score_step, tuple(jnp.full((8, MINI), masked_score, jnp.float32) for _ in heads)
        )
        tops = [jnp.max(top, axis=0, keepdims=True) for top in tops]

        def value_step(step, carried):
            keys = pl.ds(pl.multiple_of(step * KEYS, KEYS), KEYS)
            values = kv_t[micro, HD:, keys]
            found = []
            for n in range(GROUP):
                output, total = carried[n]
                weights = jnp.exp2(score_ref[n, keys, :MINI] - tops[n])
                total = total + jnp.sum(weights.reshape(KEYS // 8, 8, MINI), axis=0)
                weight_ref[n, keys, :] = bf(weights)
                found.append((output + dot(values, bf(weights)), total))
            return tuple(found)

        sums = lax.fori_loop(
            0,
            steps,
            value_step,
            tuple((jnp.zeros((HD, MINI), jnp.float32), jnp.zeros((8, MINI), jnp.float32)) for _ in heads),
        )
        inverses, deltas = [], []
        for n, head in enumerate(heads):
            inverse = 1.0 / jnp.sum(sums[n][1], axis=0, keepdims=True)
            output = sums[n][0] * inverse
            upstream = f32(do_t[head, cols])
            deltas.append(jnp.sum(output * upstream, axis=0, keepdims=True))
            inverses.append(inverse)
            att_t[head, cols] = bf(output)
            scaled[n, :HD, :MINI] = bf(f32(q_t[head, cols]) * inverse)
            scaled[n, HD:, MINI:] = bf(upstream * inverse)

        def grad_step(step, carried):
            keys = pl.ds(pl.multiple_of(step * KEYS, KEYS), KEYS)
            key_block = kv_t[micro, :HD, keys]
            total = dkv[micro, keys, :]
            found = []
            for n in range(GROUP):
                weights = weight_ref[n, keys, :]
                d_scores = bf(f32(weights) * (score_ref[n, keys, MINI:] - deltas[n]))
                found.append(carried[n] + dot(key_block, d_scores))
                total = total + dot_nt(d_scores, scaled[n, :, :MINI])
                total = total + dot_nt(weights, scaled[n, :, MINI:])
            dkv[micro, keys, :] = total
            return tuple(found)

        grads = lax.fori_loop(
            0, steps, grad_step, tuple(jnp.zeros((HD, MINI), jnp.float32) for _ in heads)
        )
        for n, head in enumerate(heads):
            dq_t[head, cols] = grads[n] * (inverses[n] * 0.125)
        tick(micro, group)


def spread(slabs):
    lane = lax.broadcasted_iota(jnp.int32, (8, 128), 1)
    row = lax.broadcasted_iota(jnp.int32, (8, 128), 0)
    rows = [jnp.zeros((8, 128), jnp.float32) for _ in range(6)]
    wide = [jnp.zeros((8, 128), jnp.float32) for _ in range(24)]
    for number in range(32):
        for width, target, keep in ((24, rows, row < 7), (96, wide, row == 7)):
            block, shift = divmod(number * width, 128)
            piece = jnp.where(keep, slabs[number], 0.0)
            piece = pltpu.roll(piece, shift, 1) if shift else piece
            target[block] = target[block] + jnp.where(lane >= shift, piece, 0.0)
            if shift + width > 128:
                target[block + 1] = target[block + 1] + jnp.where(lane < shift, piece, 0.0)
    return jnp.concatenate(rows, axis=1), jnp.concatenate(wide, axis=1)


def slab_order(store, block, dp_index, rows):
    for z in range(4):
        for core in range(2):
            first = (2 * z + core) * rows
            store(dp_index, core, z, bf(block[first : first + rows]))


def attention_kernel(
    x_ref, cot_ref, begin_ref, cos_ref, sin_ref, bkv_ref, small_ref, up_ref, down_ref,
    up_slabs, down_slabs, vec_ref, bup_ref, wkv_ref, attn_ref, dn_ref, dkv_out, grads_ref, dqsum_ref,
    slabs, weights, n1_ref, n1t_ref, q_t, do_t, att_t, dq_t, kv_ref, kv_t, dkv, pair, scaled, score_ref, weight_ref,
    send_a, recv_a, send_u, recv_u, send_d, recv_d, send_kv, recv_kv, local_sem,
):
    dp, seq = here()
    wide = slabs.shape[2] // 2
    gather_a = Gather(small_ref, slabs, ((slice(None), slice(0, wide)), (slice(None), slice(wide, 2 * wide))), send_a, recv_a)
    half = up_ref.shape[1] // 2
    gather_u = Gather(up_ref, up_slabs, ((slice(None), slice(0, half)), (slice(None), slice(half, 2 * half))), send_u, recv_u)
    half = down_ref.shape[0] // 2
    gather_d = Gather(down_ref, down_slabs, ((slice(0, half), slice(None)), (slice(half, 2 * half), slice(None))), send_d, recv_d)
    greet(
        [(dp, seq ^ 1), (dp, seq ^ 2), (dp, seq ^ 4), (dp, seq ^ 6), (dp ^ 1, seq), (dp ^ 2, seq)]
    )
    gather_a.own()
    mine = gather_a.index(0, 0)
    local_copies = [
        pltpu.make_async_copy(small_ref, slabs.at[mine], local_sem.at[0]),
        pltpu.make_async_copy(up_ref, up_slabs.at[mine], local_sem.at[1]),
        pltpu.make_async_copy(down_ref, down_slabs.at[mine], local_sem.at[2]),
    ]
    for copy in local_copies:
        copy.start()
    pair[...] = jnp.zeros_like(pair)
    scaled[...] = jnp.zeros_like(scaled)
    dkv[...] = jnp.zeros_like(dkv)
    normed, _ = normalize(f32(x_ref[...]))
    for flip in (1, 2, 3):
        gather_a.from_z(flip)
    for flip in range(4):
        gather_a.from_xy(flip)
    for flip in range(4):
        gather_a.from_diagonal(flip)
    gather_a.from_core()
    local_copies[0].wait()

    for number in range(16):
        block = jnp.concatenate([f32(slabs[2 * number]), f32(slabs[2 * number + 1])], axis=0)
        weights[48 * number : 48 * number + 48, :] = bf(block)
    vectors, wide_row = spread([f32(slabs[number, 0:8, 896:1024]) for number in range(32)])
    vec_ref[...] = vectors
    bup_ref[...] = wide_row[7:8]
    wkv_ref[...] = weights[:, 768:896]

    hidden = bf(normed * vectors[0:1] + vectors[1:2])
    n1_ref[...] = hidden
    kv_pre = dot(hidden, weights[:, 768:896]) + bkv_ref[...]
    kv_pre_t = kv_pre.T
    cosine, sine_part = cos_ref[...], sin_ref[...]
    shared_t = bf(jnp.concatenate([rotate_rows(kv_pre_t[:HD], cosine, sine_part), kv_pre_t[HD:]], axis=0))
    shared = bf(f32(shared_t).T)
    place = pl.ds(pl.multiple_of(seq * MINI, MINI), MINI)
    kv_copies = []
    for micro in range(2):
        kv_ref[micro, place, :] = shared[micro * MINI : (micro + 1) * MINI]

    def kv_block(micro, flip):
        return kv_ref.at[micro, pl.ds(pl.multiple_of((seq ^ flip) * MINI, MINI), MINI)]

    def kv_send(micro, flip, number, device):
        block = kv_block(micro, flip)
        copy = remote(block, block, send_kv.at[micro, number], recv_kv.at[micro, number], device)
        copy.start()
        kv_copies.append(copy)

    def kv_arrived(micro, flip, number):
        block = kv_block(micro, flip)
        remote(block, block, send_kv.at[micro, number], recv_kv.at[micro, number], (dp, seq ^ 1)).wait_recv()

    for micro in range(2):
        for flip in (1, 2, 3):
            kv_send(micro, 0, flip - 1, (dp, seq ^ (2 * flip)))
        kv_send(micro, 0, 3, (dp, seq ^ 1))
    gather_u.own()
    gather_d.own()

    n1t_ref[...] = bf(f32(hidden).T)
    query = (dot(hidden, weights[:, :768]) + vectors[4:5]).T
    for head in range(H):
        q_t[head * HD : (head + 1) * HD, :] = bf(
            rotate_rows(query[head * HD : (head + 1) * HD], cosine, sine_part)
        )
    do_t[...] = bf(dot_nt(weights[:, 1024:1792], cot_ref[...]))

    def kv_forward(micro):
        for flip in (1, 2, 3):
            kv_arrived(micro, 2 * flip, flip - 1)
            kv_send(micro, 2 * flip, 3 + flip, (dp, seq ^ 1))

    def kv_finish(micro):
        for flip in range(4):
            kv_arrived(micro, 2 * flip + 1, 3 + flip)
        kv_t[micro] = bf(f32(kv_ref[micro]).T)

    kv_forward(0)
    kv_forward(1)
    kv_finish(0)

    def tick(micro, group):
        at = micro * (H // GROUP) + group
        if at == 0:
            gather_u.from_z(1)
            gather_d.from_z(1)
        if at == 1:
            gather_u.from_z(2)
            gather_d.from_z(2)
            gather_u.from_z(3)
            gather_d.from_z(3)
        if at == 2:
            for flip in (0, 1):
                gather_u.from_xy(flip)
                gather_d.from_xy(flip)
        if at == 3:
            for flip in (2, 3):
                gather_u.from_xy(flip)
                gather_d.from_xy(flip)
        if at == 4:
            for flip in range(4):
                gather_u.from_diagonal(flip)
                gather_d.from_diagonal(flip)

    steps = lax.div((seq + 1) * MINI + KEYS - 1, KEYS)
    for micro in range(2):
        if micro == 1:
            kv_finish(1)
        attend(
            micro, steps, seq * MINI, begin_ref, q_t, do_t, kv_ref, kv_t, att_t, dq_t, dkv,
            pair, scaled, score_ref, weight_ref, tick,
        )
    for micro in range(2):
        for core in range(2):
            for z in range(4):
                first = (2 * z + core) * MINI
                block = dkv[micro, first : first + MINI, :]
                scale = jnp.where(lax.broadcasted_iota(jnp.int32, (1, 2 * HD), 1) < HD, 0.125, 1.0)
                dkv_out[core, z, micro] = bf(block * scale)
    attn_ref[...] = dot(bf(f32(att_t[...]).T), weights[:, 1024:1792]) + vectors[5:6]
    for head in range(H):
        dq_t[head * HD : (head + 1) * HD, :] = rotate_rows(
            dq_t[head * HD : (head + 1) * HD, :], cosine, -sine_part
        )
    d_query = bf(dq_t[...].T)
    dqsum_ref[...] = jnp.sum(f32(d_query), axis=0, keepdims=True)
    dn_ref[...] = dot_nt(d_query, weights[:, :768])
    for block in range(4):
        rows = slice(192 * block, 192 * block + 192)

        def put_query(dp_index, core, z, piece):
            grads_ref[dp_index, core, z, :, 0:768] = piece

        def put_out(dp_index, core, z, piece):
            grads_ref[dp_index, core, z, :, 768:1536] = piece

        slab_order(put_query, dot(n1t_ref[rows, :], d_query), block, 24)
        slab_order(put_out, dot(att_t[rows, :], cot_ref[...]), block, 24)
    for gather in (gather_u, gather_d):
        gather.from_core()
    for gather in (gather_a, gather_u, gather_d):
        gather.finish()
    for copy in kv_copies:
        copy.wait_send()
    for copy in local_copies[1:]:
        copy.wait()


def attention_call(x, cot, begin, cosine, sine_part, b_kv, small, w_up, w_down):
    rows = x.shape[0]
    dma = pltpu.SemaphoreType.DMA
    out = lambda shape, kind: jax.ShapeDtypeStruct(shape, kind)
    seqlen = 8 * MINI
    return pl.pallas_call(
        attention_kernel,
        out_shape=(
            out((32,) + w_up.shape, jnp.bfloat16),
            out((32,) + w_down.shape, jnp.bfloat16),
            out((8, 768), jnp.float32),
            out((1, 3072), jnp.float32),
            out((768, 128), jnp.bfloat16),
            out((rows, 768), jnp.float32),
            out((rows, 768), jnp.float32),
            out((2, 4, 2, MINI, 2 * HD), jnp.bfloat16),
            out((4, 2, 4, 24, 1536), jnp.bfloat16),
            out((1, 768), jnp.float32),
        ),
        in_specs=[VM] * 7 + [HBM] * 2,
        out_specs=(HBM, HBM) + (VM,) * 8,
        scratch_shapes=[
            pltpu.VMEM((32,) + small.shape, jnp.bfloat16),
            pltpu.VMEM((768, small.shape[1]), jnp.bfloat16),
            pltpu.VMEM((rows, 768), jnp.bfloat16),
            pltpu.VMEM((768, rows), jnp.bfloat16),
            pltpu.VMEM((768, rows), jnp.bfloat16),
            pltpu.VMEM((768, rows), jnp.bfloat16),
            pltpu.VMEM((768, rows), jnp.bfloat16),
            pltpu.VMEM((768, rows), jnp.float32),
            pltpu.VMEM((2, seqlen, 2 * HD), jnp.bfloat16),
            pltpu.VMEM((2, 2 * HD, seqlen), jnp.bfloat16),
            pltpu.VMEM((2, seqlen, 2 * HD), jnp.float32),
            pltpu.VMEM((GROUP, 2 * HD, 2 * MINI), jnp.bfloat16),
            pltpu.VMEM((GROUP, 2 * HD, 2 * MINI), jnp.bfloat16),
            pltpu.VMEM((GROUP, seqlen, 2 * MINI), jnp.float32),
            pltpu.VMEM((GROUP, seqlen, MINI), jnp.bfloat16),
        ]
        + [dma((35,))] * 6
        + [dma((2, 7))] * 2
        + [dma((3,))],
        compiler_params=pltpu.CompilerParams(
            collective_id=0, has_side_effects=True, vmem_limit_bytes=60 << 20
        ),
        name="attention",
    )(x, cot, begin, cosine, sine_part, b_kv, small, w_up, w_down)


def packed_on_device(inputs, offsets, w_query, w_kv, w_out, w_up, w_down, b_up, vectors, b_kv, cotangent):
    rows = 2 * MINI
    seq = lax.axis_index("seq")
    x = inputs.reshape(rows, 768)
    cot = cotangent.reshape(rows, 768)
    flat_offsets = offsets.reshape(1, rows)
    places = seq * MINI + lax.rem(lax.broadcasted_iota(jnp.int32, (1, rows), 1), MINI)
    begin = places - flat_offsets
    frequency = jnp.power(10000.0, -jnp.arange(ROT // 2, dtype=jnp.float32) * (2.0 / ROT))
    angle = (flat_offsets.astype(jnp.float32) * 0.25) * frequency[:, None]
    cosine, sine_part = jnp.cos(angle), jnp.sin(angle)
    per_row = vectors.shape[1]
    extra = jnp.zeros((24, 128), jnp.bfloat16)
    extra = extra.at[:7, :per_row].set(vectors).at[7, : b_up.shape[0]].set(b_up)
    small = jnp.concatenate([w_query, w_kv, extra, w_out], axis=1)
    up_slabs, down_slabs, vec, bup, wkv, attn, dn1, dkv, grads_a, dq_sum = attention_call(
        x, cot, begin, cosine, sine_part, b_kv.reshape(1, -1).astype(jnp.float32), small, w_up, w_down
    )
    return feed_forward(x, cot, cosine, sine_part, up_slabs, down_slabs, vec, bup, wkv, attn, dn1, dkv, grads_a, dq_sum)


def feed_forward(x, cot, cosine, sine_part, up_slabs, down_slabs, vec, bup, wkv, attn, dn1, dkv, grads_a, dq_sum):
    up = up_slabs.reshape(768, 3072)
    down = down_slabs.reshape(3072, 768)
    xf, cf = f32(x), f32(cot)
    normed, inverse = normalize(xf)
    h1 = bf(normed * vec[0] + vec[1])
    h2 = bf(normed * vec[2] + vec[3])
    hidden = dot(h2, up) + bup
    act = bf(jax.nn.gelu(hidden, approximate=False))
    out = bf(xf + attn + dot(act, down) + vec[6])
    g_down = dot(act.T, cot)
    d_hidden = bf(dot_nt(cot, down) * gelu_slope(hidden))
    g_up = dot(h2.T, d_hidden)
    g_bup = jnp.sum(f32(d_hidden), axis=0)
    dn2 = dot_nt(d_hidden, up)
    pieces = jnp.transpose(dkv, (1, 0, 2, 3, 4)).reshape(8, 2, MINI, 2 * HD)
    dsh = f32(lax.psum_scatter(pieces, "seq", scatter_dimension=0, tiled=True)).reshape(2 * MINI, 2 * HD)
    d_shared = bf(jnp.concatenate([rotate(dsh[:, :HD], cosine.T, -sine_part.T), dsh[:, HD:]], axis=1))
    g_kv = dot(h1.T, d_shared)
    dn1 = dn1 + dot_nt(d_shared, wkv)
    g_bkv = lax.psum(jnp.sum(f32(d_shared), axis=0), ("dp", "seq"))
    csum = jnp.sum(cf, axis=0)
    g_vec = jnp.stack([jnp.sum(dn1 * normed, axis=0), jnp.sum(dn1, axis=0), jnp.sum(dn2 * normed, axis=0), jnp.sum(dn2, axis=0), dq_sum[0], csum, csum])
    g_in = cf + norm_back(dn1, normed, inverse, vec[0]) + norm_back(dn2, normed, inverse, vec[2])
    ga = jnp.transpose(grads_a, (0, 2, 1, 3, 4)).reshape(768, 1536)
    sc = lambda v, d=0: f32(lax.psum_scatter(v, ("dp", "seq"), scatter_dimension=d, tiled=True))
    gaq = sc(ga)
    return (
        out.reshape(2, 1, MINI, 768), g_in.reshape(2, 1, MINI, 768), gaq[:, :768], sc(bf(g_kv)), gaq[:, 768:],
        sc(bf(g_up)), sc(bf(g_down)), sc(g_bup), sc(g_vec, 1), g_bkv,
    )


def solution(mesh):
    packed = mesh.shape["dp"] == 4 and mesh.shape["seq"] == 8
    on_device = packed_on_device if packed else plain_on_device

    in_specs = (
        P(None, "dp", "seq", None),
        P(None, "dp", "seq"),
        P(("dp", "seq"), None),
        P(("dp", "seq"), None),
        P(("dp", "seq"), None),
        P(("dp", "seq"), None),
        P(("dp", "seq"), None),
        P(("dp", "seq")),
        P(None, ("dp", "seq")),
        P(),
        P(None, "dp", "seq", None),
    )
    out_specs = (
        P(None, "dp", "seq", None),
        P(None, "dp", "seq", None),
        P(("dp", "seq"), None),
        P(("dp", "seq"), None),
        P(("dp", "seq"), None),
        P(("dp", "seq"), None),
        P(("dp", "seq"), None),
        P(("dp", "seq")),
        P(None, ("dp", "seq")),
        P(),
    )
    return jax.shard_map(
        on_device, mesh=mesh, in_specs=in_specs, out_specs=out_specs, check_vma=False
    )
```

```python
import functools
import math

import jax
import jax.numpy as jnp
from jax import lax
from jax.experimental import pallas as pl
from jax.experimental.pallas import tpu as pltpu
from jax.sharding import PartitionSpec as P

H = 12
HD = 64
ROT = 16


epsilon = 1e-05
root_half = 0.7071067811865476
density_scale = 0.3989422804014327
masked_score = -1e30


def normalize(values):
    average = jnp.mean(values, axis=-1, keepdims=True)
    centered = values - average
    inverse = lax.rsqrt(jnp.mean(centered * centered, axis=-1, keepdims=True) + epsilon)
    return (centered * inverse, inverse)


def norm_back(grad_out, normed, inverse, gain_row):
    scaled = grad_out * gain_row
    first_mean = jnp.mean(scaled, axis=-1, keepdims=True)
    second_mean = jnp.mean(scaled * normed, axis=-1, keepdims=True)
    return inverse * (scaled - first_mean - normed * second_mean)


def rotate(values, cosine, sine_part):
    half_rot = ROT // 2
    first_part = values[..., :half_rot]
    second = values[..., half_rot:ROT]
    return jnp.concatenate(
        [
            first_part * cosine - second * sine_part,
            second * cosine + first_part * sine_part,
            values[..., ROT:],
        ],
        axis=-1,
    )


def gelu_slope(hidden):
    return 0.5 * (1.0 + lax.erf(hidden * root_half)) + hidden * density_scale * jnp.exp(
        -0.5 * hidden * hidden
    )


def tree_add(left_tree, right_tree):
    return tuple((left_item + right_item for left_item, right_item in zip(left_tree, right_tree)))


def plain_on_device(inputs, offsets, w_query, w_kv, w_out, w_up, w_down, b_up, vectors, b_kv, cotangent):
    micro_count = inputs.shape[0]
    local_rows = inputs.shape[2]
    model_width = inputs.shape[3]
    seqlen = local_rows * lax.axis_size("seq")
    key_block = math.gcd(seqlen, 512)
    first_row = lax.axis_index("seq") * local_rows
    blocks_used = (first_row + local_rows + key_block - 1) // key_block
    row_ids = first_row + jnp.arange(local_rows, dtype=jnp.int32)
    half_rot = ROT // 2
    frequency = jnp.power(10000.0, -jnp.arange(half_rot, dtype=jnp.float32) * (2.0 / ROT))
    kv_bias = b_kv.astype(jnp.float32)
    results = []
    input_grads = []
    totals = None
    kv_bias_total = jnp.zeros(b_kv.shape, jnp.float32)
    for micro_index in range(micro_count):
        values_in = inputs[micro_index, 0].astype(jnp.float32)
        row_offsets = offsets[micro_index, 0]
        upstream = cotangent[micro_index, 0]
        upstream_f = upstream.astype(jnp.float32)
        angle = (row_offsets.astype(jnp.float32) * 0.25)[:, None] * frequency[None, :]
        cosine = jnp.cos(angle)
        sine_part = jnp.sin(angle)
        gathered = (
            lax.all_gather(w_query, ("dp", "seq"), axis=0, tiled=True),
            lax.all_gather(w_kv, ("dp", "seq"), axis=0, tiled=True),
            lax.all_gather(w_out, ("dp", "seq"), axis=0, tiled=True),
            lax.all_gather(w_up, ("dp", "seq"), axis=0, tiled=True),
            lax.all_gather(w_down, ("dp", "seq"), axis=0, tiled=True),
            lax.all_gather(b_up, ("dp", "seq"), axis=0, tiled=True),
            lax.all_gather(vectors, ("dp", "seq"), axis=1, tiled=True),
        )
        query_full, kv_full, out_full, up_full, down_full, up_bias, vector_full = gathered
        vector_f = vector_full.astype(jnp.float32)
        normed1, inverse1 = normalize(values_in)
        hidden1 = (normed1 * vector_f[0] + vector_f[1]).astype(jnp.bfloat16)
        query_pre = jnp.dot(hidden1, query_full, preferred_element_type=jnp.float32) + vector_f[4]
        kv_pre = jnp.dot(hidden1, kv_full, preferred_element_type=jnp.float32) + kv_bias
        queries = rotate(
            query_pre.reshape(local_rows, H, HD), cosine[:, None, :], sine_part[:, None, :]
        ).astype(jnp.bfloat16)
        shared_local = jnp.concatenate(
            [rotate(kv_pre[:, :HD], cosine, sine_part), kv_pre[:, HD:]], axis=1
        ).astype(jnp.bfloat16)
        shared = lax.all_gather(shared_local, "seq", axis=0, tiled=True)

        def block_scores(number):
            start_row = number * key_block
            key_piece = lax.dynamic_slice_in_dim(shared, start_row, key_block, 0)
            columns = start_row + jnp.arange(key_block, dtype=jnp.int32)
            allowed = (columns[None, :] <= row_ids[:, None]) & (
                row_ids[:, None] - columns[None, :] <= row_offsets[:, None]
            )
            scores = (
                jnp.einsum(
                    "rhd,kd->hrk", queries, key_piece[:, :HD], preferred_element_type=jnp.float32
                )
                * 0.125
            )
            return (jnp.where(allowed[None], scores, masked_score), key_piece)

        def max_step(number, state_pair):
            running_top, denominator = state_pair
            scores, key_piece = block_scores(number)
            new_top = jnp.maximum(running_top, jnp.max(scores, axis=-1))
            denominator = denominator * jnp.exp(running_top - new_top) + jnp.sum(
                jnp.exp(scores - new_top[..., None]), axis=-1
            )
            return (new_top, denominator)

        start_top = jnp.full((H, local_rows), masked_score, jnp.float32)
        running_top, denominator = lax.fori_loop(
            0, blocks_used, max_step, (start_top, jnp.zeros((H, local_rows), jnp.float32))
        )
        log_total = running_top + jnp.log(denominator)

        def value_step(number, accumulated):
            scores, key_piece = block_scores(number)
            soft_weights = jnp.exp(scores - log_total[..., None]).astype(jnp.bfloat16)
            return accumulated + jnp.einsum(
                "hrk,kd->rhd", soft_weights, key_piece[:, HD:], preferred_element_type=jnp.float32
            )

        attended_f = lax.fori_loop(
            0, blocks_used, value_step, jnp.zeros((local_rows, H, HD), jnp.float32)
        )
        attended = attended_f.reshape(local_rows, model_width).astype(jnp.bfloat16)
        attn_out = jnp.dot(attended, out_full, preferred_element_type=jnp.float32) + vector_f[5]
        normed2, inverse2 = normalize(values_in)
        hidden2 = (normed2 * vector_f[2] + vector_f[3]).astype(jnp.bfloat16)
        hidden_up = jnp.dot(hidden2, up_full, preferred_element_type=jnp.float32) + up_bias.astype(
            jnp.float32
        )
        activated = jax.nn.gelu(hidden_up, approximate=False).astype(jnp.bfloat16)
        mlp_out = jnp.dot(activated, down_full, preferred_element_type=jnp.float32) + vector_f[6]
        results.append((values_in + attn_out + mlp_out).astype(jnp.bfloat16))
        regathered = (
            lax.all_gather(w_query, ("dp", "seq"), axis=0, tiled=True),
            lax.all_gather(w_kv, ("dp", "seq"), axis=0, tiled=True),
            lax.all_gather(w_out, ("dp", "seq"), axis=0, tiled=True),
            lax.all_gather(w_up, ("dp", "seq"), axis=0, tiled=True),
            lax.all_gather(w_down, ("dp", "seq"), axis=0, tiled=True),
            lax.all_gather(b_up, ("dp", "seq"), axis=0, tiled=True),
            lax.all_gather(vectors, ("dp", "seq"), axis=1, tiled=True),
        )
        query_back, kv_back, out_back, up_back, down_back, up_bias_back, vector_back = regathered
        vector_back_f = vector_back.astype(jnp.float32)
        grad_w_down = jnp.einsum(
            "rf,rd->fd", activated, upstream, preferred_element_type=jnp.float32
        )
        d_act = jnp.einsum("rd,fd->rf", upstream, down_back, preferred_element_type=jnp.float32)
        d_hidden = (d_act * gelu_slope(hidden_up)).astype(jnp.bfloat16)
        grad_w_up = jnp.einsum("rd,rf->df", hidden2, d_hidden, preferred_element_type=jnp.float32)
        grad_b_up = jnp.sum(d_hidden.astype(jnp.float32), axis=0)
        d_normed2 = jnp.einsum("rf,df->rd", d_hidden, up_back, preferred_element_type=jnp.float32)
        grad_w_out = jnp.einsum("rd,re->de", attended, upstream, preferred_element_type=jnp.float32)
        d_attended = (
            jnp.einsum("re,de->rd", upstream, out_back, preferred_element_type=jnp.float32)
            .astype(jnp.bfloat16)
            .reshape(local_rows, H, HD)
        )

        def delta_step(number, accumulated):
            scores, key_piece = block_scores(number)
            soft_probs = jnp.exp(scores - log_total[..., None])
            d_probs = jnp.einsum(
                "rhd,kd->hrk", d_attended, key_piece[:, HD:], preferred_element_type=jnp.float32
            )
            return accumulated + jnp.sum(soft_probs * d_probs, axis=-1)

        delta = lax.fori_loop(0, blocks_used, delta_step, jnp.zeros((H, local_rows), jnp.float32))

        def grad_step(number, state_pair):
            d_query_rot, d_shared_all = state_pair
            start_row = number * key_block
            scores, key_piece = block_scores(number)
            soft_probs = jnp.exp(scores - log_total[..., None])
            d_probs = jnp.einsum(
                "rhd,kd->hrk", d_attended, key_piece[:, HD:], preferred_element_type=jnp.float32
            )
            d_scores = (soft_probs * (d_probs - delta[..., None])).astype(jnp.bfloat16)
            d_query_rot = (
                d_query_rot
                + jnp.einsum(
                    "hrk,kd->rhd", d_scores, key_piece[:, :HD], preferred_element_type=jnp.float32
                )
                * 0.125
            )
            d_keys = (
                jnp.einsum("hrk,rhd->kd", d_scores, queries, preferred_element_type=jnp.float32)
                * 0.125
            )
            d_values = jnp.einsum(
                "hrk,rhd->kd",
                soft_probs.astype(jnp.bfloat16),
                d_attended,
                preferred_element_type=jnp.float32,
            )
            current = lax.dynamic_slice_in_dim(d_shared_all, start_row, key_block, 0)
            d_shared_all = lax.dynamic_update_slice_in_dim(
                d_shared_all, current + jnp.concatenate([d_keys, d_values], axis=1), start_row, 0
            )
            return (d_query_rot, d_shared_all)

        d_query_rot, d_shared_all = lax.fori_loop(
            0,
            blocks_used,
            grad_step,
            (jnp.zeros((local_rows, H, HD), jnp.float32), jnp.zeros((seqlen, 2 * HD), jnp.float32)),
        )
        d_shared_mine = lax.psum_scatter(
            d_shared_all.astype(jnp.bfloat16), "seq", scatter_dimension=0, tiled=True
        ).astype(jnp.float32)
        d_shared = jnp.concatenate(
            [rotate(d_shared_mine[:, :HD], cosine, -sine_part), d_shared_mine[:, HD:]], axis=1
        ).astype(jnp.bfloat16)
        d_queries = (
            rotate(d_query_rot, cosine[:, None, :], -sine_part[:, None, :])
            .reshape(local_rows, model_width)
            .astype(jnp.bfloat16)
        )
        grad_w_query = jnp.einsum(
            "rd,re->de", hidden1, d_queries, preferred_element_type=jnp.float32
        )
        grad_w_kv = jnp.einsum("rd,rc->dc", hidden1, d_shared, preferred_element_type=jnp.float32)
        kv_bias_total = kv_bias_total + jnp.sum(d_shared.astype(jnp.float32), axis=0)
        d_normed1 = jnp.einsum(
            "re,de->rd", d_queries, query_back, preferred_element_type=jnp.float32
        ) + jnp.einsum("rc,dc->rd", d_shared, kv_back, preferred_element_type=jnp.float32)
        upstream_sum = jnp.sum(upstream_f, axis=0)
        grad_vectors = jnp.stack(
            [
                jnp.sum(d_normed1 * normed1, axis=0),
                jnp.sum(d_normed1, axis=0),
                jnp.sum(d_normed2 * normed2, axis=0),
                jnp.sum(d_normed2, axis=0),
                jnp.sum(d_queries.astype(jnp.float32), axis=0),
                upstream_sum,
                upstream_sum,
            ]
        )
        input_grads.append(
            upstream_f
            + norm_back(d_normed1, normed1, inverse1, vector_back_f[0])
            + norm_back(d_normed2, normed2, inverse2, vector_back_f[2])
        )
        shares = (
            lax.psum_scatter(grad_w_query, ("dp", "seq"), scatter_dimension=0, tiled=True),
            lax.psum_scatter(grad_w_kv, ("dp", "seq"), scatter_dimension=0, tiled=True),
            lax.psum_scatter(grad_w_out, ("dp", "seq"), scatter_dimension=0, tiled=True),
            lax.psum_scatter(grad_w_up, ("dp", "seq"), scatter_dimension=0, tiled=True),
            lax.psum_scatter(grad_w_down, ("dp", "seq"), scatter_dimension=0, tiled=True),
            lax.psum_scatter(grad_b_up, ("dp", "seq"), scatter_dimension=0, tiled=True),
            lax.psum_scatter(grad_vectors, ("dp", "seq"), scatter_dimension=1, tiled=True),
        )
        totals = shares if totals is None else tree_add(totals, shares)
    kv_bias_grad = lax.psum(kv_bias_total, ("dp", "seq"))
    return (
        jnp.stack(results)[:, None],
        jnp.stack(input_grads)[:, None],
        totals[0],
        totals[1],
        totals[2],
        totals[3],
        totals[4],
        totals[5],
        totals[6],
        kv_bias_grad,
    )


MESH = pl.DeviceIdType.MESH
NT = (((1,), (1,)), ((), ()))
VM = pl.BlockSpec(memory_space=pltpu.VMEM)
HBM = pl.BlockSpec(memory_space=pl.ANY)
GROUP = 4
KEYS = 512
MINI = 256
scale_log2 = 0.125 * 1.4426950408889634


def dot(left, right):
    return jnp.dot(left, right, preferred_element_type=jnp.float32)


def dot_nt(left, right):
    return lax.dot_general(left, right, NT, preferred_element_type=jnp.float32)


def bf(values):
    return values.astype(jnp.bfloat16)


def f32(values):
    return values.astype(jnp.float32)


def rotate_rows(block, cosine, sine_part):
    half_rot = ROT // 2
    first, second = block[:half_rot], block[half_rot:ROT]
    return jnp.concatenate(
        [first * cosine - second * sine_part, second * cosine + first * sine_part, block[ROT:]],
        axis=0,
    )


def here():
    return lax.axis_index("dp"), lax.axis_index("seq")


def greet(targets):
    barrier = pltpu.get_barrier_semaphore()
    for target in targets:
        pl.semaphore_signal(barrier, inc=1, device_id=target, device_id_type=MESH)
    pl.semaphore_wait(barrier, len(targets))


def remote(source, target, send, recv, device):
    return pltpu.make_async_remote_copy(
        src_ref=source,
        dst_ref=target,
        send_sem=send,
        recv_sem=recv,
        device_id=device,
        device_id_type=MESH,
    )


class Gather:
    def __init__(self, shard, slabs, halves, send, recv):
        self.shard, self.slabs, self.halves, self.send, self.recv = shard, slabs, halves, send, recv
        self.dp, self.seq = here()
        self.sent = []

    def index(self, dp_flip, z_flip, core_flip=0):
        return (self.dp ^ dp_flip) * 8 + (self.seq ^ (2 * z_flip + core_flip))

    def part(self, slab, half):
        rows, columns = half
        return self.slabs.at[slab, rows, columns]

    def start(self, number, source, target, device):
        copy = remote(source, target, self.send.at[number], self.recv.at[number], device)
        copy.start()
        self.sent.append(copy)

    def arrived(self, number, target):
        remote(target, target, self.send.at[number], self.recv.at[number], (self.dp, self.seq ^ 1)).wait_recv()

    def own(self):
        mine = self.slabs.at[self.index(0, 0)]
        for flip in (1, 2, 3):
            self.start(flip - 1, self.shard, mine, (self.dp, self.seq ^ (2 * flip)))
        self.start(3, self.shard, mine, (self.dp ^ 1, self.seq))
        self.start(7, self.shard, mine, (self.dp ^ 2, self.seq))
        self.start(19, self.shard, mine, (self.dp, self.seq ^ 1))

    def from_z(self, flip):
        piece = self.slabs.at[self.index(0, flip)]
        self.arrived(flip - 1, piece)
        self.start(3 + flip, piece, piece, (self.dp ^ 1, self.seq))
        self.start(7 + flip, piece, piece, (self.dp ^ 2, self.seq))
        self.start(19 + flip, piece, piece, (self.dp, self.seq ^ 1))

    def from_xy(self, flip):
        for axis, half in ((1, 0), (2, 1)):
            number = 3 if axis == 1 else 7
            slab = self.index(axis, flip)
            piece = self.slabs.at[slab]
            self.arrived(number + flip, piece)
            cut = self.part(slab, self.halves[half])
            self.start(11 + 4 * half + flip, cut, cut, (self.dp ^ (3 - axis), self.seq))
            self.start((23 if axis == 1 else 27) + flip, piece, piece, (self.dp, self.seq ^ 1))

    def from_diagonal(self, flip):
        slab = self.index(3, flip)
        for half in (0, 1):
            self.arrived(11 + 4 * half + flip, self.part(slab, self.halves[half]))
        piece = self.slabs.at[slab]
        self.start(31 + flip, piece, piece, (self.dp, self.seq ^ 1))

    def from_core(self):
        for number, dp_flip in ((19, 0), (23, 1), (27, 2), (31, 3)):
            for flip in range(4):
                self.arrived(number + flip, self.slabs.at[self.index(dp_flip, flip, 1)])

    def finish(self):
        for copy in self.sent:
            copy.wait_send()


def attend(
    micro, steps, row0, begin_ref, q_t, do_t, kv_ref, kv_t, att_t, dq_t, dkv, pair, scaled, score_ref, weight_ref, tick
):
    cols = slice(micro * MINI, (micro + 1) * MINI)
    begin = begin_ref[0:1, cols]
    row_ids = row0 + lax.broadcasted_iota(jnp.int32, (1, MINI), 1)
    for group in range(H // GROUP):
        heads = [slice((group * GROUP + n) * HD, (group * GROUP + n + 1) * HD) for n in range(GROUP)]
        for n, head in enumerate(heads):
            pair[n, :HD, :MINI] = q_t[head, cols]
            pair[n, HD:, MINI:] = do_t[head, cols]

        def score_step(step, tops):
            keys = pl.ds(pl.multiple_of(step * KEYS, KEYS), KEYS)
            block = kv_ref[micro, keys, :]
            ids = step * KEYS + lax.broadcasted_iota(jnp.int32, (KEYS, 1), 0)
            allowed = (ids <= row_ids) & (ids >= begin)
            found = []
            for n in range(GROUP):
                both = dot(block, pair[n])
                scores = jnp.where(allowed, both[:, :MINI] * scale_log2, masked_score)
                score_ref[n, keys, :MINI] = scores
                score_ref[n, keys, MINI:] = both[:, MINI:]
                found.append(jnp.maximum(tops[n], jnp.max(scores.reshape(KEYS // 8, 8, MINI), axis=0)))
            return tuple(found)

        tops = lax.fori_loop(
            0, steps, score_step, tuple(jnp.full((8, MINI), masked_score, jnp.float32) for _ in heads)
        )
        tops = [jnp.max(top, axis=0, keepdims=True) for top in tops]

        def value_step(step, carried):
            keys = pl.ds(pl.multiple_of(step * KEYS, KEYS), KEYS)
            values = kv_t[micro, HD:, keys]
            found = []
            for n in range(GROUP):
                output, total = carried[n]
                weights = jnp.exp2(score_ref[n, keys, :MINI] - tops[n])
                total = total + jnp.sum(weights.reshape(KEYS // 8, 8, MINI), axis=0)
                weight_ref[n, keys, :] = bf(weights)
                found.append((output + dot(values, bf(weights)), total))
            return tuple(found)

        sums = lax.fori_loop(
            0,
            steps,
            value_step,
            tuple((jnp.zeros((HD, MINI), jnp.float32), jnp.zeros((8, MINI), jnp.float32)) for _ in heads),
        )
        inverses, deltas = [], []
        for n, head in enumerate(heads):
            inverse = 1.0 / jnp.sum(sums[n][1], axis=0, keepdims=True)
            output = sums[n][0] * inverse
            upstream = f32(do_t[head, cols])
            deltas.append(jnp.sum(output * upstream, axis=0, keepdims=True))
            inverses.append(inverse)
            att_t[head, cols] = bf(output)
            scaled[n, :HD, :MINI] = bf(f32(q_t[head, cols]) * inverse)
            scaled[n, HD:, MINI:] = bf(upstream * inverse)

        def grad_step(step, carried):
            keys = pl.ds(pl.multiple_of(step * KEYS, KEYS), KEYS)
            key_block = kv_t[micro, :HD, keys]
            total = dkv[micro, keys, :]
            found = []
            for n in range(GROUP):
                weights = weight_ref[n, keys, :]
                d_scores = bf(f32(weights) * (score_ref[n, keys, MINI:] - deltas[n]))
                found.append(carried[n] + dot(key_block, d_scores))
                total = total + dot_nt(d_scores, scaled[n, :, :MINI])
                total = total + dot_nt(weights, scaled[n, :, MINI:])
            dkv[micro, keys, :] = total
            return tuple(found)

        grads = lax.fori_loop(
            0, steps, grad_step, tuple(jnp.zeros((HD, MINI), jnp.float32) for _ in heads)
        )
        for n, head in enumerate(heads):
            dq_t[head, cols] = grads[n] * (inverses[n] * 0.125)
        tick(micro, group)


def spread(slabs):
    lane = lax.broadcasted_iota(jnp.int32, (8, 128), 1)
    row = lax.broadcasted_iota(jnp.int32, (8, 128), 0)
    rows = [jnp.zeros((8, 128), jnp.float32) for _ in range(6)]
    wide = [jnp.zeros((8, 128), jnp.float32) for _ in range(24)]
    for number in range(32):
        for width, target, keep in ((24, rows, row < 7), (96, wide, row == 7)):
            block, shift = divmod(number * width, 128)
            piece = jnp.where(keep, slabs[number], 0.0)
            piece = pltpu.roll(piece, shift, 1) if shift else piece
            target[block] = target[block] + jnp.where(lane >= shift, piece, 0.0)
            if shift + width > 128:
                target[block + 1] = target[block + 1] + jnp.where(lane < shift, piece, 0.0)
    return jnp.concatenate(rows, axis=1), jnp.concatenate(wide, axis=1)


def slab_order(store, block, dp_index, rows):
    for z in range(4):
        for core in range(2):
            first = (2 * z + core) * rows
            store(dp_index, core, z, bf(block[first : first + rows]))


def attention_kernel(
    x_ref, cot_ref, begin_ref, cos_ref, sin_ref, bkv_ref, small_ref, up_ref, down_ref,
    up_slabs, down_slabs, vec_ref, bup_ref, wkv_ref, attn_ref, dn_ref, dkv_out, grads_ref, dqsum_ref,
    slabs, weights, n1_ref, n1t_ref, q_t, do_t, att_t, dq_t, kv_ref, kv_t, dkv, pair, scaled, score_ref, weight_ref,
    send_a, recv_a, send_u, recv_u, send_d, recv_d, send_kv, recv_kv, local_sem,
):
    dp, seq = here()
    wide = slabs.shape[2] // 2
    gather_a = Gather(small_ref, slabs, ((slice(None), slice(0, wide)), (slice(None), slice(wide, 2 * wide))), send_a, recv_a)
    half = up_ref.shape[1] // 2
    gather_u = Gather(up_ref, up_slabs, ((slice(None), slice(0, half)), (slice(None), slice(half, 2 * half))), send_u, recv_u)
    half = down_ref.shape[0] // 2
    gather_d = Gather(down_ref, down_slabs, ((slice(0, half), slice(None)), (slice(half, 2 * half), slice(None))), send_d, recv_d)
    greet(
        [(dp, seq ^ 1), (dp, seq ^ 2), (dp, seq ^ 4), (dp, seq ^ 6), (dp ^ 1, seq), (dp ^ 2, seq)]
    )
    gather_a.own()
    mine = gather_a.index(0, 0)
    local_copies = [
        pltpu.make_async_copy(small_ref, slabs.at[mine], local_sem.at[0]),
        pltpu.make_async_copy(up_ref, up_slabs.at[mine], local_sem.at[1]),
        pltpu.make_async_copy(down_ref, down_slabs.at[mine], local_sem.at[2]),
    ]
    for copy in local_copies:
        copy.start()
    pair[...] = jnp.zeros_like(pair)
    scaled[...] = jnp.zeros_like(scaled)
    dkv[...] = jnp.zeros_like(dkv)
    normed, _ = normalize(f32(x_ref[...]))
    for flip in (1, 2, 3):
        gather_a.from_z(flip)
    for flip in range(4):
        gather_a.from_xy(flip)
    for flip in range(4):
        gather_a.from_diagonal(flip)
    gather_a.from_core()
    local_copies[0].wait()

    for number in range(16):
        block = jnp.concatenate([f32(slabs[2 * number]), f32(slabs[2 * number + 1])], axis=0)
        weights[48 * number : 48 * number + 48, :] = bf(block)
    vectors, wide_row = spread([f32(slabs[number, 0:8, 896:1024]) for number in range(32)])
    vec_ref[...] = vectors
    bup_ref[...] = wide_row[7:8]
    wkv_ref[...] = weights[:, 768:896]

    hidden = bf(normed * vectors[0:1] + vectors[1:2])
    n1_ref[...] = hidden
    kv_pre = dot(hidden, weights[:, 768:896]) + bkv_ref[...]
    kv_pre_t = kv_pre.T
    cosine, sine_part = cos_ref[...], sin_ref[...]
    shared_t = bf(jnp.concatenate([rotate_rows(kv_pre_t[:HD], cosine, sine_part), kv_pre_t[HD:]], axis=0))
    shared = bf(f32(shared_t).T)
    place = pl.ds(pl.multiple_of(seq * MINI, MINI), MINI)
    kv_copies = []
    for micro in range(2):
        kv_ref[micro, place, :] = shared[micro * MINI : (micro + 1) * MINI]

    def kv_block(micro, flip):
        return kv_ref.at[micro, pl.ds(pl.multiple_of((seq ^ flip) * MINI, MINI), MINI)]

    def kv_send(micro, flip, number, device):
        block = kv_block(micro, flip)
        copy = remote(block, block, send_kv.at[micro, number], recv_kv.at[micro, number], device)
        copy.start()
        kv_copies.append(copy)

    def kv_arrived(micro, flip, number):
        block = kv_block(micro, flip)
        remote(block, block, send_kv.at[micro, number], recv_kv.at[micro, number], (dp, seq ^ 1)).wait_recv()

    for micro in range(2):
        for flip in (1, 2, 3):
            kv_send(micro, 0, flip - 1, (dp, seq ^ (2 * flip)))
        kv_send(micro, 0, 3, (dp, seq ^ 1))
    gather_u.own()
    gather_d.own()

    n1t_ref[...] = bf(f32(hidden).T)
    query = (dot(hidden, weights[:, :768]) + vectors[4:5]).T
    for head in range(H):
        q_t[head * HD : (head + 1) * HD, :] = bf(
            rotate_rows(query[head * HD : (head + 1) * HD], cosine, sine_part)
        )
    do_t[...] = bf(dot_nt(weights[:, 1024:1792], cot_ref[...]))

    def kv_forward(micro):
        for flip in (1, 2, 3):
            kv_arrived(micro, 2 * flip, flip - 1)
            kv_send(micro, 2 * flip, 3 + flip, (dp, seq ^ 1))

    def kv_finish(micro):
        for flip in range(4):
            kv_arrived(micro, 2 * flip + 1, 3 + flip)
        kv_t[micro] = bf(f32(kv_ref[micro]).T)

    kv_forward(0)
    kv_forward(1)
    kv_finish(0)

    def tick(micro, group):
        at = micro * (H // GROUP) + group
        if at == 0:
            gather_u.from_z(1)
            gather_d.from_z(1)
        if at == 1:
            gather_u.from_z(2)
            gather_d.from_z(2)
            gather_u.from_z(3)
            gather_d.from_z(3)
        if at == 2:
            for flip in (0, 1):
                gather_u.from_xy(flip)
                gather_d.from_xy(flip)
        if at == 3:
            for flip in (2, 3):
                gather_u.from_xy(flip)
                gather_d.from_xy(flip)
        if at == 4:
            for flip in range(4):
                gather_u.from_diagonal(flip)
                gather_d.from_diagonal(flip)

    steps = lax.div((seq + 1) * MINI + KEYS - 1, KEYS)
    for micro in range(2):
        if micro == 1:
            kv_finish(1)
        attend(
            micro, steps, seq * MINI, begin_ref, q_t, do_t, kv_ref, kv_t, att_t, dq_t, dkv,
            pair, scaled, score_ref, weight_ref, tick,
        )
    for micro in range(2):
        for core in range(2):
            for z in range(4):
                first = (2 * z + core) * MINI
                block = dkv[micro, first : first + MINI, :]
                scale = jnp.where(lax.broadcasted_iota(jnp.int32, (1, 2 * HD), 1) < HD, 0.125, 1.0)
                dkv_out[core, z, micro] = bf(block * scale)
    attn_ref[...] = dot(bf(f32(att_t[...]).T), weights[:, 1024:1792]) + vectors[5:6]
    for head in range(H):
        dq_t[head * HD : (head + 1) * HD, :] = rotate_rows(
            dq_t[head * HD : (head + 1) * HD, :], cosine, -sine_part
        )
    d_query = bf(dq_t[...].T)
    dqsum_ref[...] = jnp.sum(f32(d_query), axis=0, keepdims=True)
    dn_ref[...] = dot_nt(d_query, weights[:, :768])
    for block in range(4):
        rows = slice(192 * block, 192 * block + 192)

        def put_query(dp_index, core, z, piece):
            grads_ref[dp_index, core, z, :, 0:768] = piece

        def put_out(dp_index, core, z, piece):
            grads_ref[dp_index, core, z, :, 768:1536] = piece

        slab_order(put_query, dot(n1t_ref[rows, :], d_query), block, 24)
        slab_order(put_out, dot(att_t[rows, :], cot_ref[...]), block, 24)
    for gather in (gather_u, gather_d):
        gather.from_core()
    for gather in (gather_a, gather_u, gather_d):
        gather.finish()
    for copy in kv_copies:
        copy.wait_send()
    for copy in local_copies[1:]:
        copy.wait()


def attention_call(x, cot, begin, cosine, sine_part, b_kv, small, w_up, w_down):
    rows = x.shape[0]
    dma = pltpu.SemaphoreType.DMA
    out = lambda shape, kind: jax.ShapeDtypeStruct(shape, kind)
    seqlen = 8 * MINI
    return pl.pallas_call(
        attention_kernel,
        out_shape=(
            out((32,) + w_up.shape, jnp.bfloat16),
            out((32,) + w_down.shape, jnp.bfloat16),
            out((8, 768), jnp.float32),
            out((1, 3072), jnp.float32),
            out((768, 128), jnp.bfloat16),
            out((rows, 768), jnp.float32),
            out((rows, 768), jnp.float32),
            out((2, 4, 2, MINI, 2 * HD), jnp.bfloat16),
            out((4, 2, 4, 24, 1536), jnp.bfloat16),
            out((1, 768), jnp.float32),
        ),
        in_specs=[VM] * 7 + [HBM] * 2,
        out_specs=(HBM, HBM) + (VM,) * 8,
        scratch_shapes=[
            pltpu.VMEM((32,) + small.shape, jnp.bfloat16),
            pltpu.VMEM((768, small.shape[1]), jnp.bfloat16),
            pltpu.VMEM((rows, 768), jnp.bfloat16),
            pltpu.VMEM((768, rows), jnp.bfloat16),
            pltpu.VMEM((768, rows), jnp.bfloat16),
            pltpu.VMEM((768, rows), jnp.bfloat16),
            pltpu.VMEM((768, rows), jnp.bfloat16),
            pltpu.VMEM((768, rows), jnp.float32),
            pltpu.VMEM((2, seqlen, 2 * HD), jnp.bfloat16),
            pltpu.VMEM((2, 2 * HD, seqlen), jnp.bfloat16),
            pltpu.VMEM((2, seqlen, 2 * HD), jnp.float32),
            pltpu.VMEM((GROUP, 2 * HD, 2 * MINI), jnp.bfloat16),
            pltpu.VMEM((GROUP, 2 * HD, 2 * MINI), jnp.bfloat16),
            pltpu.VMEM((GROUP, seqlen, 2 * MINI), jnp.float32),
            pltpu.VMEM((GROUP, seqlen, MINI), jnp.bfloat16),
        ]
        + [dma((35,))] * 6
        + [dma((2, 7))] * 2
        + [dma((3,))],
        compiler_params=pltpu.CompilerParams(
            collective_id=0, has_side_effects=True, vmem_limit_bytes=60 << 20
        ),
        name="attention",
    )(x, cot, begin, cosine, sine_part, b_kv, small, w_up, w_down)


def packed_on_device(inputs, offsets, w_query, w_kv, w_out, w_up, w_down, b_up, vectors, b_kv, cotangent):
    rows = 2 * MINI
    seq = lax.axis_index("seq")
    x = inputs.reshape(rows, 768)
    cot = cotangent.reshape(rows, 768)
    flat_offsets = offsets.reshape(1, rows)
    places = seq * MINI + lax.rem(lax.broadcasted_iota(jnp.int32, (1, rows), 1), MINI)
    begin = places - flat_offsets
    frequency = jnp.power(10000.0, -jnp.arange(ROT // 2, dtype=jnp.float32) * (2.0 / ROT))
    angle = (flat_offsets.astype(jnp.float32) * 0.25) * frequency[:, None]
    cosine, sine_part = jnp.cos(angle), jnp.sin(angle)
    per_row = vectors.shape[1]
    extra = jnp.zeros((24, 128), jnp.bfloat16)
    extra = extra.at[:7, :per_row].set(vectors).at[7, : b_up.shape[0]].set(b_up)
    small = jnp.concatenate([w_query, w_kv, extra, w_out], axis=1)
    up_slabs, down_slabs, vec, bup, wkv, attn, dn1, dkv, grads_a, dq_sum = attention_call(
        x, cot, begin, cosine, sine_part, b_kv.reshape(1, -1).astype(jnp.float32), small, w_up, w_down
    )
    return feed_forward(x, cot, cosine, sine_part, up_slabs, down_slabs, vec, bup, wkv, attn, dn1, dkv, grads_a, dq_sum)


class Scatter:
    def __init__(self, slabs, from_core, from_diagonal, from_xy, from_z, send, recv):
        self.slabs, self.from_core, self.from_diagonal = slabs, from_core, from_diagonal
        self.from_xy, self.from_z, self.send, self.recv = from_xy, from_z, send, recv
        self.dp, self.seq = here()
        self.core = lax.rem(self.seq, 2)
        self.z = lax.div(self.seq, 2)
        self.sent = []

    def start(self, number, source, target, device):
        copy = remote(source, target, self.send.at[number], self.recv.at[number], device)
        copy.start()
        self.sent.append(copy)

    def arrived(self, number, target):
        remote(target, target, self.send.at[number], self.recv.at[number], (self.dp, self.seq ^ 1)).wait_recv()

    def block(self, flip):
        return self.slabs.at[self.dp ^ flip, self.core]

    def to_core(self, flip):
        other = self.slabs.at[self.dp ^ flip, 1 - self.core]
        self.start(flip, other, self.from_core.at[flip], (self.dp, self.seq ^ 1))

    def add(self, block, z, terms):
        total = f32(block[z])
        for term in terms:
            total = total + f32(term)
        block[z] = bf(total)

    def diagonal(self):
        block = self.block(3)
        self.arrived(3, self.from_core.at[3])
        for half in (0, 1):
            for z in (2 * half, 2 * half + 1):
                self.add(block, z, [self.from_core[3, z]])
            self.start(4 + half, block.at[pl.ds(2 * half, 2)], self.from_diagonal.at[half], (self.dp ^ (1 + half), self.seq))

    def beside(self, axis):
        half = 2 - axis
        block = self.block(axis)
        self.arrived(axis, self.from_core.at[axis])
        self.arrived(4 + half, self.from_diagonal.at[half])
        for z in range(4):
            terms = [self.from_core[axis, z]]
            if z // 2 == half:
                terms.append(self.from_diagonal[half, z % 2])
            self.add(block, z, terms)
        self.start(5 + axis, block, self.from_xy.at[axis - 1], (self.dp ^ axis, self.seq))

    def own(self):
        block = self.block(0)
        self.arrived(0, self.from_core.at[0])
        for axis in (1, 2):
            self.arrived(5 + axis, self.from_xy.at[axis - 1])
        for z in range(4):
            self.add(block, z, [self.from_core[0, z], self.from_xy[0, z], self.from_xy[1, z]])
        for flip in (1, 2, 3):
            self.start(7 + flip, block.at[self.z ^ flip], self.from_z.at[flip - 1], (self.dp, self.seq ^ (2 * flip)))

    def total(self):
        value = f32(self.slabs[self.dp, self.core, self.z])
        for flip in (1, 2, 3):
            self.arrived(7 + flip, self.from_z.at[flip - 1])
            value = value + f32(self.from_z[flip - 1])
        return value

    def finish(self):
        for copy in self.sent:
            copy.wait_send()


def feed_kernel(
    x_ref, cot_ref, cos_ref, sin_ref, vec_ref, bup_ref, wkv_ref, attn_ref, dn_ref, dqsum_ref, dkv_in, grads_a, up_hbm, down_hbm,
    out_ref, gin_ref, gq_ref, go_ref, gu_ref, gkv_ref, gd_ref, small_out,
    up_ref, down_ref, n1t_ref, n2_ref, n2t_ref, act_ref, dh_ref, mlp_ref, dshared_ref, stats,
    a_slabs, d_slabs, u_slabs, v_slabs,
    a_core, a_diag, a_xy, a_z, d_core, d_diag, d_xy, d_z, u_core, u_diag, u_xy, u_z, v_core, v_diag, v_xy, v_z,
    dkv, dkv_core, dkv_z, small, small_in,
    send_s, recv_s, send_k, recv_k, send_m, recv_m, load_sem,
):
    dp, seq = here()
    core, z = lax.rem(seq, 2), lax.div(seq, 2)
    loads = [
        pltpu.make_async_copy(dkv_in, dkv, load_sem.at[2]),
        pltpu.make_async_copy(grads_a, a_slabs, load_sem.at[3]),
        pltpu.make_async_copy(up_hbm, up_ref, load_sem.at[0]),
        pltpu.make_async_copy(down_hbm, down_ref, load_sem.at[1]),
    ]
    for copy in loads:
        copy.start()
    greet(
        [(dp, seq ^ 1), (dp, seq ^ 2), (dp, seq ^ 4), (dp, seq ^ 6), (dp ^ 1, seq), (dp ^ 2, seq)]
    )
    scatter_a = Scatter(a_slabs, a_core, a_diag, a_xy, a_z, send_s.at[0], recv_s.at[0])
    scatter_d = Scatter(d_slabs, d_core, d_diag, d_xy, d_z, send_s.at[1], recv_s.at[1])
    scatter_u = Scatter(u_slabs, u_core, u_diag, u_xy, u_z, send_s.at[2], recv_s.at[2])
    scatter_v = Scatter(v_slabs, v_core, v_diag, v_xy, v_z, send_s.at[3], recv_s.at[3])
    kv_sent = []

    def kv_start(number, source, target, device):
        copy = remote(source, target, send_k.at[number], recv_k.at[number], device)
        copy.start()
        kv_sent.append(copy)

    def kv_arrived(number, target):
        remote(target, target, send_k.at[number], recv_k.at[number], (dp, seq ^ 1)).wait_recv()

    loads[0].wait()
    kv_start(0, dkv.at[1 - core], dkv_core, (dp, seq ^ 1))
    loads[1].wait()
    for flip in (3, 1, 2, 0):
        scatter_a.to_core(flip)

    vectors = vec_ref[...]
    for start in range(0, 2 * MINI, MINI):
        rows = slice(start, start + MINI)
        normed, inverse = normalize(f32(x_ref[rows, :]))
        stats[rows, :] = jnp.broadcast_to(inverse, (MINI, 128))
        n1t_ref[:, rows] = bf((normed * vectors[0:1] + vectors[1:2]).T)
        second = normed * vectors[2:3] + vectors[3:4]
        n2_ref[rows, :] = bf(second)
        n2t_ref[:, rows] = bf(second.T)
    kv_arrived(0, dkv_core)
    for index in range(4):
        for micro in range(2):
            dkv[core, index, micro] = bf(f32(dkv[core, index, micro]) + f32(dkv_core[index, micro]))
    for flip in (1, 2, 3):
        kv_start(flip, dkv.at[core, z ^ flip], dkv_z.at[flip - 1], (dp, seq ^ (2 * flip)))
    scatter_a.diagonal()
    loads[2].wait()
    loads[3].wait()

    def chunk(flip, first):
        base = (dp ^ flip) * 768

        def tile(number, carry):
            columns = pl.ds(pl.multiple_of(base + number * 256, 256), 256)
            hidden = dot(n2_ref[...], up_ref[:, columns]) + bup_ref[0:1, columns]
            d_act = dot_nt(cot_ref[...], down_ref[columns, :])
            normal = 0.5 + 0.5 * lax.erf(hidden * root_half)
            density = density_scale * jnp.exp(-0.5 * hidden * hidden)
            d_hidden = bf(d_act * (normal + hidden * density))
            act_ref[:, pl.ds(pl.multiple_of(number * 256, 256), 256)] = bf(hidden * normal)
            dh_ref[:, columns] = d_hidden
            return carry

        lax.fori_loop(0, 3, tile, 0)
        down_rows = pl.ds(pl.multiple_of(base, 768), 768)
        part = dot(act_ref[...], down_ref[down_rows, :])
        mlp_ref[...] = part if first else mlp_ref[...] + part

        grad_t = bf(f32(act_ref[...]).T)
        for number in range(4):
            grad = dot(grad_t[192 * number : 192 * number + 192], cot_ref[...])
            for half in range(2):
                d_slabs[dp ^ flip, half, number] = bf(grad[96 * half : 96 * half + 96])
        scatter_d.to_core(flip)

    def put(store, block, flip, rows):
        for index in range(4):
            for half in range(2):
                first = (2 * index + half) * rows
                store(dp ^ flip, half, index, bf(block[first : first + rows]))

    def up_block(flip, left):
        rows = pl.ds(pl.multiple_of((dp ^ flip) * 192, 192), 192)
        if left:

            def put_left(target, half, index, piece):
                u_slabs[target, half, index, :, 0:1536] = piece

            def put_kv(target, half, index, piece):
                u_slabs[target, half, index, :, 1536:1664] = piece

            put(put_left, dot(n2t_ref[rows, :], dh_ref[:, 0:1536]), flip, 24)
            put(put_kv, dot(n1t_ref[rows, :], dshared_ref[...]), flip, 24)
            scatter_u.to_core(flip)
        else:

            def put_right(target, half, index, piece):
                v_slabs[target, half, index] = piece

            put(put_right, dot(n2t_ref[rows, :], dh_ref[:, 1536:3072]), flip, 24)
            scatter_v.to_core(flip)

    chunk(3, True)
    scatter_a.beside(1)
    scatter_a.beside(2)
    chunk(1, False)
    scatter_d.diagonal()
    for flip in (1, 2, 3):
        kv_arrived(flip, dkv_z.at[flip - 1])
    cosine, sine_part = cos_ref[...], sin_ref[...]
    for micro in range(2):
        cols = slice(micro * MINI, (micro + 1) * MINI)
        total = f32(dkv[core, z, micro])
        for flip in (1, 2, 3):
            total = total + f32(dkv_z[flip - 1, micro])
        total_t = total.T
        total_t = jnp.concatenate(
            [rotate_rows(total_t[:HD], cosine[:, cols], -sine_part[:, cols]), total_t[HD:]], axis=0
        )
        dshared_ref[cols, :] = bf(total_t.T)
    chunk(2, False)
    scatter_a.own()
    scatter_d.beside(1)
    chunk(0, False)
    scatter_d.beside(2)
    up_block(3, True)
    up_block(1, True)
    scatter_u.diagonal()
    up_block(2, True)
    up_block(0, True)
    scatter_d.own()
    up_block(3, False)
    up_block(1, False)
    scatter_u.beside(1)
    scatter_u.beside(2)
    scatter_v.diagonal()
    up_block(2, False)
    up_block(0, False)

    zero = jnp.zeros((1, 768), jnp.float32)
    sums = [zero] * 5
    for start in range(0, 2 * MINI, 128):
        rows = slice(start, start + 128)
        values = f32(x_ref[rows, :])
        upstream = f32(cot_ref[rows, :])
        inverse = stats[rows, 0:1]
        normed = (values - jnp.mean(values, axis=-1, keepdims=True)) * inverse
        out_ref[rows, :] = bf(values + attn_ref[rows, :] + mlp_ref[rows, :] + vectors[6:7])
        first = dn_ref[rows, :] + dot_nt(dshared_ref[rows, :], wkv_ref[...])
        second = dot_nt(dh_ref[rows, :], up_ref[...])
        gin_ref[rows, :] = (
            upstream
            + norm_back(first, normed, inverse, vectors[0:1])
            + norm_back(second, normed, inverse, vectors[2:3])
        )
        news = (first * normed, first, second * normed, second, upstream)
        sums = [total + jnp.sum(new, axis=0, keepdims=True) for total, new in zip(sums, news)]
    b_up_sum = jnp.sum(f32(dh_ref[...]), axis=0, keepdims=True)
    kv_sum = jnp.sum(f32(dshared_ref[...]), axis=0, keepdims=True)
    small[0] = jnp.concatenate(
        sums[:4]
        + [dqsum_ref[...], sums[4], sums[4], zero]
        + [b_up_sum[:, 768 * n : 768 * n + 768] for n in range(4)]
        + [jnp.concatenate([kv_sum, zero[:, 128:]], axis=1)]
        + [zero] * 3,
        axis=0,
    )
    partners = [(dp, seq ^ 1), (dp, seq ^ 2), (dp, seq ^ 4), (dp ^ 1, seq), (dp ^ 2, seq)]
    small_sent = []

    def small_start(number):
        copy = remote(small.at[number], small_in.at[number], send_m.at[number], recv_m.at[number], partners[number])
        copy.start()
        small_sent.append(copy)

    def small_end(number):
        small_sent[number].wait_recv()
        small[number + 1] = small[number] + small_in[number]

    small_start(0)
    total = scatter_a.total()
    gq_ref[...] = total[:, :768]
    go_ref[...] = total[:, 768:]
    small_end(0)
    small_start(1)
    scatter_v.beside(1)
    scatter_v.beside(2)
    small_end(1)
    small_start(2)
    scatter_u.own()
    gd_ref[...] = scatter_d.total()
    small_end(2)
    small_start(3)
    scatter_v.own()
    small_end(3)
    small_start(4)
    total = scatter_u.total()
    gu_ref[:, 0:1536] = total[:, 0:1536]
    gkv_ref[...] = total[:, 1536:1664]
    small_end(4)
    small_out[...] = small[5]
    gu_ref[:, 1536:3072] = scatter_v.total()
    for scatter in (scatter_a, scatter_d, scatter_u, scatter_v):
        scatter.finish()
    for copy in kv_sent + small_sent:
        copy.wait_send()


def feed_forward(x, cot, cosine, sine_part, up_slabs, down_slabs, vec, bup, wkv, attn, dn1, dkv, grads_a, dq_sum):
    rows = x.shape[0]
    dma = pltpu.SemaphoreType.DMA
    out = jax.ShapeDtypeStruct
    b16 = jnp.bfloat16
    shapes = ((24, 1536), (96, 768), (24, 1664), (24, 1536))
    buffers = [pltpu.VMEM((4, 2, 4) + shape, b16) for shape in shapes]
    for shape in shapes:
        for lead in ((4, 4), (2, 2), (2, 4), (3,)):
            buffers.append(pltpu.VMEM(lead + shape, b16))
    out_rows, g_in, g_query, g_out, g_up, g_kv, g_down, small = pl.pallas_call(
        feed_kernel,
        out_shape=(
            out((rows, 768), b16),
            out((rows, 768), jnp.float32),
            out((24, 768), jnp.float32),
            out((24, 768), jnp.float32),
            out((24, 3072), jnp.float32),
            out((24, 128), jnp.float32),
            out((96, 768), jnp.float32),
            out((16, 768), jnp.float32),
        ),
        in_specs=[VM] * 10 + [HBM] * 4,
        out_specs=(VM,) * 8,
        scratch_shapes=[
            pltpu.VMEM((768, 3072), b16),
            pltpu.VMEM((3072, 768), b16),
            pltpu.VMEM((768, rows), b16),
            pltpu.VMEM((rows, 768), b16),
            pltpu.VMEM((768, rows), b16),
            pltpu.VMEM((rows, 768), b16),
            pltpu.VMEM((rows, 3072), b16),
            pltpu.VMEM((rows, 768), jnp.float32),
            pltpu.VMEM((rows, 2 * HD), b16),
            pltpu.VMEM((rows, 128), jnp.float32),
        ]
        + buffers
        + [
            pltpu.VMEM((2, 4, 2, MINI, 2 * HD), b16),
            pltpu.VMEM((4, 2, MINI, 2 * HD), b16),
            pltpu.VMEM((3, 2, MINI, 2 * HD), b16),
            pltpu.VMEM((6, 16, 768), jnp.float32),
            pltpu.VMEM((5, 16, 768), jnp.float32),
            dma((4, 11)),
            dma((4, 11)),
            dma((4,)),
            dma((4,)),
            dma((5,)),
            dma((5,)),
            dma((4,)),
        ],
        compiler_params=pltpu.CompilerParams(
            collective_id=1, has_side_effects=True, vmem_limit_bytes=63 << 20
        ),
        name="feed_forward",
    )(
        x, cot, cosine, sine_part, vec, bup, wkv, attn, dn1, dq_sum, dkv, grads_a,
        up_slabs.reshape(768, 3072), down_slabs.reshape(3072, 768),
    )
    device = lax.axis_index("dp") * 8 + lax.axis_index("seq")
    g_vectors = lax.dynamic_slice_in_dim(small[:7], device * 24, 24, 1)
    g_b_up = lax.dynamic_slice_in_dim(small[8:12].reshape(3072), device * 96, 96, 0)
    return (
        out_rows.reshape(2, 1, MINI, 768), g_in.reshape(2, 1, MINI, 768), g_query, g_kv, g_out,
        g_up, g_down, g_b_up, g_vectors, small[12, :128],
    )


def solution(mesh):
    packed = mesh.shape["dp"] == 4 and mesh.shape["seq"] == 8
    on_device = packed_on_device if packed else plain_on_device

    in_specs = (
        P(None, "dp", "seq", None),
        P(None, "dp", "seq"),
        P(("dp", "seq"), None),
        P(("dp", "seq"), None),
        P(("dp", "seq"), None),
        P(("dp", "seq"), None),
        P(("dp", "seq"), None),
        P(("dp", "seq")),
        P(None, ("dp", "seq")),
        P(),
        P(None, "dp", "seq", None),
    )
    out_specs = (
        P(None, "dp", "seq", None),
        P(None, "dp", "seq", None),
        P(("dp", "seq"), None),
        P(("dp", "seq"), None),
        P(("dp", "seq"), None),
        P(("dp", "seq"), None),
        P(("dp", "seq"), None),
        P(("dp", "seq")),
        P(None, ("dp", "seq")),
        P(),
    )
    return jax.shard_map(
        on_device, mesh=mesh, in_specs=in_specs, out_specs=out_specs, check_vma=False
    )
```

```python
import functools
import math

import jax
import jax.numpy as jnp
from jax import lax
from jax.experimental import pallas as pl
from jax.experimental.pallas import tpu as pltpu
from jax.sharding import PartitionSpec as P

H = 12
HD = 64
ROT = 16


epsilon = 1e-05
root_half = 0.7071067811865476
density_scale = 0.3989422804014327
masked_score = -1e30


def normalize(values):
    average = jnp.mean(values, axis=-1, keepdims=True)
    centered = values - average
    inverse = lax.rsqrt(jnp.mean(centered * centered, axis=-1, keepdims=True) + epsilon)
    return (centered * inverse, inverse)


def norm_back(grad_out, normed, inverse, gain_row):
    scaled = grad_out * gain_row
    first_mean = jnp.mean(scaled, axis=-1, keepdims=True)
    second_mean = jnp.mean(scaled * normed, axis=-1, keepdims=True)
    return inverse * (scaled - first_mean - normed * second_mean)


def rotate(values, cosine, sine_part):
    half_rot = ROT // 2
    first_part = values[..., :half_rot]
    second = values[..., half_rot:ROT]
    return jnp.concatenate(
        [
            first_part * cosine - second * sine_part,
            second * cosine + first_part * sine_part,
            values[..., ROT:],
        ],
        axis=-1,
    )


def gelu_slope(hidden):
    return 0.5 * (1.0 + lax.erf(hidden * root_half)) + hidden * density_scale * jnp.exp(
        -0.5 * hidden * hidden
    )


def tree_add(left_tree, right_tree):
    return tuple((left_item + right_item for left_item, right_item in zip(left_tree, right_tree)))


def plain_on_device(inputs, offsets, w_query, w_kv, w_out, w_up, w_down, b_up, vectors, b_kv, cotangent):
    micro_count = inputs.shape[0]
    local_rows = inputs.shape[2]
    model_width = inputs.shape[3]
    seqlen = local_rows * lax.axis_size("seq")
    key_block = math.gcd(seqlen, 512)
    first_row = lax.axis_index("seq") * local_rows
    blocks_used = (first_row + local_rows + key_block - 1) // key_block
    row_ids = first_row + jnp.arange(local_rows, dtype=jnp.int32)
    half_rot = ROT // 2
    frequency = jnp.power(10000.0, -jnp.arange(half_rot, dtype=jnp.float32) * (2.0 / ROT))
    kv_bias = b_kv.astype(jnp.float32)
    results = []
    input_grads = []
    totals = None
    kv_bias_total = jnp.zeros(b_kv.shape, jnp.float32)
    for micro_index in range(micro_count):
        values_in = inputs[micro_index, 0].astype(jnp.float32)
        row_offsets = offsets[micro_index, 0]
        upstream = cotangent[micro_index, 0]
        upstream_f = upstream.astype(jnp.float32)
        angle = (row_offsets.astype(jnp.float32) * 0.25)[:, None] * frequency[None, :]
        cosine = jnp.cos(angle)
        sine_part = jnp.sin(angle)
        gathered = (
            lax.all_gather(w_query, ("dp", "seq"), axis=0, tiled=True),
            lax.all_gather(w_kv, ("dp", "seq"), axis=0, tiled=True),
            lax.all_gather(w_out, ("dp", "seq"), axis=0, tiled=True),
            lax.all_gather(w_up, ("dp", "seq"), axis=0, tiled=True),
            lax.all_gather(w_down, ("dp", "seq"), axis=0, tiled=True),
            lax.all_gather(b_up, ("dp", "seq"), axis=0, tiled=True),
            lax.all_gather(vectors, ("dp", "seq"), axis=1, tiled=True),
        )
        query_full, kv_full, out_full, up_full, down_full, up_bias, vector_full = gathered
        vector_f = vector_full.astype(jnp.float32)
        normed1, inverse1 = normalize(values_in)
        hidden1 = (normed1 * vector_f[0] + vector_f[1]).astype(jnp.bfloat16)
        query_pre = jnp.dot(hidden1, query_full, preferred_element_type=jnp.float32) + vector_f[4]
        kv_pre = jnp.dot(hidden1, kv_full, preferred_element_type=jnp.float32) + kv_bias
        queries = rotate(
            query_pre.reshape(local_rows, H, HD), cosine[:, None, :], sine_part[:, None, :]
        ).astype(jnp.bfloat16)
        shared_local = jnp.concatenate(
            [rotate(kv_pre[:, :HD], cosine, sine_part), kv_pre[:, HD:]], axis=1
        ).astype(jnp.bfloat16)
        shared = lax.all_gather(shared_local, "seq", axis=0, tiled=True)

        def block_scores(number):
            start_row = number * key_block
            key_piece = lax.dynamic_slice_in_dim(shared, start_row, key_block, 0)
            columns = start_row + jnp.arange(key_block, dtype=jnp.int32)
            allowed = (columns[None, :] <= row_ids[:, None]) & (
                row_ids[:, None] - columns[None, :] <= row_offsets[:, None]
            )
            scores = (
                jnp.einsum(
                    "rhd,kd->hrk", queries, key_piece[:, :HD], preferred_element_type=jnp.float32
                )
                * 0.125
            )
            return (jnp.where(allowed[None], scores, masked_score), key_piece)

        def max_step(number, state_pair):
            running_top, denominator = state_pair
            scores, key_piece = block_scores(number)
            new_top = jnp.maximum(running_top, jnp.max(scores, axis=-1))
            denominator = denominator * jnp.exp(running_top - new_top) + jnp.sum(
                jnp.exp(scores - new_top[..., None]), axis=-1
            )
            return (new_top, denominator)

        start_top = jnp.full((H, local_rows), masked_score, jnp.float32)
        running_top, denominator = lax.fori_loop(
            0, blocks_used, max_step, (start_top, jnp.zeros((H, local_rows), jnp.float32))
        )
        log_total = running_top + jnp.log(denominator)

        def value_step(number, accumulated):
            scores, key_piece = block_scores(number)
            soft_weights = jnp.exp(scores - log_total[..., None]).astype(jnp.bfloat16)
            return accumulated + jnp.einsum(
                "hrk,kd->rhd", soft_weights, key_piece[:, HD:], preferred_element_type=jnp.float32
            )

        attended_f = lax.fori_loop(
            0, blocks_used, value_step, jnp.zeros((local_rows, H, HD), jnp.float32)
        )
        attended = attended_f.reshape(local_rows, model_width).astype(jnp.bfloat16)
        attn_out = jnp.dot(attended, out_full, preferred_element_type=jnp.float32) + vector_f[5]
        normed2, inverse2 = normalize(values_in)
        hidden2 = (normed2 * vector_f[2] + vector_f[3]).astype(jnp.bfloat16)
        hidden_up = jnp.dot(hidden2, up_full, preferred_element_type=jnp.float32) + up_bias.astype(
            jnp.float32
        )
        activated = jax.nn.gelu(hidden_up, approximate=False).astype(jnp.bfloat16)
        mlp_out = jnp.dot(activated, down_full, preferred_element_type=jnp.float32) + vector_f[6]
        results.append((values_in + attn_out + mlp_out).astype(jnp.bfloat16))
        regathered = (
            lax.all_gather(w_query, ("dp", "seq"), axis=0, tiled=True),
            lax.all_gather(w_kv, ("dp", "seq"), axis=0, tiled=True),
            lax.all_gather(w_out, ("dp", "seq"), axis=0, tiled=True),
            lax.all_gather(w_up, ("dp", "seq"), axis=0, tiled=True),
            lax.all_gather(w_down, ("dp", "seq"), axis=0, tiled=True),
            lax.all_gather(b_up, ("dp", "seq"), axis=0, tiled=True),
            lax.all_gather(vectors, ("dp", "seq"), axis=1, tiled=True),
        )
        query_back, kv_back, out_back, up_back, down_back, up_bias_back, vector_back = regathered
        vector_back_f = vector_back.astype(jnp.float32)
        grad_w_down = jnp.einsum(
            "rf,rd->fd", activated, upstream, preferred_element_type=jnp.float32
        )
        d_act = jnp.einsum("rd,fd->rf", upstream, down_back, preferred_element_type=jnp.float32)
        d_hidden = (d_act * gelu_slope(hidden_up)).astype(jnp.bfloat16)
        grad_w_up = jnp.einsum("rd,rf->df", hidden2, d_hidden, preferred_element_type=jnp.float32)
        grad_b_up = jnp.sum(d_hidden.astype(jnp.float32), axis=0)
        d_normed2 = jnp.einsum("rf,df->rd", d_hidden, up_back, preferred_element_type=jnp.float32)
        grad_w_out = jnp.einsum("rd,re->de", attended, upstream, preferred_element_type=jnp.float32)
        d_attended = (
            jnp.einsum("re,de->rd", upstream, out_back, preferred_element_type=jnp.float32)
            .astype(jnp.bfloat16)
            .reshape(local_rows, H, HD)
        )

        def delta_step(number, accumulated):
            scores, key_piece = block_scores(number)
            soft_probs = jnp.exp(scores - log_total[..., None])
            d_probs = jnp.einsum(
                "rhd,kd->hrk", d_attended, key_piece[:, HD:], preferred_element_type=jnp.float32
            )
            return accumulated + jnp.sum(soft_probs * d_probs, axis=-1)

        delta = lax.fori_loop(0, blocks_used, delta_step, jnp.zeros((H, local_rows), jnp.float32))

        def grad_step(number, state_pair):
            d_query_rot, d_shared_all = state_pair
            start_row = number * key_block
            scores, key_piece = block_scores(number)
            soft_probs = jnp.exp(scores - log_total[..., None])
            d_probs = jnp.einsum(
                "rhd,kd->hrk", d_attended, key_piece[:, HD:], preferred_element_type=jnp.float32
            )
            d_scores = (soft_probs * (d_probs - delta[..., None])).astype(jnp.bfloat16)
            d_query_rot = (
                d_query_rot
                + jnp.einsum(
                    "hrk,kd->rhd", d_scores, key_piece[:, :HD], preferred_element_type=jnp.float32
                )
                * 0.125
            )
            d_keys = (
                jnp.einsum("hrk,rhd->kd", d_scores, queries, preferred_element_type=jnp.float32)
                * 0.125
            )
            d_values = jnp.einsum(
                "hrk,rhd->kd",
                soft_probs.astype(jnp.bfloat16),
                d_attended,
                preferred_element_type=jnp.float32,
            )
            current = lax.dynamic_slice_in_dim(d_shared_all, start_row, key_block, 0)
            d_shared_all = lax.dynamic_update_slice_in_dim(
                d_shared_all, current + jnp.concatenate([d_keys, d_values], axis=1), start_row, 0
            )
            return (d_query_rot, d_shared_all)

        d_query_rot, d_shared_all = lax.fori_loop(
            0,
            blocks_used,
            grad_step,
            (jnp.zeros((local_rows, H, HD), jnp.float32), jnp.zeros((seqlen, 2 * HD), jnp.float32)),
        )
        d_shared_mine = lax.psum_scatter(
            d_shared_all.astype(jnp.bfloat16), "seq", scatter_dimension=0, tiled=True
        ).astype(jnp.float32)
        d_shared = jnp.concatenate(
            [rotate(d_shared_mine[:, :HD], cosine, -sine_part), d_shared_mine[:, HD:]], axis=1
        ).astype(jnp.bfloat16)
        d_queries = (
            rotate(d_query_rot, cosine[:, None, :], -sine_part[:, None, :])
            .reshape(local_rows, model_width)
            .astype(jnp.bfloat16)
        )
        grad_w_query = jnp.einsum(
            "rd,re->de", hidden1, d_queries, preferred_element_type=jnp.float32
        )
        grad_w_kv = jnp.einsum("rd,rc->dc", hidden1, d_shared, preferred_element_type=jnp.float32)
        kv_bias_total = kv_bias_total + jnp.sum(d_shared.astype(jnp.float32), axis=0)
        d_normed1 = jnp.einsum(
            "re,de->rd", d_queries, query_back, preferred_element_type=jnp.float32
        ) + jnp.einsum("rc,dc->rd", d_shared, kv_back, preferred_element_type=jnp.float32)
        upstream_sum = jnp.sum(upstream_f, axis=0)
        grad_vectors = jnp.stack(
            [
                jnp.sum(d_normed1 * normed1, axis=0),
                jnp.sum(d_normed1, axis=0),
                jnp.sum(d_normed2 * normed2, axis=0),
                jnp.sum(d_normed2, axis=0),
                jnp.sum(d_queries.astype(jnp.float32), axis=0),
                upstream_sum,
                upstream_sum,
            ]
        )
        input_grads.append(
            upstream_f
            + norm_back(d_normed1, normed1, inverse1, vector_back_f[0])
            + norm_back(d_normed2, normed2, inverse2, vector_back_f[2])
        )
        shares = (
            lax.psum_scatter(grad_w_query, ("dp", "seq"), scatter_dimension=0, tiled=True),
            lax.psum_scatter(grad_w_kv, ("dp", "seq"), scatter_dimension=0, tiled=True),
            lax.psum_scatter(grad_w_out, ("dp", "seq"), scatter_dimension=0, tiled=True),
            lax.psum_scatter(grad_w_up, ("dp", "seq"), scatter_dimension=0, tiled=True),
            lax.psum_scatter(grad_w_down, ("dp", "seq"), scatter_dimension=0, tiled=True),
            lax.psum_scatter(grad_b_up, ("dp", "seq"), scatter_dimension=0, tiled=True),
            lax.psum_scatter(grad_vectors, ("dp", "seq"), scatter_dimension=1, tiled=True),
        )
        totals = shares if totals is None else tree_add(totals, shares)
    kv_bias_grad = lax.psum(kv_bias_total, ("dp", "seq"))
    return (
        jnp.stack(results)[:, None],
        jnp.stack(input_grads)[:, None],
        totals[0],
        totals[1],
        totals[2],
        totals[3],
        totals[4],
        totals[5],
        totals[6],
        kv_bias_grad,
    )


MESH = pl.DeviceIdType.MESH
NT = (((1,), (1,)), ((), ()))
VM = pl.BlockSpec(memory_space=pltpu.VMEM)
HBM = pl.BlockSpec(memory_space=pl.ANY)
GROUP = 4
KEYS = 512
MINI = 256
scale_log2 = 0.125 * 1.4426950408889634


def dot(left, right):
    return jnp.dot(left, right, preferred_element_type=jnp.float32)


def dot_nt(left, right):
    return lax.dot_general(left, right, NT, preferred_element_type=jnp.float32)


def bf(values):
    return values.astype(jnp.bfloat16)


def f32(values):
    return values.astype(jnp.float32)


def rotate_rows(block, cosine, sine_part):
    half_rot = ROT // 2
    first, second = block[:half_rot], block[half_rot:ROT]
    return jnp.concatenate(
        [first * cosine - second * sine_part, second * cosine + first * sine_part, block[ROT:]],
        axis=0,
    )


def here():
    return lax.axis_index("dp"), lax.axis_index("seq")


def greet(targets):
    barrier = pltpu.get_barrier_semaphore()
    for target in targets:
        pl.semaphore_signal(barrier, inc=1, device_id=target, device_id_type=MESH)
    pl.semaphore_wait(barrier, len(targets))


def remote(source, target, send, recv, device):
    return pltpu.make_async_remote_copy(
        src_ref=source,
        dst_ref=target,
        send_sem=send,
        recv_sem=recv,
        device_id=device,
        device_id_type=MESH,
    )


class Gather:
    def __init__(self, shard, slabs, halves, send, recv):
        self.shard, self.slabs, self.halves, self.send, self.recv = shard, slabs, halves, send, recv
        self.dp, self.seq = here()
        self.sent = []

    def index(self, dp_flip, z_flip, core_flip=0):
        return (self.dp ^ dp_flip) * 8 + (self.seq ^ (2 * z_flip + core_flip))

    def part(self, slab, half):
        rows, columns = half
        return self.slabs.at[slab, rows, columns]

    def start(self, number, source, target, device):
        copy = remote(source, target, self.send.at[number], self.recv.at[number], device)
        copy.start()
        self.sent.append(copy)

    def arrived(self, number, target):
        remote(target, target, self.send.at[number], self.recv.at[number], (self.dp, self.seq ^ 1)).wait_recv()

    def along_z(self, flip):
        self.start(flip - 1, self.shard, self.slabs.at[self.index(0, 0)], (self.dp, self.seq ^ (2 * flip)))

    def own(self):
        mine = self.slabs.at[self.index(0, 0)]
        self.start(3, self.shard, mine, (self.dp ^ 1, self.seq))
        self.start(7, self.shard, mine, (self.dp ^ 2, self.seq))
        self.start(19, self.shard, mine, (self.dp, self.seq ^ 1))

    def from_z(self, flip):
        piece = self.slabs.at[self.index(0, flip)]
        self.arrived(flip - 1, piece)
        self.start(3 + flip, piece, piece, (self.dp ^ 1, self.seq))
        self.start(7 + flip, piece, piece, (self.dp ^ 2, self.seq))
        if flip == 2:
            self.start(2, piece, piece, (self.dp, self.seq ^ 2))
        self.start(19 + flip, piece, piece, (self.dp, self.seq ^ 1))

    def from_xy(self, flip):
        for axis, half in ((1, 0), (2, 1)):
            number = 3 if axis == 1 else 7
            slab = self.index(axis, flip)
            piece = self.slabs.at[slab]
            self.arrived(number + flip, piece)
            cut = self.part(slab, self.halves[half])
            self.start(11 + 4 * half + flip, cut, cut, (self.dp ^ (3 - axis), self.seq))
            self.start((23 if axis == 1 else 27) + flip, piece, piece, (self.dp, self.seq ^ 1))

    def from_diagonal(self, flip):
        slab = self.index(3, flip)
        for half in (0, 1):
            self.arrived(11 + 4 * half + flip, self.part(slab, self.halves[half]))
        piece = self.slabs.at[slab]
        self.start(31 + flip, piece, piece, (self.dp, self.seq ^ 1))

    def from_core(self):
        for number, dp_flip in ((19, 0), (23, 1), (27, 2), (31, 3)):
            for flip in range(4):
                self.arrived(number + flip, self.slabs.at[self.index(dp_flip, flip, 1)])

    def finish(self):
        for copy in self.sent:
            copy.wait_send()


def attend(
    micro, steps, row0, off_ref, q_t, do_t, kv_ref, kv_t, att_t, dq_t, dkv, pair, scaled, score_ref, weight_ref, tick
):
    cols = slice(micro * MINI, (micro + 1) * MINI)
    row_ids = row0 + lax.broadcasted_iota(jnp.int32, (1, MINI), 1)
    begin = row_ids - off_ref[micro]
    for group in range(H // GROUP):
        heads = [slice((group * GROUP + n) * HD, (group * GROUP + n + 1) * HD) for n in range(GROUP)]
        for n, head in enumerate(heads):
            pair[n, :HD, :MINI] = q_t[head, cols]
            pair[n, HD:, MINI:] = do_t[head, cols]

        def score_step(step, tops):
            keys = pl.ds(pl.multiple_of(step * KEYS, KEYS), KEYS)
            block = kv_ref[micro, keys, :]
            ids = step * KEYS + lax.broadcasted_iota(jnp.int32, (KEYS, 1), 0)
            allowed = (ids <= row_ids) & (ids >= begin)
            found = []
            for n in range(GROUP):
                both = dot(block, pair[n])
                scores = jnp.where(allowed, both[:, :MINI] * scale_log2, masked_score)
                score_ref[n, keys, :MINI] = scores
                score_ref[n, keys, MINI:] = both[:, MINI:]
                found.append(jnp.maximum(tops[n], jnp.max(scores.reshape(KEYS // 8, 8, MINI), axis=0)))
            return tuple(found)

        tops = lax.fori_loop(
            0, steps, score_step, tuple(jnp.full((8, MINI), masked_score, jnp.float32) for _ in heads)
        )
        tops = [jnp.max(top, axis=0, keepdims=True) for top in tops]
        tick()

        def value_step(step, carried):
            keys = pl.ds(pl.multiple_of(step * KEYS, KEYS), KEYS)
            values = kv_t[micro, HD:, keys]
            found = []
            for n in range(GROUP):
                output, total = carried[n]
                weights = jnp.exp2(score_ref[n, keys, :MINI] - tops[n])
                total = total + jnp.sum(weights.reshape(KEYS // 8, 8, MINI), axis=0)
                weight_ref[n, keys, :] = bf(weights)
                found.append((output + dot(values, bf(weights)), total))
            return tuple(found)

        sums = lax.fori_loop(
            0,
            steps,
            value_step,
            tuple((jnp.zeros((HD, MINI), jnp.float32), jnp.zeros((8, MINI), jnp.float32)) for _ in heads),
        )
        tick()
        inverses, deltas = [], []
        for n, head in enumerate(heads):
            inverse = 1.0 / jnp.sum(sums[n][1], axis=0, keepdims=True)
            output = sums[n][0] * inverse
            upstream = f32(do_t[head, cols])
            deltas.append(jnp.sum(output * upstream, axis=0, keepdims=True))
            inverses.append(inverse)
            att_t[head, cols] = bf(output)
            scaled[n, :HD, :MINI] = bf(f32(q_t[head, cols]) * inverse)
            scaled[n, HD:, MINI:] = bf(upstream * inverse)

        def grad_step(step, carried):
            keys = pl.ds(pl.multiple_of(step * KEYS, KEYS), KEYS)
            key_block = kv_t[micro, :HD, keys]
            total = dkv[micro, keys, :]
            found = []
            for n in range(GROUP):
                weights = weight_ref[n, keys, :]
                d_scores = bf(f32(weights) * (score_ref[n, keys, MINI:] - deltas[n]))
                found.append(carried[n] + dot(key_block, d_scores))
                total = total + dot_nt(d_scores, scaled[n, :, :MINI])
                total = total + dot_nt(weights, scaled[n, :, MINI:])
            dkv[micro, keys, :] = total
            return tuple(found)

        grads = lax.fori_loop(
            0, steps, grad_step, tuple(jnp.zeros((HD, MINI), jnp.float32) for _ in heads)
        )
        for n, head in enumerate(heads):
            dq_t[head, cols] = grads[n] * (inverses[n] * 0.125)
        tick()


def spread(slabs):
    lane = lax.broadcasted_iota(jnp.int32, (8, 128), 1)
    row = lax.broadcasted_iota(jnp.int32, (8, 128), 0)
    rows = [jnp.zeros((8, 128), jnp.float32) for _ in range(6)]
    wide = [jnp.zeros((8, 128), jnp.float32) for _ in range(24)]
    for number in range(32):
        for width, target, keep in ((24, rows, row < 7), (96, wide, row == 7)):
            block, shift = divmod(number * width, 128)
            piece = jnp.where(keep, slabs[number], 0.0)
            piece = pltpu.roll(piece, shift, 1) if shift else piece
            target[block] = target[block] + jnp.where(lane >= shift, piece, 0.0)
            if shift + width > 128:
                target[block + 1] = target[block + 1] + jnp.where(lane < shift, piece, 0.0)
    return jnp.concatenate(rows, axis=1), jnp.concatenate(wide, axis=1)


def slab_order(store, block, dp_index, rows):
    for z in range(4):
        for core in range(2):
            first = (2 * z + core) * rows
            store(dp_index, core, z, bf(block[first : first + rows]))


def attention_kernel(
    x_ref, cot_ref, off_ref, wq_ref, wkv_in, wout_ref, vec_in, bup_in, bkv_ref, up_ref, down_ref,
    up_slabs, down_slabs, vec_ref, bup_ref, wkv_ref, cos_ref, sin_ref, attn_ref, dn_ref, dkv_out, grads_ref, dqsum_ref,
    small_ref, pair_ref, extra, slabs, pair_slabs, weights, out_weights, n1t_ref, q_t, do_t, att_t, dq_t, kv_ref, kv_t, dkv, pair, scaled,
    score_ref, weight_ref,
    send_a, recv_a, send_o, recv_o, send_u, recv_u, send_d, recv_d, send_kv, recv_kv, local_sem,
):
    dp, seq = here()

    def halves(shape, axis):
        middle = shape[axis] // 2
        cuts = [slice(0, middle), slice(middle, 2 * middle)]
        return tuple((cut, slice(None)) if axis == 0 else (slice(None), cut) for cut in cuts)

    gather_a = Gather(small_ref, slabs, halves(small_ref.shape, 1), send_a, recv_a)
    gather_o = Gather(pair_ref, pair_slabs, halves(pair_ref.shape, 1), send_o, recv_o)
    gather_u = Gather(up_ref, up_slabs, halves(up_ref.shape, 1), send_u, recv_u)
    gather_d = Gather(down_ref, down_slabs, halves(down_ref.shape, 0), send_d, recv_d)

    def signal():
        barrier = pltpu.get_barrier_semaphore()
        for target in friends:
            pl.semaphore_signal(barrier, inc=1, device_id=target, device_id_type=MESH)

    friends = [(dp, seq ^ 1), (dp, seq ^ 2), (dp, seq ^ 4), (dp, seq ^ 6), (dp ^ 1, seq), (dp ^ 2, seq)]
    signal()
    extra[...] = jnp.zeros_like(extra)
    extra[0:7, 0 : vec_in.shape[1]] = f32(vec_in[...])
    extra[7:8, 0 : bup_in.shape[1]] = f32(bup_in[...])
    small_ref[:, 0:128] = wkv_in[...]
    small_ref[:, 128:256] = bf(extra[...])
    pair_ref[:, 0:768] = wq_ref[...]
    pair_ref[:, 768:1536] = wout_ref[...]
    pl.semaphore_wait(pltpu.get_barrier_semaphore(), len(friends))
    for flip in (1, 2):
        gather_a.along_z(flip)
    gather_a.own()
    gather_o.along_z(1)
    gather_o.own()
    gather_u.own()
    mine = gather_a.index(0, 0)
    local_copies = [
        pltpu.make_async_copy(small_ref, slabs.at[mine], local_sem.at[0]),
        pltpu.make_async_copy(pair_ref, pair_slabs.at[mine], local_sem.at[1]),
        pltpu.make_async_copy(up_ref, up_slabs.at[mine], local_sem.at[2]),
        pltpu.make_async_copy(down_ref, down_slabs.at[mine], local_sem.at[3]),
    ]
    for copy in local_copies:
        copy.start()
    pair[...] = jnp.zeros_like(pair)
    scaled[...] = jnp.zeros_like(scaled)
    dkv[...] = jnp.zeros_like(dkv)
    rank = f32(lax.broadcasted_iota(jnp.int32, (ROT // 2, 1), 0))
    frequency = jnp.exp(rank * (-2.0 / ROT * math.log(10000.0)))
    for micro in range(2):
        cols = slice(micro * MINI, (micro + 1) * MINI)
        angle = (f32(off_ref[micro]) * 0.25) * frequency
        cos_ref[:, cols] = jnp.cos(angle)
        sin_ref[:, cols] = jnp.sin(angle)
    normed, _ = normalize(f32(x_ref[...]))
    for flip in (1, 2, 3):
        gather_a.from_z(flip)
    for flip in range(4):
        gather_a.from_xy(flip)
    gather_o.along_z(2)
    gather_o.from_z(1)
    for flip in range(4):
        gather_a.from_diagonal(flip)
    gather_o.from_xy(0)
    gather_u.along_z(1)
    gather_u.along_z(2)
    gather_a.from_core()
    local_copies[0].wait()

    vectors, wide_row = spread([f32(slabs[number, 0:8, 128:256]) for number in range(32)])
    vec_ref[...] = vectors
    bup_ref[...] = wide_row[7:8]

    def unpack(source, target, columns):
        for number in range(16):
            block = jnp.concatenate(
                [f32(source[2 * number, :, columns]), f32(source[2 * number + 1, :, columns])], axis=0
            )
            target[48 * number : 48 * number + 48, :] = bf(block)

    unpack(slabs, wkv_ref, slice(0, 128))
    hidden = bf(normed * vectors[0:1] + vectors[1:2])
    kv_pre = dot(hidden, wkv_ref[...]) + f32(bkv_ref[...])
    kv_pre_t = kv_pre.T
    cosine, sine_part = cos_ref[...], sin_ref[...]
    shared_t = bf(jnp.concatenate([rotate_rows(kv_pre_t[:HD], cosine, sine_part), kv_pre_t[HD:]], axis=0))
    shared = bf(f32(shared_t).T)
    place = pl.ds(pl.multiple_of(seq * MINI, MINI), MINI)
    kv_copies = []
    for micro in range(2):
        kv_ref[micro, place, :] = shared[micro * MINI : (micro + 1) * MINI]

    def kv_block(micro, flip):
        return kv_ref.at[micro, pl.ds(pl.multiple_of((seq ^ flip) * MINI, MINI), MINI)]

    def kv_send(micro, flip, number, device):
        block = kv_block(micro, flip)
        copy = remote(block, block, send_kv.at[micro, number], recv_kv.at[micro, number], device)
        copy.start()
        kv_copies.append(copy)

    def kv_arrived(micro, flip, number):
        block = kv_block(micro, flip)
        remote(block, block, send_kv.at[micro, number], recv_kv.at[micro, number], (dp, seq ^ 1)).wait_recv()

    def kv_start(micro):
        for flip in (1, 2, 3):
            kv_send(micro, 0, flip - 1, (dp, seq ^ (2 * flip)))
        kv_send(micro, 0, 3, (dp, seq ^ 1))

    def kv_forward(micro):
        for flip in (1, 2, 3):
            kv_arrived(micro, 2 * flip, flip - 1)
            kv_send(micro, 2 * flip, 3 + flip, (dp, seq ^ 1))

    def kv_finish(micro):
        for flip in range(4):
            kv_arrived(micro, 2 * flip + 1, 3 + flip)
        kv_t[micro] = bf(f32(kv_ref[micro]).T)

    kv_start(0)
    gather_o.from_z(2)
    gather_o.from_xy(1)
    gather_o.from_diagonal(0)
    gather_o.from_z(3)
    gather_o.from_xy(2)
    gather_o.from_diagonal(1)
    n1t_ref[...] = bf(f32(hidden).T)
    kv_forward(0)
    gather_o.from_xy(3)
    gather_d.along_z(1)
    gather_d.along_z(2)
    gather_d.own()
    gather_u.from_z(1)
    gather_u.from_xy(0)
    gather_o.from_diagonal(2)
    gather_o.from_diagonal(3)
    kv_start(1)
    kv_finish(0)
    local_copies[1].wait()
    gather_o.from_core()
    unpack(pair_slabs, weights, slice(0, 768))
    unpack(pair_slabs, out_weights, slice(768, 1536))
    query = (dot(hidden, weights[...]) + vectors[4:5]).T
    for head in range(H):
        q_t[head * HD : (head + 1) * HD, :] = bf(
            rotate_rows(query[head * HD : (head + 1) * HD], cosine, sine_part)
        )
    do_t[...] = bf(dot_nt(out_weights[...], cot_ref[...]))

    def each(name, *flips):
        def act():
            for gather in (gather_u, gather_d):
                for flip in flips:
                    getattr(gather, name)(flip)

        return act

    def then(*acts):
        def act():
            for one in acts:
                one()

        return act

    actions = [
        lambda: kv_forward(1),
        lambda: gather_d.from_z(1),
        lambda: gather_d.from_xy(0),
        then(each("from_z", 2), lambda: gather_u.from_diagonal(0)),
        each("from_xy", 1),
        lambda: gather_d.from_diagonal(0),
        each("from_z", 3),
        each("from_diagonal", 1),
        each("from_xy", 2),
        None,
        each("from_diagonal", 2),
        None,
        each("from_xy", 3),
        None,
        None,
        each("from_diagonal", 3),
    ]

    def tick():
        act = actions.pop(0) if actions else None
        if act is not None:
            act()

    steps = lax.div((seq + 1) * MINI + KEYS - 1, KEYS)
    for micro in range(2):
        if micro == 1:
            kv_finish(1)
        attend(
            micro, steps, seq * MINI, off_ref, q_t, do_t, kv_ref, kv_t, att_t, dq_t, dkv,
            pair, scaled, score_ref, weight_ref, tick,
        )
    while actions:
        tick()
    for micro in range(2):
        for core in range(2):
            for z in range(4):
                first = (2 * z + core) * MINI
                block = dkv[micro, first : first + MINI, :]
                scale = jnp.where(lax.broadcasted_iota(jnp.int32, (1, 2 * HD), 1) < HD, 0.125, 1.0)
                dkv_out[core, z, micro] = bf(block * scale)
    attn_ref[...] = dot(bf(f32(att_t[...]).T), out_weights[...]) + vectors[5:6]
    for head in range(H):
        dq_t[head * HD : (head + 1) * HD, :] = rotate_rows(
            dq_t[head * HD : (head + 1) * HD, :], cosine, -sine_part
        )
    d_query = bf(dq_t[...].T)
    dqsum_ref[...] = jnp.sum(f32(d_query), axis=0, keepdims=True)
    dn_ref[...] = dot_nt(d_query, weights[...])
    for block in range(4):
        rows = slice(192 * block, 192 * block + 192)

        def put_query(dp_index, core, z, piece):
            grads_ref[dp_index, core, z, :, 0:768] = piece

        def put_out(dp_index, core, z, piece):
            grads_ref[dp_index, core, z, :, 768:1536] = piece

        slab_order(put_query, dot(n1t_ref[rows, :], d_query), block, 24)
        slab_order(put_out, dot(att_t[rows, :], cot_ref[...]), block, 24)
    for gather in (gather_u, gather_d):
        gather.from_core()
    for gather in (gather_a, gather_o, gather_u, gather_d):
        gather.finish()
    for copy in kv_copies:
        copy.wait_send()
    for copy in local_copies[2:]:
        copy.wait()


def attention_call(x, cot, offsets, w_query, w_kv, w_out, vectors, b_up, b_kv, w_up, w_down):
    rows = x.shape[0]
    dma = pltpu.SemaphoreType.DMA
    out = jax.ShapeDtypeStruct
    seqlen = 8 * MINI
    b16 = jnp.bfloat16
    return pl.pallas_call(
        attention_kernel,
        out_shape=(
            out((32,) + w_up.shape, b16),
            out((32,) + w_down.shape, b16),
            out((8, 768), jnp.float32),
            out((1, 3072), jnp.float32),
            out((768, 128), b16),
            out((ROT // 2, rows), jnp.float32),
            out((ROT // 2, rows), jnp.float32),
            out((rows, 768), jnp.float32),
            out((rows, 768), jnp.float32),
            out((2, 4, 2, MINI, 2 * HD), b16),
            out((4, 2, 4, 24, 1536), b16),
            out((1, 768), jnp.float32),
        ),
        in_specs=[VM] * 9 + [HBM] * 2,
        out_specs=(HBM, HBM) + (VM,) * 10,
        scratch_shapes=[
            pltpu.VMEM((24, 256), b16),
            pltpu.VMEM((24, 1536), b16),
            pltpu.VMEM((24, 128), jnp.float32),
            pltpu.VMEM((32, 24, 256), b16),
            pltpu.VMEM((32, 24, 1536), b16),
            pltpu.VMEM((768, 768), b16),
            pltpu.VMEM((768, 768), b16),
            pltpu.VMEM((768, rows), b16),
            pltpu.VMEM((768, rows), b16),
            pltpu.VMEM((768, rows), b16),
            pltpu.VMEM((768, rows), b16),
            pltpu.VMEM((768, rows), jnp.float32),
            pltpu.VMEM((2, seqlen, 2 * HD), b16),
            pltpu.VMEM((2, 2 * HD, seqlen), b16),
            pltpu.VMEM((2, seqlen, 2 * HD), jnp.float32),
            pltpu.VMEM((GROUP, 2 * HD, 2 * MINI), b16),
            pltpu.VMEM((GROUP, 2 * HD, 2 * MINI), b16),
            pltpu.VMEM((GROUP, seqlen, 2 * MINI), jnp.float32),
            pltpu.VMEM((GROUP, seqlen, MINI), b16),
        ]
        + [dma((35,))] * 8
        + [dma((2, 7))] * 2
        + [dma((4,))],
        compiler_params=pltpu.CompilerParams(
            collective_id=0, has_side_effects=True, vmem_limit_bytes=60 << 20
        ),
        name="attention",
    )(x, cot, offsets, w_query, w_kv, w_out, vectors, b_up, b_kv, w_up, w_down)


def packed_on_device(inputs, offsets, w_query, w_kv, w_out, w_up, w_down, b_up, vectors, b_kv, cotangent):
    rows = 2 * MINI
    x = inputs.reshape(rows, 768)
    cot = cotangent.reshape(rows, 768)
    up_slabs, down_slabs, vec, bup, wkv, cosine, sine_part, attn, dn1, dkv, grads_a, dq_sum = attention_call(
        x, cot, offsets, w_query, w_kv, w_out, vectors, b_up.reshape(1, -1), b_kv.reshape(1, -1), w_up, w_down
    )
    return feed_forward(x, cot, cosine, sine_part, up_slabs, down_slabs, vec, bup, wkv, attn, dn1, dkv, grads_a, dq_sum)


class Scatter:
    def __init__(self, slabs, from_core, from_diagonal, from_xy, from_z, send, recv):
        self.slabs, self.from_core, self.from_diagonal = slabs, from_core, from_diagonal
        self.from_xy, self.from_z, self.send, self.recv = from_xy, from_z, send, recv
        self.dp, self.seq = here()
        self.core = lax.rem(self.seq, 2)
        self.z = lax.div(self.seq, 2)
        self.sent = []

    def start(self, number, source, target, device):
        copy = remote(source, target, self.send.at[number], self.recv.at[number], device)
        copy.start()
        self.sent.append(copy)

    def arrived(self, number, target):
        remote(target, target, self.send.at[number], self.recv.at[number], (self.dp, self.seq ^ 1)).wait_recv()

    def block(self, flip):
        return self.slabs.at[self.dp ^ flip, self.core]

    def to_core(self, flip):
        other = self.slabs.at[self.dp ^ flip, 1 - self.core]
        self.start(flip, other, self.from_core.at[flip], (self.dp, self.seq ^ 1))

    def add(self, block, z, terms):
        total = f32(block[z])
        for term in terms:
            total = total + f32(term)
        block[z] = bf(total)

    def diagonal(self):
        block = self.block(3)
        self.arrived(3, self.from_core.at[3])
        for half in (0, 1):
            for z in (2 * half, 2 * half + 1):
                self.add(block, z, [self.from_core[3, z]])
            self.start(4 + half, block.at[pl.ds(2 * half, 2)], self.from_diagonal.at[half], (self.dp ^ (1 + half), self.seq))

    def beside(self, axis):
        half = 2 - axis
        block = self.block(axis)
        self.arrived(axis, self.from_core.at[axis])
        self.arrived(4 + half, self.from_diagonal.at[half])
        for z in range(4):
            terms = [self.from_core[axis, z]]
            if z // 2 == half:
                terms.append(self.from_diagonal[half, z % 2])
            self.add(block, z, terms)
        self.start(5 + axis, block, self.from_xy.at[axis - 1], (self.dp ^ axis, self.seq))

    def own(self):
        block = self.block(0)
        self.arrived(0, self.from_core.at[0])
        for axis in (1, 2):
            self.arrived(5 + axis, self.from_xy.at[axis - 1])
        for z in range(4):
            self.add(block, z, [self.from_core[0, z], self.from_xy[0, z], self.from_xy[1, z]])
        for flip in (1, 2, 3):
            self.start(7 + flip, block.at[self.z ^ flip], self.from_z.at[flip - 1], (self.dp, self.seq ^ (2 * flip)))

    def total(self):
        value = f32(self.slabs[self.dp, self.core, self.z])
        for flip in (1, 2, 3):
            self.arrived(7 + flip, self.from_z.at[flip - 1])
            value = value + f32(self.from_z[flip - 1])
        return value

    def finish(self):
        for copy in self.sent:
            copy.wait_send()


def feed_kernel(
    x_ref, cot_ref, cos_ref, sin_ref, vec_ref, bup_ref, wkv_ref, attn_ref, dn_ref, dqsum_ref, dkv_in, grads_a, up_hbm, down_hbm,
    out_ref, gin_ref, gq_ref, go_ref, gu_ref, gkv_ref, gd_ref, small_out,
    up_ref, down_ref, n1t_ref, n2_ref, n2t_ref, act_ref, dh_ref, mlp_ref, dshared_ref, stats,
    a_slabs, d_slabs, u_slabs, v_slabs,
    a_core, a_diag, a_xy, a_z, d_core, d_diag, d_xy, d_z, u_core, u_diag, u_xy, u_z, v_core, v_diag, v_xy, v_z,
    dkv, dkv_core, dkv_z, small, small_in,
    send_s, recv_s, send_k, recv_k, send_m, recv_m, load_sem,
):
    dp, seq = here()
    core, z = lax.rem(seq, 2), lax.div(seq, 2)
    loads = [
        pltpu.make_async_copy(dkv_in, dkv, load_sem.at[2]),
        pltpu.make_async_copy(grads_a, a_slabs, load_sem.at[3]),
        pltpu.make_async_copy(up_hbm, up_ref, load_sem.at[0]),
        pltpu.make_async_copy(down_hbm, down_ref, load_sem.at[1]),
    ]
    for copy in loads:
        copy.start()
    greet(
        [(dp, seq ^ 1), (dp, seq ^ 2), (dp, seq ^ 4), (dp, seq ^ 6), (dp ^ 1, seq), (dp ^ 2, seq)]
    )
    scatter_a = Scatter(a_slabs, a_core, a_diag, a_xy, a_z, send_s.at[0], recv_s.at[0])
    scatter_d = Scatter(d_slabs, d_core, d_diag, d_xy, d_z, send_s.at[1], recv_s.at[1])
    scatter_u = Scatter(u_slabs, u_core, u_diag, u_xy, u_z, send_s.at[2], recv_s.at[2])
    scatter_v = Scatter(v_slabs, v_core, v_diag, v_xy, v_z, send_s.at[3], recv_s.at[3])
    kv_sent = []

    def kv_start(number, source, target, device):
        copy = remote(source, target, send_k.at[number], recv_k.at[number], device)
        copy.start()
        kv_sent.append(copy)

    def kv_arrived(number, target):
        remote(target, target, send_k.at[number], recv_k.at[number], (dp, seq ^ 1)).wait_recv()

    loads[1].wait()
    for flip in (3, 1, 2, 0):
        scatter_a.to_core(flip)
    loads[0].wait()
    kv_start(0, dkv.at[1 - core], dkv_core, (dp, seq ^ 1))
    scatter_a.diagonal()

    vectors = vec_ref[...]
    for start in range(0, 2 * MINI, MINI):
        rows = slice(start, start + MINI)
        normed, inverse = normalize(f32(x_ref[rows, :]))
        stats[rows, :] = jnp.broadcast_to(inverse, (MINI, 128))
        n1t_ref[:, rows] = bf((normed * vectors[0:1] + vectors[1:2]).T)
        second = normed * vectors[2:3] + vectors[3:4]
        n2_ref[rows, :] = bf(second)
        n2t_ref[:, rows] = bf(second.T)
    kv_arrived(0, dkv_core)
    for index in range(4):
        for micro in range(2):
            dkv[core, index, micro] = bf(f32(dkv[core, index, micro]) + f32(dkv_core[index, micro]))
    for flip in (1, 2, 3):
        kv_start(flip, dkv.at[core, z ^ flip], dkv_z.at[flip - 1], (dp, seq ^ (2 * flip)))
    scatter_a.beside(1)
    scatter_a.beside(2)
    loads[2].wait()
    loads[3].wait()

    def chunk(flip, first):
        base = (dp ^ flip) * 768

        def tile(number, carry):
            columns = pl.ds(pl.multiple_of(base + number * 256, 256), 256)
            hidden = dot(n2_ref[...], up_ref[:, columns]) + bup_ref[0:1, columns]
            d_act = dot_nt(cot_ref[...], down_ref[columns, :])
            normal = 0.5 + 0.5 * lax.erf(hidden * root_half)
            density = density_scale * jnp.exp(-0.5 * hidden * hidden)
            d_hidden = bf(d_act * (normal + hidden * density))
            act_ref[:, pl.ds(pl.multiple_of(number * 256, 256), 256)] = bf(hidden * normal)
            dh_ref[:, columns] = d_hidden
            return carry

        lax.fori_loop(0, 3, tile, 0)
        down_rows = pl.ds(pl.multiple_of(base, 768), 768)
        part = dot(act_ref[...], down_ref[down_rows, :])
        mlp_ref[...] = part if first else mlp_ref[...] + part

        grad_t = bf(f32(act_ref[...]).T)
        for number in range(4):
            grad = dot(grad_t[192 * number : 192 * number + 192], cot_ref[...])
            for half in range(2):
                d_slabs[dp ^ flip, half, number] = bf(grad[96 * half : 96 * half + 96])
        scatter_d.to_core(flip)

    def put(store, block, flip, rows):
        for index in range(4):
            for half in range(2):
                first = (2 * index + half) * rows
                store(dp ^ flip, half, index, bf(block[first : first + rows]))

    def up_block(flip, left):
        rows = pl.ds(pl.multiple_of((dp ^ flip) * 192, 192), 192)
        if left:

            def put_left(target, half, index, piece):
                u_slabs[target, half, index, :, 0:1536] = piece

            def put_kv(target, half, index, piece):
                u_slabs[target, half, index, :, 1536:1664] = piece

            put(put_left, dot(n2t_ref[rows, :], dh_ref[:, 0:1536]), flip, 24)
            put(put_kv, dot(n1t_ref[rows, :], dshared_ref[...]), flip, 24)
            scatter_u.to_core(flip)
        else:

            def put_right(target, half, index, piece):
                v_slabs[target, half, index] = piece

            put(put_right, dot(n2t_ref[rows, :], dh_ref[:, 1536:3072]), flip, 24)
            scatter_v.to_core(flip)

    chunk(3, True)
    scatter_d.diagonal()
    chunk(1, False)
    scatter_a.own()
    scatter_d.beside(1)
    for flip in (1, 2, 3):
        kv_arrived(flip, dkv_z.at[flip - 1])
    cosine, sine_part = cos_ref[...], sin_ref[...]
    for micro in range(2):
        cols = slice(micro * MINI, (micro + 1) * MINI)
        total = f32(dkv[core, z, micro])
        for flip in (1, 2, 3):
            total = total + f32(dkv_z[flip - 1, micro])
        total_t = total.T
        total_t = jnp.concatenate(
            [rotate_rows(total_t[:HD], cosine[:, cols], -sine_part[:, cols]), total_t[HD:]], axis=0
        )
        dshared_ref[cols, :] = bf(total_t.T)
    chunk(2, False)
    scatter_d.beside(2)
    chunk(0, False)
    up_block(3, True)
    up_block(1, True)
    scatter_u.diagonal()
    up_block(2, True)
    up_block(0, True)
    scatter_d.own()
    up_block(3, False)
    up_block(1, False)
    scatter_u.beside(1)
    scatter_u.beside(2)
    scatter_v.diagonal()
    up_block(2, False)
    up_block(0, False)
    zero = jnp.zeros((1, 768), jnp.float32)
    sums = [zero] * 5
    for start in range(0, 2 * MINI, 128):
        rows = slice(start, start + 128)
        values = f32(x_ref[rows, :])
        upstream = f32(cot_ref[rows, :])
        inverse = stats[rows, 0:1]
        normed = (values - jnp.mean(values, axis=-1, keepdims=True)) * inverse
        out_ref[rows, :] = bf(values + attn_ref[rows, :] + mlp_ref[rows, :] + vectors[6:7])
        first = dn_ref[rows, :] + dot_nt(dshared_ref[rows, :], wkv_ref[...])
        second = dot_nt(dh_ref[rows, :], up_ref[...])
        gin_ref[rows, :] = (
            upstream
            + norm_back(first, normed, inverse, vectors[0:1])
            + norm_back(second, normed, inverse, vectors[2:3])
        )
        news = (first * normed, first, second * normed, second, upstream)
        sums = [total + jnp.sum(new, axis=0, keepdims=True) for total, new in zip(sums, news)]
    b_up_sum = jnp.sum(f32(dh_ref[...]), axis=0, keepdims=True)
    kv_sum = jnp.sum(f32(dshared_ref[...]), axis=0, keepdims=True)
    small[0] = jnp.concatenate(
        sums[:4]
        + [dqsum_ref[...], sums[4], sums[4], zero]
        + [b_up_sum[:, 768 * n : 768 * n + 768] for n in range(4)]
        + [jnp.concatenate([kv_sum, zero[:, 128:]], axis=1)]
        + [zero] * 3,
        axis=0,
    )
    partners = [(dp, seq ^ 1), (dp, seq ^ 2), (dp, seq ^ 4), (dp ^ 1, seq), (dp ^ 2, seq)]
    small_sent = []

    def small_start(number):
        copy = remote(small.at[number], small_in.at[number], send_m.at[number], recv_m.at[number], partners[number])
        copy.start()
        small_sent.append(copy)

    def small_end(number):
        small_sent[number].wait_recv()
        small[number + 1] = small[number] + small_in[number]

    total = scatter_a.total()
    gq_ref[...] = total[:, :768]
    go_ref[...] = total[:, 768:]
    small_start(0)
    scatter_v.beside(1)
    scatter_v.beside(2)
    small_end(0)
    small_start(1)
    scatter_u.own()
    small_end(1)
    small_start(2)
    gd_ref[...] = scatter_d.total()
    scatter_v.own()
    small_end(2)
    small_start(3)
    total = scatter_u.total()
    gu_ref[:, 0:1536] = total[:, 0:1536]
    gkv_ref[...] = total[:, 1536:1664]
    small_end(3)
    small_start(4)
    small_end(4)
    small_out[...] = small[5]
    gu_ref[:, 1536:3072] = scatter_v.total()
    for scatter in (scatter_a, scatter_d, scatter_u, scatter_v):
        scatter.finish()
    for copy in kv_sent + small_sent:
        copy.wait_send()


def place_kernel(small, *refs):
    wholes, results = refs[:7], refs[7:17]
    for source, target in zip(wholes, results):
        target[...] = source[...]
    dp, seq = here()
    rows = small[0:8, :]
    shift = lax.rem(768 - 24 * (8 * dp + seq), 768)
    results[7][...] = pltpu.roll(rows, shift, 1)[0:7, 0:24]
    wide = jnp.broadcast_to(small[pl.ds(8 + dp, 1), :], (8, 768))
    shift = lax.rem(768 - 96 * seq, 768)
    results[8][...] = pltpu.roll(wide, shift, 1)[0:1, 0:96]
    results[9][...] = small[12:13, 0 : 2 * HD]


def feed_forward(x, cot, cosine, sine_part, up_slabs, down_slabs, vec, bup, wkv, attn, dn1, dkv, grads_a, dq_sum):
    rows = x.shape[0]
    dma = pltpu.SemaphoreType.DMA
    out = jax.ShapeDtypeStruct
    b16 = jnp.bfloat16
    shapes = ((24, 1536), (96, 768), (24, 1664), (24, 1536))
    buffers = [pltpu.VMEM((4, 2, 4) + shape, b16) for shape in shapes]
    for shape in shapes:
        for lead in ((4, 4), (2, 2), (2, 4), (3,)):
            buffers.append(pltpu.VMEM(lead + shape, b16))
    out_rows, g_in, g_query, g_out, g_up, g_kv, g_down, small = pl.pallas_call(
        feed_kernel,
        out_shape=(
            out((rows, 768), b16),
            out((rows, 768), jnp.float32),
            out((24, 768), jnp.float32),
            out((24, 768), jnp.float32),
            out((24, 3072), jnp.float32),
            out((24, 128), jnp.float32),
            out((96, 768), jnp.float32),
            out((16, 768), jnp.float32),
        ),
        in_specs=[VM] * 10 + [HBM] * 4,
        out_specs=(VM,) * 8,
        scratch_shapes=[
            pltpu.VMEM((768, 3072), b16),
            pltpu.VMEM((3072, 768), b16),
            pltpu.VMEM((768, rows), b16),
            pltpu.VMEM((rows, 768), b16),
            pltpu.VMEM((768, rows), b16),
            pltpu.VMEM((rows, 768), b16),
            pltpu.VMEM((rows, 3072), b16),
            pltpu.VMEM((rows, 768), jnp.float32),
            pltpu.VMEM((rows, 2 * HD), b16),
            pltpu.VMEM((rows, 128), jnp.float32),
        ]
        + buffers
        + [
            pltpu.VMEM((2, 4, 2, MINI, 2 * HD), b16),
            pltpu.VMEM((4, 2, MINI, 2 * HD), b16),
            pltpu.VMEM((3, 2, MINI, 2 * HD), b16),
            pltpu.VMEM((6, 16, 768), jnp.float32),
            pltpu.VMEM((5, 16, 768), jnp.float32),
            dma((4, 11)),
            dma((4, 11)),
            dma((4,)),
            dma((4,)),
            dma((5,)),
            dma((5,)),
            dma((4,)),
        ],
        compiler_params=pltpu.CompilerParams(
            collective_id=1, has_side_effects=True, vmem_limit_bytes=63 << 20
        ),
        name="feed_forward",
    )(
        x, cot, cosine, sine_part, vec, bup, wkv, attn, dn1, dq_sum, dkv, grads_a,
        up_slabs.reshape(768, 3072), down_slabs.reshape(3072, 768),
    )
    wholes = (out_rows, g_in, g_query, g_kv, g_out, g_up, g_down)
    like = tuple(out(one.shape, one.dtype) for one in wholes)
    results = pl.pallas_call(
        place_kernel,
        out_shape=like + (out((7, 24), jnp.float32), out((1, 96), jnp.float32), out((1, 2 * HD), jnp.float32)),
        in_specs=[VM] * (1 + len(wholes)),
        out_specs=(VM,) * (3 + len(wholes)),
        compiler_params=pltpu.CompilerParams(vmem_limit_bytes=62 << 20),
        name="place",
    )(small, *wholes)
    out_rows, g_in, g_query, g_kv, g_out, g_up, g_down, g_vectors, g_b_up, g_b_kv = results
    return (
        out_rows.reshape(2, 1, MINI, 768), g_in.reshape(2, 1, MINI, 768), g_query, g_kv, g_out,
        g_up, g_down, g_b_up.reshape(-1), g_vectors, g_b_kv.reshape(-1),
    )


def solution(mesh):
    packed = mesh.shape["dp"] == 4 and mesh.shape["seq"] == 8
    on_device = packed_on_device if packed else plain_on_device

    in_specs = (
        P(None, "dp", "seq", None),
        P(None, "dp", "seq"),
        P(("dp", "seq"), None),
        P(("dp", "seq"), None),
        P(("dp", "seq"), None),
        P(("dp", "seq"), None),
        P(("dp", "seq"), None),
        P(("dp", "seq")),
        P(None, ("dp", "seq")),
        P(),
        P(None, "dp", "seq", None),
    )
    out_specs = (
        P(None, "dp", "seq", None),
        P(None, "dp", "seq", None),
        P(("dp", "seq"), None),
        P(("dp", "seq"), None),
        P(("dp", "seq"), None),
        P(("dp", "seq"), None),
        P(("dp", "seq"), None),
        P(("dp", "seq")),
        P(None, ("dp", "seq")),
        P(),
    )
    return jax.shard_map(
        on_device, mesh=mesh, in_specs=in_specs, out_specs=out_specs, check_vma=False
    )
```

```python
import functools
import math

import jax
import jax.numpy as jnp
from jax import lax
from jax.experimental import pallas as pl
from jax.experimental.pallas import tpu as pltpu
from jax.sharding import PartitionSpec as P

H = 12
HD = 64
ROT = 16


epsilon = 1e-05
root_half = 0.7071067811865476
density_scale = 0.3989422804014327
masked_score = -1e30


def normalize(values):
    average = jnp.mean(values, axis=-1, keepdims=True)
    centered = values - average
    inverse = lax.rsqrt(jnp.mean(centered * centered, axis=-1, keepdims=True) + epsilon)
    return (centered * inverse, inverse)


def norm_back(grad_out, normed, inverse, gain_row):
    scaled = grad_out * gain_row
    first_mean = jnp.mean(scaled, axis=-1, keepdims=True)
    second_mean = jnp.mean(scaled * normed, axis=-1, keepdims=True)
    return inverse * (scaled - first_mean - normed * second_mean)


def rotate(values, cosine, sine_part):
    half_rot = ROT // 2
    first_part = values[..., :half_rot]
    second = values[..., half_rot:ROT]
    return jnp.concatenate(
        [
            first_part * cosine - second * sine_part,
            second * cosine + first_part * sine_part,
            values[..., ROT:],
        ],
        axis=-1,
    )


def gelu_slope(hidden):
    return 0.5 * (1.0 + lax.erf(hidden * root_half)) + hidden * density_scale * jnp.exp(
        -0.5 * hidden * hidden
    )


def tree_add(left_tree, right_tree):
    return tuple((left_item + right_item for left_item, right_item in zip(left_tree, right_tree)))


def plain_on_device(inputs, offsets, w_query, w_kv, w_out, w_up, w_down, b_up, vectors, b_kv, cotangent):
    micro_count = inputs.shape[0]
    local_rows = inputs.shape[2]
    model_width = inputs.shape[3]
    seqlen = local_rows * lax.axis_size("seq")
    key_block = math.gcd(seqlen, 512)
    first_row = lax.axis_index("seq") * local_rows
    blocks_used = (first_row + local_rows + key_block - 1) // key_block
    row_ids = first_row + jnp.arange(local_rows, dtype=jnp.int32)
    half_rot = ROT // 2
    frequency = jnp.power(10000.0, -jnp.arange(half_rot, dtype=jnp.float32) * (2.0 / ROT))
    kv_bias = b_kv.astype(jnp.float32)
    results = []
    input_grads = []
    totals = None
    kv_bias_total = jnp.zeros(b_kv.shape, jnp.float32)
    for micro_index in range(micro_count):
        values_in = inputs[micro_index, 0].astype(jnp.float32)
        row_offsets = offsets[micro_index, 0]
        upstream = cotangent[micro_index, 0]
        upstream_f = upstream.astype(jnp.float32)
        angle = (row_offsets.astype(jnp.float32) * 0.25)[:, None] * frequency[None, :]
        cosine = jnp.cos(angle)
        sine_part = jnp.sin(angle)
        gathered = (
            lax.all_gather(w_query, ("dp", "seq"), axis=0, tiled=True),
            lax.all_gather(w_kv, ("dp", "seq"), axis=0, tiled=True),
            lax.all_gather(w_out, ("dp", "seq"), axis=0, tiled=True),
            lax.all_gather(w_up, ("dp", "seq"), axis=0, tiled=True),
            lax.all_gather(w_down, ("dp", "seq"), axis=0, tiled=True),
            lax.all_gather(b_up, ("dp", "seq"), axis=0, tiled=True),
            lax.all_gather(vectors, ("dp", "seq"), axis=1, tiled=True),
        )
        query_full, kv_full, out_full, up_full, down_full, up_bias, vector_full = gathered
        vector_f = vector_full.astype(jnp.float32)
        normed1, inverse1 = normalize(values_in)
        hidden1 = (normed1 * vector_f[0] + vector_f[1]).astype(jnp.bfloat16)
        query_pre = jnp.dot(hidden1, query_full, preferred_element_type=jnp.float32) + vector_f[4]
        kv_pre = jnp.dot(hidden1, kv_full, preferred_element_type=jnp.float32) + kv_bias
        queries = rotate(
            query_pre.reshape(local_rows, H, HD), cosine[:, None, :], sine_part[:, None, :]
        ).astype(jnp.bfloat16)
        shared_local = jnp.concatenate(
            [rotate(kv_pre[:, :HD], cosine, sine_part), kv_pre[:, HD:]], axis=1
        ).astype(jnp.bfloat16)
        shared = lax.all_gather(shared_local, "seq", axis=0, tiled=True)

        def block_scores(number):
            start_row = number * key_block
            key_piece = lax.dynamic_slice_in_dim(shared, start_row, key_block, 0)
            columns = start_row + jnp.arange(key_block, dtype=jnp.int32)
            allowed = (columns[None, :] <= row_ids[:, None]) & (
                row_ids[:, None] - columns[None, :] <= row_offsets[:, None]
            )
            scores = (
                jnp.einsum(
                    "rhd,kd->hrk", queries, key_piece[:, :HD], preferred_element_type=jnp.float32
                )
                * 0.125
            )
            return (jnp.where(allowed[None], scores, masked_score), key_piece)

        def max_step(number, state_pair):
            running_top, denominator = state_pair
            scores, key_piece = block_scores(number)
            new_top = jnp.maximum(running_top, jnp.max(scores, axis=-1))
            denominator = denominator * jnp.exp(running_top - new_top) + jnp.sum(
                jnp.exp(scores - new_top[..., None]), axis=-1
            )
            return (new_top, denominator)

        start_top = jnp.full((H, local_rows), masked_score, jnp.float32)
        running_top, denominator = lax.fori_loop(
            0, blocks_used, max_step, (start_top, jnp.zeros((H, local_rows), jnp.float32))
        )
        log_total = running_top + jnp.log(denominator)

        def value_step(number, accumulated):
            scores, key_piece = block_scores(number)
            soft_weights = jnp.exp(scores - log_total[..., None]).astype(jnp.bfloat16)
            return accumulated + jnp.einsum(
                "hrk,kd->rhd", soft_weights, key_piece[:, HD:], preferred_element_type=jnp.float32
            )

        attended_f = lax.fori_loop(
            0, blocks_used, value_step, jnp.zeros((local_rows, H, HD), jnp.float32)
        )
        attended = attended_f.reshape(local_rows, model_width).astype(jnp.bfloat16)
        attn_out = jnp.dot(attended, out_full, preferred_element_type=jnp.float32) + vector_f[5]
        normed2, inverse2 = normalize(values_in)
        hidden2 = (normed2 * vector_f[2] + vector_f[3]).astype(jnp.bfloat16)
        hidden_up = jnp.dot(hidden2, up_full, preferred_element_type=jnp.float32) + up_bias.astype(
            jnp.float32
        )
        activated = jax.nn.gelu(hidden_up, approximate=False).astype(jnp.bfloat16)
        mlp_out = jnp.dot(activated, down_full, preferred_element_type=jnp.float32) + vector_f[6]
        results.append((values_in + attn_out + mlp_out).astype(jnp.bfloat16))
        regathered = (
            lax.all_gather(w_query, ("dp", "seq"), axis=0, tiled=True),
            lax.all_gather(w_kv, ("dp", "seq"), axis=0, tiled=True),
            lax.all_gather(w_out, ("dp", "seq"), axis=0, tiled=True),
            lax.all_gather(w_up, ("dp", "seq"), axis=0, tiled=True),
            lax.all_gather(w_down, ("dp", "seq"), axis=0, tiled=True),
            lax.all_gather(b_up, ("dp", "seq"), axis=0, tiled=True),
            lax.all_gather(vectors, ("dp", "seq"), axis=1, tiled=True),
        )
        query_back, kv_back, out_back, up_back, down_back, up_bias_back, vector_back = regathered
        vector_back_f = vector_back.astype(jnp.float32)
        grad_w_down = jnp.einsum(
            "rf,rd->fd", activated, upstream, preferred_element_type=jnp.float32
        )
        d_act = jnp.einsum("rd,fd->rf", upstream, down_back, preferred_element_type=jnp.float32)
        d_hidden = (d_act * gelu_slope(hidden_up)).astype(jnp.bfloat16)
        grad_w_up = jnp.einsum("rd,rf->df", hidden2, d_hidden, preferred_element_type=jnp.float32)
        grad_b_up = jnp.sum(d_hidden.astype(jnp.float32), axis=0)
        d_normed2 = jnp.einsum("rf,df->rd", d_hidden, up_back, preferred_element_type=jnp.float32)
        grad_w_out = jnp.einsum("rd,re->de", attended, upstream, preferred_element_type=jnp.float32)
        d_attended = (
            jnp.einsum("re,de->rd", upstream, out_back, preferred_element_type=jnp.float32)
            .astype(jnp.bfloat16)
            .reshape(local_rows, H, HD)
        )

        def delta_step(number, accumulated):
            scores, key_piece = block_scores(number)
            soft_probs = jnp.exp(scores - log_total[..., None])
            d_probs = jnp.einsum(
                "rhd,kd->hrk", d_attended, key_piece[:, HD:], preferred_element_type=jnp.float32
            )
            return accumulated + jnp.sum(soft_probs * d_probs, axis=-1)

        delta = lax.fori_loop(0, blocks_used, delta_step, jnp.zeros((H, local_rows), jnp.float32))

        def grad_step(number, state_pair):
            d_query_rot, d_shared_all = state_pair
            start_row = number * key_block
            scores, key_piece = block_scores(number)
            soft_probs = jnp.exp(scores - log_total[..., None])
            d_probs = jnp.einsum(
                "rhd,kd->hrk", d_attended, key_piece[:, HD:], preferred_element_type=jnp.float32
            )
            d_scores = (soft_probs * (d_probs - delta[..., None])).astype(jnp.bfloat16)
            d_query_rot = (
                d_query_rot
                + jnp.einsum(
                    "hrk,kd->rhd", d_scores, key_piece[:, :HD], preferred_element_type=jnp.float32
                )
                * 0.125
            )
            d_keys = (
                jnp.einsum("hrk,rhd->kd", d_scores, queries, preferred_element_type=jnp.float32)
                * 0.125
            )
            d_values = jnp.einsum(
                "hrk,rhd->kd",
                soft_probs.astype(jnp.bfloat16),
                d_attended,
                preferred_element_type=jnp.float32,
            )
            current = lax.dynamic_slice_in_dim(d_shared_all, start_row, key_block, 0)
            d_shared_all = lax.dynamic_update_slice_in_dim(
                d_shared_all, current + jnp.concatenate([d_keys, d_values], axis=1), start_row, 0
            )
            return (d_query_rot, d_shared_all)

        d_query_rot, d_shared_all = lax.fori_loop(
            0,
            blocks_used,
            grad_step,
            (jnp.zeros((local_rows, H, HD), jnp.float32), jnp.zeros((seqlen, 2 * HD), jnp.float32)),
        )
        d_shared_mine = lax.psum_scatter(
            d_shared_all.astype(jnp.bfloat16), "seq", scatter_dimension=0, tiled=True
        ).astype(jnp.float32)
        d_shared = jnp.concatenate(
            [rotate(d_shared_mine[:, :HD], cosine, -sine_part), d_shared_mine[:, HD:]], axis=1
        ).astype(jnp.bfloat16)
        d_queries = (
            rotate(d_query_rot, cosine[:, None, :], -sine_part[:, None, :])
            .reshape(local_rows, model_width)
            .astype(jnp.bfloat16)
        )
        grad_w_query = jnp.einsum(
            "rd,re->de", hidden1, d_queries, preferred_element_type=jnp.float32
        )
        grad_w_kv = jnp.einsum("rd,rc->dc", hidden1, d_shared, preferred_element_type=jnp.float32)
        kv_bias_total = kv_bias_total + jnp.sum(d_shared.astype(jnp.float32), axis=0)
        d_normed1 = jnp.einsum(
            "re,de->rd", d_queries, query_back, preferred_element_type=jnp.float32
        ) + jnp.einsum("rc,dc->rd", d_shared, kv_back, preferred_element_type=jnp.float32)
        upstream_sum = jnp.sum(upstream_f, axis=0)
        grad_vectors = jnp.stack(
            [
                jnp.sum(d_normed1 * normed1, axis=0),
                jnp.sum(d_normed1, axis=0),
                jnp.sum(d_normed2 * normed2, axis=0),
                jnp.sum(d_normed2, axis=0),
                jnp.sum(d_queries.astype(jnp.float32), axis=0),
                upstream_sum,
                upstream_sum,
            ]
        )
        input_grads.append(
            upstream_f
            + norm_back(d_normed1, normed1, inverse1, vector_back_f[0])
            + norm_back(d_normed2, normed2, inverse2, vector_back_f[2])
        )
        shares = (
            lax.psum_scatter(grad_w_query, ("dp", "seq"), scatter_dimension=0, tiled=True),
            lax.psum_scatter(grad_w_kv, ("dp", "seq"), scatter_dimension=0, tiled=True),
            lax.psum_scatter(grad_w_out, ("dp", "seq"), scatter_dimension=0, tiled=True),
            lax.psum_scatter(grad_w_up, ("dp", "seq"), scatter_dimension=0, tiled=True),
            lax.psum_scatter(grad_w_down, ("dp", "seq"), scatter_dimension=0, tiled=True),
            lax.psum_scatter(grad_b_up, ("dp", "seq"), scatter_dimension=0, tiled=True),
            lax.psum_scatter(grad_vectors, ("dp", "seq"), scatter_dimension=1, tiled=True),
        )
        totals = shares if totals is None else tree_add(totals, shares)
    kv_bias_grad = lax.psum(kv_bias_total, ("dp", "seq"))
    return (
        jnp.stack(results)[:, None],
        jnp.stack(input_grads)[:, None],
        totals[0],
        totals[1],
        totals[2],
        totals[3],
        totals[4],
        totals[5],
        totals[6],
        kv_bias_grad,
    )


MESH = pl.DeviceIdType.MESH
NT = (((1,), (1,)), ((), ()))
VM = pl.BlockSpec(memory_space=pltpu.VMEM)
HBM = pl.BlockSpec(memory_space=pl.ANY)
GROUP = 4
KEYS = 512
MINI = 256
scale_log2 = 0.125 * 1.4426950408889634


def dot(left, right):
    return jnp.dot(left, right, preferred_element_type=jnp.float32)


def dot_nt(left, right):
    return lax.dot_general(left, right, NT, preferred_element_type=jnp.float32)


def bf(values):
    return values.astype(jnp.bfloat16)


def f32(values):
    return values.astype(jnp.float32)


def rotate_rows(block, cosine, sine_part):
    half_rot = ROT // 2
    first, second = block[:half_rot], block[half_rot:ROT]
    return jnp.concatenate(
        [first * cosine - second * sine_part, second * cosine + first * sine_part, block[ROT:]],
        axis=0,
    )


def here():
    return lax.axis_index("dp"), lax.axis_index("seq")


def greet(targets):
    barrier = pltpu.get_barrier_semaphore()
    for target in targets:
        pl.semaphore_signal(barrier, inc=1, device_id=target, device_id_type=MESH)
    pl.semaphore_wait(barrier, len(targets))


def remote(source, target, send, recv, device):
    return pltpu.make_async_remote_copy(
        src_ref=source,
        dst_ref=target,
        send_sem=send,
        recv_sem=recv,
        device_id=device,
        device_id_type=MESH,
    )


class Gather:
    def __init__(self, shard, slabs, halves, send, recv):
        self.shard, self.slabs, self.halves, self.send, self.recv = shard, slabs, halves, send, recv
        self.dp, self.seq = here()
        self.sent = []

    def index(self, dp_flip, z_flip, core_flip=0):
        return (self.dp ^ dp_flip) * 8 + (self.seq ^ (2 * z_flip + core_flip))

    def part(self, slab, half):
        rows, columns = half
        return self.slabs.at[slab, rows, columns]

    def start(self, number, source, target, device):
        remote(source, target, self.send.at[number], self.recv.at[number], device).start()
        self.sent.append(number)

    def arrived(self, number, target):
        remote(target, target, self.send.at[number], self.recv.at[number], (self.dp, self.seq ^ 1)).wait_recv()

    def along_z(self, flip):
        self.start(flip - 1, self.shard, self.slabs.at[self.index(0, 0)], (self.dp, self.seq ^ (2 * flip)))

    def own(self):
        mine = self.slabs.at[self.index(0, 0)]
        self.start(3, self.shard, mine, (self.dp ^ 1, self.seq))
        self.start(7, self.shard, mine, (self.dp ^ 2, self.seq))
        self.start(19, self.shard, mine, (self.dp, self.seq ^ 1))

    def from_z(self, flip):
        piece = self.slabs.at[self.index(0, flip)]
        self.arrived(flip - 1, piece)
        self.start(3 + flip, piece, piece, (self.dp ^ 1, self.seq))
        self.start(7 + flip, piece, piece, (self.dp ^ 2, self.seq))
        if flip == 2:
            self.start(2, piece, piece, (self.dp, self.seq ^ 2))
        self.start(19 + flip, piece, piece, (self.dp, self.seq ^ 1))

    def from_xy(self, flip):
        for axis, half in ((1, 0), (2, 1)):
            number = 3 if axis == 1 else 7
            slab = self.index(axis, flip)
            piece = self.slabs.at[slab]
            self.arrived(number + flip, piece)
            cut = self.part(slab, self.halves[half])
            self.start(11 + 4 * half + flip, cut, cut, (self.dp ^ (3 - axis), self.seq))
            self.start((23 if axis == 1 else 27) + flip, piece, piece, (self.dp, self.seq ^ 1))

    def from_diagonal(self, flip):
        slab = self.index(3, flip)
        for half in (0, 1):
            self.arrived(11 + 4 * half + flip, self.part(slab, self.halves[half]))
        piece = self.slabs.at[slab]
        self.start(31 + flip, piece, piece, (self.dp, self.seq ^ 1))

    def from_core(self):
        for number, dp_flip in ((19, 0), (23, 1), (27, 2), (31, 3)):
            for flip in range(4):
                self.arrived(number + flip, self.slabs.at[self.index(dp_flip, flip, 1)])

    def finish(self):
        for number in self.sent:
            view = self.part(0, self.halves[(number - 11) // 4]) if 11 <= number < 19 else self.slabs.at[0]
            remote(view, view, self.send.at[number], self.recv.at[number], (self.dp, self.seq ^ 1)).wait_send()


def attend(
    micro, steps, row0, off_ref, q_t, do_t, kv_ref, kv_t, att_t, dq_t, dkv, pair, scaled, score_ref, weight_ref, tick
):
    cols = slice(micro * MINI, (micro + 1) * MINI)
    row_ids = row0 + lax.broadcasted_iota(jnp.int32, (1, MINI), 1)
    begin = row_ids - off_ref[micro]

    def group_step(group, carry):
        heads = [pl.ds(pl.multiple_of((group * GROUP + n) * HD, HD), HD) for n in range(GROUP)]
        for n, head in enumerate(heads):
            pair[n, :HD, :MINI] = q_t[head, cols]
            pair[n, HD:, MINI:] = do_t[head, cols]

        def score_step(step, tops):
            keys = pl.ds(pl.multiple_of(step * KEYS, KEYS), KEYS)
            block = kv_ref[micro, keys, :]
            ids = step * KEYS + lax.broadcasted_iota(jnp.int32, (KEYS, 1), 0)
            allowed = (ids <= row_ids) & (ids >= begin)
            found = []
            for n in range(GROUP):
                both = dot(block, pair[n])
                scores = jnp.where(allowed, both[:, :MINI] * scale_log2, masked_score)
                score_ref[n, keys, :MINI] = scores
                score_ref[n, keys, MINI:] = both[:, MINI:]
                found.append(jnp.maximum(tops[n], jnp.max(scores.reshape(KEYS // 8, 8, MINI), axis=0)))
            return tuple(found)

        tops = lax.fori_loop(
            0, steps, score_step, tuple(jnp.full((8, MINI), masked_score, jnp.float32) for _ in heads)
        )
        tops = [jnp.max(top, axis=0, keepdims=True) for top in tops]
        tick(micro, group, 0)

        def value_step(step, carried):
            keys = pl.ds(pl.multiple_of(step * KEYS, KEYS), KEYS)
            values = kv_t[micro, HD:, keys]
            found = []
            for n in range(GROUP):
                output, total = carried[n]
                weights = jnp.exp2(score_ref[n, keys, :MINI] - tops[n])
                total = total + jnp.sum(weights.reshape(KEYS // 8, 8, MINI), axis=0)
                weight_ref[n, keys, :] = bf(weights)
                found.append((output + dot(values, bf(weights)), total))
            return tuple(found)

        sums = lax.fori_loop(
            0,
            steps,
            value_step,
            tuple((jnp.zeros((HD, MINI), jnp.float32), jnp.zeros((8, MINI), jnp.float32)) for _ in heads),
        )
        tick(micro, group, 1)
        inverses, deltas = [], []
        for n, head in enumerate(heads):
            inverse = 1.0 / jnp.sum(sums[n][1], axis=0, keepdims=True)
            output = sums[n][0] * inverse
            upstream = f32(do_t[head, cols])
            deltas.append(jnp.sum(output * upstream, axis=0, keepdims=True))
            inverses.append(inverse)
            att_t[head, cols] = bf(output)
            scaled[n, :HD, :MINI] = bf(f32(q_t[head, cols]) * inverse)
            scaled[n, HD:, MINI:] = bf(upstream * inverse)

        def grad_step(step, carried):
            keys = pl.ds(pl.multiple_of(step * KEYS, KEYS), KEYS)
            key_block = kv_t[micro, :HD, keys]
            total = dkv[micro, keys, :]
            found = []
            for n in range(GROUP):
                weights = weight_ref[n, keys, :]
                d_scores = bf(f32(weights) * (score_ref[n, keys, MINI:] - deltas[n]))
                found.append(carried[n] + dot(key_block, d_scores))
                total = total + dot_nt(d_scores, scaled[n, :, :MINI])
                total = total + dot_nt(weights, scaled[n, :, MINI:])
            dkv[micro, keys, :] = total
            return tuple(found)

        grads = lax.fori_loop(
            0, steps, grad_step, tuple(jnp.zeros((HD, MINI), jnp.float32) for _ in heads)
        )
        for n, head in enumerate(heads):
            dq_t[head, cols] = grads[n] * (inverses[n] * 0.125)
        tick(micro, group, 2)
        return carry

    lax.fori_loop(0, H // GROUP, group_step, 0)


def spread(slabs):
    lane = lax.broadcasted_iota(jnp.int32, (8, 128), 1)
    row = lax.broadcasted_iota(jnp.int32, (8, 128), 0)
    rows = [jnp.zeros((8, 128), jnp.float32) for _ in range(6)]
    wide = [jnp.zeros((8, 128), jnp.float32) for _ in range(24)]
    for number in range(32):
        for width, target, keep in ((24, rows, row < 7), (96, wide, row == 7)):
            block, shift = divmod(number * width, 128)
            piece = jnp.where(keep, slabs[number], 0.0)
            piece = pltpu.roll(piece, shift, 1) if shift else piece
            target[block] = target[block] + jnp.where(lane >= shift, piece, 0.0)
            if shift + width > 128:
                target[block + 1] = target[block + 1] + jnp.where(lane < shift, piece, 0.0)
    return jnp.concatenate(rows, axis=1), jnp.concatenate(wide, axis=1)


def slab_order(store, block, dp_index, rows):
    for z in range(4):
        for core in range(2):
            first = (2 * z + core) * rows
            store(dp_index, core, z, bf(block[first : first + rows]))


def attention_kernel(
    x_ref, cot_ref, off_ref, wq_ref, wkv_in, wout_ref, vec_in, bup_in, bkv_ref, up_ref, down_ref,
    up_slabs, down_slabs, vec_ref, bup_ref, wkv_ref, cos_ref, sin_ref, attn_ref, dn_ref, dkv_out, grads_ref, dqsum_ref,
    small_ref, pair_ref, extra, slabs, pair_slabs, weights, out_weights, n1t_ref, q_t, do_t, att_t, dq_t, kv_ref, kv_t, dkv, pair, scaled,
    score_ref, weight_ref,
    send_a, recv_a, send_o, recv_o, send_u, recv_u, send_d, recv_d, send_kv, recv_kv, local_sem,
):
    dp, seq = here()

    def halves(shape, axis):
        middle = shape[axis] // 2
        cuts = [slice(0, middle), slice(middle, 2 * middle)]
        return tuple((cut, slice(None)) if axis == 0 else (slice(None), cut) for cut in cuts)

    gather_a = Gather(small_ref, slabs, halves(small_ref.shape, 1), send_a, recv_a)
    gather_o = Gather(pair_ref, pair_slabs, halves(pair_ref.shape, 1), send_o, recv_o)
    gather_u = Gather(up_ref, up_slabs, halves(up_ref.shape, 1), send_u, recv_u)
    gather_d = Gather(down_ref, down_slabs, halves(down_ref.shape, 0), send_d, recv_d)

    def signal():
        barrier = pltpu.get_barrier_semaphore()
        for target in friends:
            pl.semaphore_signal(barrier, inc=1, device_id=target, device_id_type=MESH)

    friends = [(dp, seq ^ 1), (dp, seq ^ 2), (dp, seq ^ 4), (dp, seq ^ 6), (dp ^ 1, seq), (dp ^ 2, seq)]
    signal()
    extra[...] = jnp.zeros_like(extra)
    extra[0:7, 0 : vec_in.shape[1]] = f32(vec_in[...])
    extra[7:8, 0 : bup_in.shape[1]] = f32(bup_in[...])
    small_ref[:, 0:128] = wkv_in[...]
    small_ref[:, 128:256] = bf(extra[...])
    pair_ref[:, 0:768] = wq_ref[...]
    pair_ref[:, 768:1536] = wout_ref[...]
    pl.semaphore_wait(pltpu.get_barrier_semaphore(), len(friends))
    for flip in (1, 2):
        gather_a.along_z(flip)
    gather_a.own()
    gather_o.along_z(1)
    gather_o.own()
    gather_u.own()
    mine = gather_a.index(0, 0)
    local_copies = [
        pltpu.make_async_copy(small_ref, slabs.at[mine], local_sem.at[0]),
        pltpu.make_async_copy(pair_ref, pair_slabs.at[mine], local_sem.at[1]),
        pltpu.make_async_copy(up_ref, up_slabs.at[mine], local_sem.at[2]),
        pltpu.make_async_copy(down_ref, down_slabs.at[mine], local_sem.at[3]),
    ]
    for copy in local_copies:
        copy.start()
    pair[...] = jnp.zeros_like(pair)
    scaled[...] = jnp.zeros_like(scaled)
    dkv[...] = jnp.zeros_like(dkv)
    rank = f32(lax.broadcasted_iota(jnp.int32, (ROT // 2, 1), 0))
    frequency = jnp.exp(rank * (-2.0 / ROT * math.log(10000.0)))
    for micro in range(2):
        cols = slice(micro * MINI, (micro + 1) * MINI)
        angle = (f32(off_ref[micro]) * 0.25) * frequency
        cos_ref[:, cols] = jnp.cos(angle)
        sin_ref[:, cols] = jnp.sin(angle)
    normed, _ = normalize(f32(x_ref[...]))
    for flip in (1, 2, 3):
        gather_a.from_z(flip)
    for flip in range(4):
        gather_a.from_xy(flip)
    gather_o.along_z(2)
    gather_o.from_z(1)
    for flip in range(4):
        gather_a.from_diagonal(flip)
    gather_o.from_xy(0)
    gather_u.along_z(1)
    gather_u.along_z(2)
    gather_a.from_core()
    local_copies[0].wait()

    vectors, wide_row = spread([f32(slabs[number, 0:8, 128:256]) for number in range(32)])
    vec_ref[...] = vectors
    bup_ref[...] = wide_row[7:8]

    def unpack(source, target, columns):
        for number in range(16):
            block = jnp.concatenate(
                [f32(source[2 * number, :, columns]), f32(source[2 * number + 1, :, columns])], axis=0
            )
            target[48 * number : 48 * number + 48, :] = bf(block)

    unpack(slabs, wkv_ref, slice(0, 128))
    hidden = bf(normed * vectors[0:1] + vectors[1:2])
    kv_pre = dot(hidden, wkv_ref[...]) + f32(bkv_ref[...])
    kv_pre_t = kv_pre.T
    cosine, sine_part = cos_ref[...], sin_ref[...]
    shared_t = bf(jnp.concatenate([rotate_rows(kv_pre_t[:HD], cosine, sine_part), kv_pre_t[HD:]], axis=0))
    shared = bf(f32(shared_t).T)
    place = pl.ds(pl.multiple_of(seq * MINI, MINI), MINI)
    kv_copies = []
    for micro in range(2):
        kv_ref[micro, place, :] = shared[micro * MINI : (micro + 1) * MINI]

    def kv_block(micro, flip):
        return kv_ref.at[micro, pl.ds(pl.multiple_of((seq ^ flip) * MINI, MINI), MINI)]

    def kv_send(micro, flip, number, device):
        block = kv_block(micro, flip)
        copy = remote(block, block, send_kv.at[micro, number], recv_kv.at[micro, number], device)
        copy.start()
        kv_copies.append(copy)

    def kv_arrived(micro, flip, number):
        block = kv_block(micro, flip)
        remote(block, block, send_kv.at[micro, number], recv_kv.at[micro, number], (dp, seq ^ 1)).wait_recv()

    def kv_start(micro):
        for flip in (1, 2, 3):
            kv_send(micro, 0, flip - 1, (dp, seq ^ (2 * flip)))
        kv_send(micro, 0, 3, (dp, seq ^ 1))

    def kv_forward(micro):
        for flip in (1, 2, 3):
            kv_arrived(micro, 2 * flip, flip - 1)
            kv_send(micro, 2 * flip, 3 + flip, (dp, seq ^ 1))

    def kv_finish(micro):
        for flip in range(4):
            kv_arrived(micro, 2 * flip + 1, 3 + flip)
        kv_t[micro] = bf(f32(kv_ref[micro]).T)

    kv_start(0)
    gather_o.from_z(2)
    gather_o.from_xy(1)
    gather_o.from_diagonal(0)
    gather_o.from_z(3)
    gather_o.from_xy(2)
    gather_o.from_diagonal(1)
    n1t_ref[...] = bf(f32(hidden).T)
    kv_forward(0)
    gather_o.from_xy(3)
    gather_d.along_z(1)
    gather_d.along_z(2)
    gather_d.own()
    gather_u.from_z(1)
    gather_u.from_xy(0)
    gather_o.from_diagonal(2)
    gather_o.from_diagonal(3)
    kv_start(1)
    kv_finish(0)
    local_copies[1].wait()
    gather_o.from_core()
    unpack(pair_slabs, weights, slice(0, 768))
    unpack(pair_slabs, out_weights, slice(768, 1536))
    query = (dot(hidden, weights[...]) + vectors[4:5]).T
    for head in range(H):
        q_t[head * HD : (head + 1) * HD, :] = bf(
            rotate_rows(query[head * HD : (head + 1) * HD], cosine, sine_part)
        )
    do_t[...] = bf(dot_nt(out_weights[...], cot_ref[...]))

    def each(name, *flips):
        def act():
            for gather in (gather_u, gather_d):
                for flip in flips:
                    getattr(gather, name)(flip)

        return act

    def then(*acts):
        def act():
            for one in acts:
                one()

        return act

    actions = [
        lambda: gather_d.from_z(1),
        lambda: gather_d.from_xy(0),
        None,
        then(each("from_z", 2), lambda: gather_u.from_diagonal(0)),
        each("from_xy", 1),
        lambda: gather_d.from_diagonal(0),
        each("from_z", 3),
        each("from_diagonal", 1),
        each("from_xy", 2),
        None,
        each("from_diagonal", 2),
        None,
        each("from_xy", 3),
        None,
        None,
        each("from_diagonal", 3),
        None,
        None,
    ]

    def tick(micro, group, part):
        for number in range(H // GROUP):
            act = actions[(micro * (H // GROUP) + number) * 3 + part]
            if act is not None:
                pl.when(group == number)(act)

    kv_forward(1)
    steps = lax.div((seq + 1) * MINI + KEYS - 1, KEYS)
    for micro in range(2):
        if micro == 1:
            kv_finish(1)
        attend(
            micro, steps, seq * MINI, off_ref, q_t, do_t, kv_ref, kv_t, att_t, dq_t, dkv,
            pair, scaled, score_ref, weight_ref, tick,
        )
    for micro in range(2):
        for core in range(2):
            for z in range(4):
                first = (2 * z + core) * MINI
                block = dkv[micro, first : first + MINI, :]
                scale = jnp.where(lax.broadcasted_iota(jnp.int32, (1, 2 * HD), 1) < HD, 0.125, 1.0)
                dkv_out[core, z, micro] = bf(block * scale)
    attn_ref[...] = dot(bf(f32(att_t[...]).T), out_weights[...]) + vectors[5:6]
    for head in range(H):
        dq_t[head * HD : (head + 1) * HD, :] = rotate_rows(
            dq_t[head * HD : (head + 1) * HD, :], cosine, -sine_part
        )
    d_query = bf(dq_t[...].T)
    dqsum_ref[...] = jnp.sum(f32(d_query), axis=0, keepdims=True)
    dn_ref[...] = dot_nt(d_query, weights[...])
    for block in range(4):
        rows = slice(192 * block, 192 * block + 192)

        def put_query(dp_index, core, z, piece):
            grads_ref[dp_index, core, z, :, 0:768] = piece

        def put_out(dp_index, core, z, piece):
            grads_ref[dp_index, core, z, :, 768:1536] = piece

        slab_order(put_query, dot(n1t_ref[rows, :], d_query), block, 24)
        slab_order(put_out, dot(att_t[rows, :], cot_ref[...]), block, 24)
    for gather in (gather_u, gather_d):
        gather.from_core()
    for gather in (gather_a, gather_o, gather_u, gather_d):
        gather.finish()
    for copy in kv_copies:
        copy.wait_send()
    for copy in local_copies[2:]:
        copy.wait()


def attention_call(x, cot, offsets, w_query, w_kv, w_out, vectors, b_up, b_kv, w_up, w_down):
    rows = x.shape[0]
    dma = pltpu.SemaphoreType.DMA
    out = jax.ShapeDtypeStruct
    seqlen = 8 * MINI
    b16 = jnp.bfloat16
    return pl.pallas_call(
        attention_kernel,
        out_shape=(
            out((32,) + w_up.shape, b16),
            out((32,) + w_down.shape, b16),
            out((8, 768), jnp.float32),
            out((1, 3072), jnp.float32),
            out((768, 128), b16),
            out((ROT // 2, rows), jnp.float32),
            out((ROT // 2, rows), jnp.float32),
            out((rows, 768), jnp.float32),
            out((rows, 768), jnp.float32),
            out((2, 4, 2, MINI, 2 * HD), b16),
            out((4, 2, 4, 24, 1536), b16),
            out((1, 768), jnp.float32),
        ),
        in_specs=[VM] * 9 + [HBM] * 2,
        out_specs=(HBM, HBM) + (VM,) * 10,
        scratch_shapes=[
            pltpu.VMEM((24, 256), b16),
            pltpu.VMEM((24, 1536), b16),
            pltpu.VMEM((24, 128), jnp.float32),
            pltpu.VMEM((32, 24, 256), b16),
            pltpu.VMEM((32, 24, 1536), b16),
            pltpu.VMEM((768, 768), b16),
            pltpu.VMEM((768, 768), b16),
            pltpu.VMEM((768, rows), b16),
            pltpu.VMEM((768, rows), b16),
            pltpu.VMEM((768, rows), b16),
            pltpu.VMEM((768, rows), b16),
            pltpu.VMEM((768, rows), jnp.float32),
            pltpu.VMEM((2, seqlen, 2 * HD), b16),
            pltpu.VMEM((2, 2 * HD, seqlen), b16),
            pltpu.VMEM((2, seqlen, 2 * HD), jnp.float32),
            pltpu.VMEM((GROUP, 2 * HD, 2 * MINI), b16),
            pltpu.VMEM((GROUP, 2 * HD, 2 * MINI), b16),
            pltpu.VMEM((GROUP, seqlen, 2 * MINI), jnp.float32),
            pltpu.VMEM((GROUP, seqlen, MINI), b16),
        ]
        + [dma((35,))] * 8
        + [dma((2, 7))] * 2
        + [dma((4,))],
        compiler_params=pltpu.CompilerParams(
            collective_id=0, has_side_effects=True, vmem_limit_bytes=60 << 20
        ),
        name="attention",
    )(x, cot, offsets, w_query, w_kv, w_out, vectors, b_up, b_kv, w_up, w_down)


def packed_on_device(inputs, offsets, w_query, w_kv, w_out, w_up, w_down, b_up, vectors, b_kv, cotangent):
    rows = 2 * MINI
    x = inputs.reshape(rows, 768)
    cot = cotangent.reshape(rows, 768)
    up_slabs, down_slabs, vec, bup, wkv, cosine, sine_part, attn, dn1, dkv, grads_a, dq_sum = attention_call(
        x, cot, offsets, w_query, w_kv, w_out, vectors, b_up.reshape(1, -1), b_kv.reshape(1, -1), w_up, w_down
    )
    return feed_forward(x, cot, cosine, sine_part, up_slabs, down_slabs, vec, bup, wkv, attn, dn1, dkv, grads_a, dq_sum)


class Scatter:
    def __init__(self, slabs, from_core, from_diagonal, from_xy, from_z, send, recv):
        self.slabs, self.from_core, self.from_diagonal = slabs, from_core, from_diagonal
        self.from_xy, self.from_z, self.send, self.recv = from_xy, from_z, send, recv
        self.dp, self.seq = here()
        self.core = lax.rem(self.seq, 2)
        self.z = lax.div(self.seq, 2)
        self.sent = []

    def start(self, number, source, target, device):
        copy = remote(source, target, self.send.at[number], self.recv.at[number], device)
        copy.start()
        self.sent.append(copy)

    def arrived(self, number, target):
        remote(target, target, self.send.at[number], self.recv.at[number], (self.dp, self.seq ^ 1)).wait_recv()

    def block(self, flip):
        return self.slabs.at[self.dp ^ flip, self.core]

    def to_core(self, flip):
        other = self.slabs.at[self.dp ^ flip, 1 - self.core]
        self.start(flip, other, self.from_core.at[flip], (self.dp, self.seq ^ 1))

    def add(self, block, z, terms):
        total = f32(block[z])
        for term in terms:
            total = total + f32(term)
        block[z] = bf(total)

    def diagonal(self):
        block = self.block(3)
        self.arrived(3, self.from_core.at[3])
        for half in (0, 1):
            for z in (2 * half, 2 * half + 1):
                self.add(block, z, [self.from_core[3, z]])
            self.start(4 + half, block.at[pl.ds(2 * half, 2)], self.from_diagonal.at[half], (self.dp ^ (1 + half), self.seq))

    def beside(self, axis):
        half = 2 - axis
        block = self.block(axis)
        self.arrived(axis, self.from_core.at[axis])
        self.arrived(4 + half, self.from_diagonal.at[half])
        for z in range(4):
            terms = [self.from_core[axis, z]]
            if z // 2 == half:
                terms.append(self.from_diagonal[half, z % 2])
            self.add(block, z, terms)
        self.start(5 + axis, block, self.from_xy.at[axis - 1], (self.dp ^ axis, self.seq))

    def own(self):
        block = self.block(0)
        self.arrived(0, self.from_core.at[0])
        for axis in (1, 2):
            self.arrived(5 + axis, self.from_xy.at[axis - 1])
        for z in range(4):
            self.add(block, z, [self.from_core[0, z], self.from_xy[0, z], self.from_xy[1, z]])
        for flip in (1, 2, 3):
            self.start(7 + flip, block.at[self.z ^ flip], self.from_z.at[flip - 1], (self.dp, self.seq ^ (2 * flip)))

    def total(self):
        value = f32(self.slabs[self.dp, self.core, self.z])
        for flip in (1, 2, 3):
            self.arrived(7 + flip, self.from_z.at[flip - 1])
            value = value + f32(self.from_z[flip - 1])
        return value

    def finish(self):
        for copy in self.sent:
            copy.wait_send()


def feed_kernel(
    x_ref, cot_ref, cos_ref, sin_ref, vec_ref, bup_ref, wkv_ref, attn_ref, dn_ref, dqsum_ref, dkv_in, grads_a, up_hbm, down_hbm,
    out_ref, gin_ref, gq_ref, go_ref, gu_ref, gkv_ref, gd_ref, small_out,
    up_ref, down_ref, n1t_ref, n2_ref, n2t_ref, act_ref, dh_ref, mlp_ref, dshared_ref, stats,
    a_slabs, d_slabs, u_slabs, v_slabs,
    a_core, a_diag, a_xy, a_z, d_core, d_diag, d_xy, d_z, u_core, u_diag, u_xy, u_z, v_core, v_diag, v_xy, v_z,
    dkv, dkv_core, dkv_z, small, small_in,
    send_s, recv_s, send_k, recv_k, send_m, recv_m, load_sem,
):
    dp, seq = here()
    core, z = lax.rem(seq, 2), lax.div(seq, 2)
    loads = [
        pltpu.make_async_copy(dkv_in, dkv, load_sem.at[2]),
        pltpu.make_async_copy(grads_a, a_slabs, load_sem.at[3]),
        pltpu.make_async_copy(up_hbm, up_ref, load_sem.at[0]),
        pltpu.make_async_copy(down_hbm, down_ref, load_sem.at[1]),
    ]
    for copy in loads:
        copy.start()
    greet(
        [(dp, seq ^ 1), (dp, seq ^ 2), (dp, seq ^ 4), (dp, seq ^ 6), (dp ^ 1, seq), (dp ^ 2, seq)]
    )
    scatter_a = Scatter(a_slabs, a_core, a_diag, a_xy, a_z, send_s.at[0], recv_s.at[0])
    scatter_d = Scatter(d_slabs, d_core, d_diag, d_xy, d_z, send_s.at[1], recv_s.at[1])
    scatter_u = Scatter(u_slabs, u_core, u_diag, u_xy, u_z, send_s.at[2], recv_s.at[2])
    scatter_v = Scatter(v_slabs, v_core, v_diag, v_xy, v_z, send_s.at[3], recv_s.at[3])
    kv_sent = []

    def kv_start(number, source, target, device):
        copy = remote(source, target, send_k.at[number], recv_k.at[number], device)
        copy.start()
        kv_sent.append(copy)

    def kv_arrived(number, target):
        remote(target, target, send_k.at[number], recv_k.at[number], (dp, seq ^ 1)).wait_recv()

    loads[1].wait()
    for flip in (3, 1, 2, 0):
        scatter_a.to_core(flip)
    loads[0].wait()
    kv_start(0, dkv.at[1 - core], dkv_core, (dp, seq ^ 1))
    scatter_a.diagonal()

    vectors = vec_ref[...]
    for start in range(0, 2 * MINI, MINI):
        rows = slice(start, start + MINI)
        normed, inverse = normalize(f32(x_ref[rows, :]))
        stats[rows, :] = jnp.broadcast_to(inverse, (MINI, 128))
        n1t_ref[:, rows] = bf((normed * vectors[0:1] + vectors[1:2]).T)
        second = normed * vectors[2:3] + vectors[3:4]
        n2_ref[rows, :] = bf(second)
        n2t_ref[:, rows] = bf(second.T)
    kv_arrived(0, dkv_core)
    for index in range(4):
        for micro in range(2):
            dkv[core, index, micro] = bf(f32(dkv[core, index, micro]) + f32(dkv_core[index, micro]))
    for flip in (1, 2, 3):
        kv_start(flip, dkv.at[core, z ^ flip], dkv_z.at[flip - 1], (dp, seq ^ (2 * flip)))
    scatter_a.beside(1)
    scatter_a.beside(2)
    loads[2].wait()
    loads[3].wait()

    def chunk(flip, first):
        base = (dp ^ flip) * 768

        def tile(number, carry):
            columns = pl.ds(pl.multiple_of(base + number * 256, 256), 256)
            hidden = dot(n2_ref[...], up_ref[:, columns]) + bup_ref[0:1, columns]
            d_act = dot_nt(cot_ref[...], down_ref[columns, :])
            normal = 0.5 + 0.5 * lax.erf(hidden * root_half)
            density = density_scale * jnp.exp(-0.5 * hidden * hidden)
            d_hidden = bf(d_act * (normal + hidden * density))
            act_ref[:, pl.ds(pl.multiple_of(number * 256, 256), 256)] = bf(hidden * normal)
            dh_ref[:, columns] = d_hidden
            return carry

        lax.fori_loop(0, 3, tile, 0)
        down_rows = pl.ds(pl.multiple_of(base, 768), 768)
        part = dot(act_ref[...], down_ref[down_rows, :])
        mlp_ref[...] = part if first else mlp_ref[...] + part

        grad_t = bf(f32(act_ref[...]).T)
        for number in range(4):
            grad = dot(grad_t[192 * number : 192 * number + 192], cot_ref[...])
            for half in range(2):
                d_slabs[dp ^ flip, half, number] = bf(grad[96 * half : 96 * half + 96])
        scatter_d.to_core(flip)

    def put(store, block, flip, rows):
        for index in range(4):
            for half in range(2):
                first = (2 * index + half) * rows
                store(dp ^ flip, half, index, bf(block[first : first + rows]))

    def up_block(flip, left):
        rows = pl.ds(pl.multiple_of((dp ^ flip) * 192, 192), 192)
        if left:

            def put_left(target, half, index, piece):
                u_slabs[target, half, index, :, 0:1536] = piece

            def put_kv(target, half, index, piece):
                u_slabs[target, half, index, :, 1536:1664] = piece

            put(put_left, dot(n2t_ref[rows, :], dh_ref[:, 0:1536]), flip, 24)
            put(put_kv, dot(n1t_ref[rows, :], dshared_ref[...]), flip, 24)
            scatter_u.to_core(flip)
        else:

            def put_right(target, half, index, piece):
                v_slabs[target, half, index] = piece

            put(put_right, dot(n2t_ref[rows, :], dh_ref[:, 1536:3072]), flip, 24)
            scatter_v.to_core(flip)

    chunk(3, True)
    scatter_d.diagonal()
    chunk(1, False)
    scatter_a.own()
    scatter_d.beside(1)
    for flip in (1, 2, 3):
        kv_arrived(flip, dkv_z.at[flip - 1])
    cosine, sine_part = cos_ref[...], sin_ref[...]
    for micro in range(2):
        cols = slice(micro * MINI, (micro + 1) * MINI)
        total = f32(dkv[core, z, micro])
        for flip in (1, 2, 3):
            total = total + f32(dkv_z[flip - 1, micro])
        total_t = total.T
        total_t = jnp.concatenate(
            [rotate_rows(total_t[:HD], cosine[:, cols], -sine_part[:, cols]), total_t[HD:]], axis=0
        )
        dshared_ref[cols, :] = bf(total_t.T)
    chunk(2, False)
    scatter_d.beside(2)
    chunk(0, False)
    up_block(3, True)
    up_block(1, True)
    scatter_u.diagonal()
    up_block(2, True)
    up_block(0, True)
    scatter_d.own()
    up_block(3, False)
    up_block(1, False)
    scatter_u.beside(1)
    scatter_u.beside(2)
    scatter_v.diagonal()
    up_block(2, False)
    up_block(0, False)
    zero = jnp.zeros((1, 768), jnp.float32)
    sums = [zero] * 5
    for start in range(0, 2 * MINI, 128):
        rows = slice(start, start + 128)
        values = f32(x_ref[rows, :])
        upstream = f32(cot_ref[rows, :])
        inverse = stats[rows, 0:1]
        normed = (values - jnp.mean(values, axis=-1, keepdims=True)) * inverse
        out_ref[rows, :] = bf(values + attn_ref[rows, :] + mlp_ref[rows, :] + vectors[6:7])
        first = dn_ref[rows, :] + dot_nt(dshared_ref[rows, :], wkv_ref[...])
        second = dot_nt(dh_ref[rows, :], up_ref[...])
        gin_ref[rows, :] = (
            upstream
            + norm_back(first, normed, inverse, vectors[0:1])
            + norm_back(second, normed, inverse, vectors[2:3])
        )
        news = (first * normed, first, second * normed, second, upstream)
        sums = [total + jnp.sum(new, axis=0, keepdims=True) for total, new in zip(sums, news)]
    b_up_sum = jnp.sum(f32(dh_ref[...]), axis=0, keepdims=True)
    kv_sum = jnp.sum(f32(dshared_ref[...]), axis=0, keepdims=True)
    small[0] = jnp.concatenate(
        sums[:4]
        + [dqsum_ref[...], sums[4], sums[4], zero]
        + [b_up_sum[:, 768 * n : 768 * n + 768] for n in range(4)]
        + [jnp.concatenate([kv_sum, zero[:, 128:]], axis=1)]
        + [zero] * 3,
        axis=0,
    )
    partners = [(dp, seq ^ 1), (dp, seq ^ 2), (dp, seq ^ 4), (dp ^ 1, seq), (dp ^ 2, seq)]
    small_sent = []

    def small_start(number):
        copy = remote(small.at[number], small_in.at[number], send_m.at[number], recv_m.at[number], partners[number])
        copy.start()
        small_sent.append(copy)

    def small_end(number):
        small_sent[number].wait_recv()
        small[number + 1] = small[number] + small_in[number]

    total = scatter_a.total()
    gq_ref[...] = total[:, :768]
    go_ref[...] = total[:, 768:]
    small_start(0)
    scatter_v.beside(1)
    scatter_v.beside(2)
    small_end(0)
    small_start(1)
    scatter_u.own()
    small_end(1)
    small_start(2)
    gd_ref[...] = scatter_d.total()
    scatter_v.own()
    small_end(2)
    small_start(3)
    total = scatter_u.total()
    gu_ref[:, 0:1536] = total[:, 0:1536]
    gkv_ref[...] = total[:, 1536:1664]
    small_end(3)
    small_start(4)
    small_end(4)
    small_out[...] = small[5]
    gu_ref[:, 1536:3072] = scatter_v.total()
    for scatter in (scatter_a, scatter_d, scatter_u, scatter_v):
        scatter.finish()
    for copy in kv_sent + small_sent:
        copy.wait_send()


def place_kernel(small, *refs):
    wholes, results = refs[:7], refs[7:17]
    for source, target in zip(wholes, results):
        target[...] = source[...]
    dp, seq = here()
    rows = small[0:8, :]
    shift = lax.rem(768 - 24 * (8 * dp + seq), 768)
    results[7][...] = pltpu.roll(rows, shift, 1)[0:7, 0:24]
    wide = jnp.broadcast_to(small[pl.ds(8 + dp, 1), :], (8, 768))
    shift = lax.rem(768 - 96 * seq, 768)
    results[8][...] = pltpu.roll(wide, shift, 1)[0:1, 0:96]
    results[9][...] = small[12:13, 0 : 2 * HD]


def feed_forward(x, cot, cosine, sine_part, up_slabs, down_slabs, vec, bup, wkv, attn, dn1, dkv, grads_a, dq_sum):
    rows = x.shape[0]
    dma = pltpu.SemaphoreType.DMA
    out = jax.ShapeDtypeStruct
    b16 = jnp.bfloat16
    shapes = ((24, 1536), (96, 768), (24, 1664), (24, 1536))
    buffers = [pltpu.VMEM((4, 2, 4) + shape, b16) for shape in shapes]
    for shape in shapes:
        for lead in ((4, 4), (2, 2), (2, 4), (3,)):
            buffers.append(pltpu.VMEM(lead + shape, b16))
    out_rows, g_in, g_query, g_out, g_up, g_kv, g_down, small = pl.pallas_call(
        feed_kernel,
        out_shape=(
            out((rows, 768), b16),
            out((rows, 768), jnp.float32),
            out((24, 768), jnp.float32),
            out((24, 768), jnp.float32),
            out((24, 3072), jnp.float32),
            out((24, 128), jnp.float32),
            out((96, 768), jnp.float32),
            out((16, 768), jnp.float32),
        ),
        in_specs=[VM] * 10 + [HBM] * 4,
        out_specs=(VM,) * 8,
        scratch_shapes=[
            pltpu.VMEM((768, 3072), b16),
            pltpu.VMEM((3072, 768), b16),
            pltpu.VMEM((768, rows), b16),
            pltpu.VMEM((rows, 768), b16),
            pltpu.VMEM((768, rows), b16),
            pltpu.VMEM((rows, 768), b16),
            pltpu.VMEM((rows, 3072), b16),
            pltpu.VMEM((rows, 768), jnp.float32),
            pltpu.VMEM((rows, 2 * HD), b16),
            pltpu.VMEM((rows, 128), jnp.float32),
        ]
        + buffers
        + [
            pltpu.VMEM((2, 4, 2, MINI, 2 * HD), b16),
            pltpu.VMEM((4, 2, MINI, 2 * HD), b16),
            pltpu.VMEM((3, 2, MINI, 2 * HD), b16),
            pltpu.VMEM((6, 16, 768), jnp.float32),
            pltpu.VMEM((5, 16, 768), jnp.float32),
            dma((4, 11)),
            dma((4, 11)),
            dma((4,)),
            dma((4,)),
            dma((5,)),
            dma((5,)),
            dma((4,)),
        ],
        compiler_params=pltpu.CompilerParams(
            collective_id=1, has_side_effects=True, vmem_limit_bytes=63 << 20
        ),
        name="feed_forward",
    )(
        x, cot, cosine, sine_part, vec, bup, wkv, attn, dn1, dq_sum, dkv, grads_a,
        up_slabs.reshape(768, 3072), down_slabs.reshape(3072, 768),
    )
    wholes = (out_rows, g_in, g_query, g_kv, g_out, g_up, g_down)
    like = tuple(out(one.shape, one.dtype) for one in wholes)
    results = pl.pallas_call(
        place_kernel,
        out_shape=like + (out((7, 24), jnp.float32), out((1, 96), jnp.float32), out((1, 2 * HD), jnp.float32)),
        in_specs=[VM] * (1 + len(wholes)),
        out_specs=(VM,) * (3 + len(wholes)),
        compiler_params=pltpu.CompilerParams(vmem_limit_bytes=62 << 20),
        name="place",
    )(small, *wholes)
    out_rows, g_in, g_query, g_kv, g_out, g_up, g_down, g_vectors, g_b_up, g_b_kv = results
    return (
        out_rows.reshape(2, 1, MINI, 768), g_in.reshape(2, 1, MINI, 768), g_query, g_kv, g_out,
        g_up, g_down, g_b_up.reshape(-1), g_vectors, g_b_kv.reshape(-1),
    )


def solution(mesh):
    packed = mesh.shape["dp"] == 4 and mesh.shape["seq"] == 8
    on_device = packed_on_device if packed else plain_on_device

    in_specs = (
        P(None, "dp", "seq", None),
        P(None, "dp", "seq"),
        P(("dp", "seq"), None),
        P(("dp", "seq"), None),
        P(("dp", "seq"), None),
        P(("dp", "seq"), None),
        P(("dp", "seq"), None),
        P(("dp", "seq")),
        P(None, ("dp", "seq")),
        P(),
        P(None, "dp", "seq", None),
    )
    out_specs = (
        P(None, "dp", "seq", None),
        P(None, "dp", "seq", None),
        P(("dp", "seq"), None),
        P(("dp", "seq"), None),
        P(("dp", "seq"), None),
        P(("dp", "seq"), None),
        P(("dp", "seq"), None),
        P(("dp", "seq")),
        P(None, ("dp", "seq")),
        P(),
    )
    return jax.shard_map(
        on_device, mesh=mesh, in_specs=in_specs, out_specs=out_specs, check_vma=False
    )
```

```python
import functools
import math

import jax
import jax.numpy as jnp
from jax import lax
from jax.experimental import pallas as pl
from jax.experimental.pallas import tpu as pltpu
from jax.sharding import PartitionSpec as P

H = 12
HD = 64
ROT = 16


epsilon = 1e-05
root_half = 0.7071067811865476
density_scale = 0.3989422804014327
masked_score = -1e30


def normalize(values):
    average = jnp.mean(values, axis=-1, keepdims=True)
    centered = values - average
    inverse = lax.rsqrt(jnp.mean(centered * centered, axis=-1, keepdims=True) + epsilon)
    return (centered * inverse, inverse)


def norm_back(grad_out, normed, inverse, gain_row):
    scaled = grad_out * gain_row
    first_mean = jnp.mean(scaled, axis=-1, keepdims=True)
    second_mean = jnp.mean(scaled * normed, axis=-1, keepdims=True)
    return inverse * (scaled - first_mean - normed * second_mean)


def rotate(values, cosine, sine_part):
    half_rot = ROT // 2
    first_part = values[..., :half_rot]
    second = values[..., half_rot:ROT]
    return jnp.concatenate(
        [
            first_part * cosine - second * sine_part,
            second * cosine + first_part * sine_part,
            values[..., ROT:],
        ],
        axis=-1,
    )


def gelu_slope(hidden):
    return 0.5 * (1.0 + lax.erf(hidden * root_half)) + hidden * density_scale * jnp.exp(
        -0.5 * hidden * hidden
    )


def tree_add(left_tree, right_tree):
    return tuple((left_item + right_item for left_item, right_item in zip(left_tree, right_tree)))


def plain_on_device(inputs, offsets, w_query, w_kv, w_out, w_up, w_down, b_up, vectors, b_kv, cotangent):
    micro_count = inputs.shape[0]
    local_rows = inputs.shape[2]
    model_width = inputs.shape[3]
    seqlen = local_rows * lax.axis_size("seq")
    key_block = math.gcd(seqlen, 512)
    first_row = lax.axis_index("seq") * local_rows
    blocks_used = (first_row + local_rows + key_block - 1) // key_block
    row_ids = first_row + jnp.arange(local_rows, dtype=jnp.int32)
    half_rot = ROT // 2
    frequency = jnp.power(10000.0, -jnp.arange(half_rot, dtype=jnp.float32) * (2.0 / ROT))
    kv_bias = b_kv.astype(jnp.float32)
    results = []
    input_grads = []
    totals = None
    kv_bias_total = jnp.zeros(b_kv.shape, jnp.float32)
    for micro_index in range(micro_count):
        values_in = inputs[micro_index, 0].astype(jnp.float32)
        row_offsets = offsets[micro_index, 0]
        upstream = cotangent[micro_index, 0]
        upstream_f = upstream.astype(jnp.float32)
        angle = (row_offsets.astype(jnp.float32) * 0.25)[:, None] * frequency[None, :]
        cosine = jnp.cos(angle)
        sine_part = jnp.sin(angle)
        gathered = (
            lax.all_gather(w_query, ("dp", "seq"), axis=0, tiled=True),
            lax.all_gather(w_kv, ("dp", "seq"), axis=0, tiled=True),
            lax.all_gather(w_out, ("dp", "seq"), axis=0, tiled=True),
            lax.all_gather(w_up, ("dp", "seq"), axis=0, tiled=True),
            lax.all_gather(w_down, ("dp", "seq"), axis=0, tiled=True),
            lax.all_gather(b_up, ("dp", "seq"), axis=0, tiled=True),
            lax.all_gather(vectors, ("dp", "seq"), axis=1, tiled=True),
        )
        query_full, kv_full, out_full, up_full, down_full, up_bias, vector_full = gathered
        vector_f = vector_full.astype(jnp.float32)
        normed1, inverse1 = normalize(values_in)
        hidden1 = (normed1 * vector_f[0] + vector_f[1]).astype(jnp.bfloat16)
        query_pre = jnp.dot(hidden1, query_full, preferred_element_type=jnp.float32) + vector_f[4]
        kv_pre = jnp.dot(hidden1, kv_full, preferred_element_type=jnp.float32) + kv_bias
        queries = rotate(
            query_pre.reshape(local_rows, H, HD), cosine[:, None, :], sine_part[:, None, :]
        ).astype(jnp.bfloat16)
        shared_local = jnp.concatenate(
            [rotate(kv_pre[:, :HD], cosine, sine_part), kv_pre[:, HD:]], axis=1
        ).astype(jnp.bfloat16)
        shared = lax.all_gather(shared_local, "seq", axis=0, tiled=True)

        def block_scores(number):
            start_row = number * key_block
            key_piece = lax.dynamic_slice_in_dim(shared, start_row, key_block, 0)
            columns = start_row + jnp.arange(key_block, dtype=jnp.int32)
            allowed = (columns[None, :] <= row_ids[:, None]) & (
                row_ids[:, None] - columns[None, :] <= row_offsets[:, None]
            )
            scores = (
                jnp.einsum(
                    "rhd,kd->hrk", queries, key_piece[:, :HD], preferred_element_type=jnp.float32
                )
                * 0.125
            )
            return (jnp.where(allowed[None], scores, masked_score), key_piece)

        def max_step(number, state_pair):
            running_top, denominator = state_pair
            scores, key_piece = block_scores(number)
            new_top = jnp.maximum(running_top, jnp.max(scores, axis=-1))
            denominator = denominator * jnp.exp(running_top - new_top) + jnp.sum(
                jnp.exp(scores - new_top[..., None]), axis=-1
            )
            return (new_top, denominator)

        start_top = jnp.full((H, local_rows), masked_score, jnp.float32)
        running_top, denominator = lax.fori_loop(
            0, blocks_used, max_step, (start_top, jnp.zeros((H, local_rows), jnp.float32))
        )
        log_total = running_top + jnp.log(denominator)

        def value_step(number, accumulated):
            scores, key_piece = block_scores(number)
            soft_weights = jnp.exp(scores - log_total[..., None]).astype(jnp.bfloat16)
            return accumulated + jnp.einsum(
                "hrk,kd->rhd", soft_weights, key_piece[:, HD:], preferred_element_type=jnp.float32
            )

        attended_f = lax.fori_loop(
            0, blocks_used, value_step, jnp.zeros((local_rows, H, HD), jnp.float32)
        )
        attended = attended_f.reshape(local_rows, model_width).astype(jnp.bfloat16)
        attn_out = jnp.dot(attended, out_full, preferred_element_type=jnp.float32) + vector_f[5]
        normed2, inverse2 = normalize(values_in)
        hidden2 = (normed2 * vector_f[2] + vector_f[3]).astype(jnp.bfloat16)
        hidden_up = jnp.dot(hidden2, up_full, preferred_element_type=jnp.float32) + up_bias.astype(
            jnp.float32
        )
        activated = jax.nn.gelu(hidden_up, approximate=False).astype(jnp.bfloat16)
        mlp_out = jnp.dot(activated, down_full, preferred_element_type=jnp.float32) + vector_f[6]
        results.append((values_in + attn_out + mlp_out).astype(jnp.bfloat16))
        regathered = (
            lax.all_gather(w_query, ("dp", "seq"), axis=0, tiled=True),
            lax.all_gather(w_kv, ("dp", "seq"), axis=0, tiled=True),
            lax.all_gather(w_out, ("dp", "seq"), axis=0, tiled=True),
            lax.all_gather(w_up, ("dp", "seq"), axis=0, tiled=True),
            lax.all_gather(w_down, ("dp", "seq"), axis=0, tiled=True),
            lax.all_gather(b_up, ("dp", "seq"), axis=0, tiled=True),
            lax.all_gather(vectors, ("dp", "seq"), axis=1, tiled=True),
        )
        query_back, kv_back, out_back, up_back, down_back, up_bias_back, vector_back = regathered
        vector_back_f = vector_back.astype(jnp.float32)
        grad_w_down = jnp.einsum(
            "rf,rd->fd", activated, upstream, preferred_element_type=jnp.float32
        )
        d_act = jnp.einsum("rd,fd->rf", upstream, down_back, preferred_element_type=jnp.float32)
        d_hidden = (d_act * gelu_slope(hidden_up)).astype(jnp.bfloat16)
        grad_w_up = jnp.einsum("rd,rf->df", hidden2, d_hidden, preferred_element_type=jnp.float32)
        grad_b_up = jnp.sum(d_hidden.astype(jnp.float32), axis=0)
        d_normed2 = jnp.einsum("rf,df->rd", d_hidden, up_back, preferred_element_type=jnp.float32)
        grad_w_out = jnp.einsum("rd,re->de", attended, upstream, preferred_element_type=jnp.float32)
        d_attended = (
            jnp.einsum("re,de->rd", upstream, out_back, preferred_element_type=jnp.float32)
            .astype(jnp.bfloat16)
            .reshape(local_rows, H, HD)
        )

        def delta_step(number, accumulated):
            scores, key_piece = block_scores(number)
            soft_probs = jnp.exp(scores - log_total[..., None])
            d_probs = jnp.einsum(
                "rhd,kd->hrk", d_attended, key_piece[:, HD:], preferred_element_type=jnp.float32
            )
            return accumulated + jnp.sum(soft_probs * d_probs, axis=-1)

        delta = lax.fori_loop(0, blocks_used, delta_step, jnp.zeros((H, local_rows), jnp.float32))

        def grad_step(number, state_pair):
            d_query_rot, d_shared_all = state_pair
            start_row = number * key_block
            scores, key_piece = block_scores(number)
            soft_probs = jnp.exp(scores - log_total[..., None])
            d_probs = jnp.einsum(
                "rhd,kd->hrk", d_attended, key_piece[:, HD:], preferred_element_type=jnp.float32
            )
            d_scores = (soft_probs * (d_probs - delta[..., None])).astype(jnp.bfloat16)
            d_query_rot = (
                d_query_rot
                + jnp.einsum(
                    "hrk,kd->rhd", d_scores, key_piece[:, :HD], preferred_element_type=jnp.float32
                )
                * 0.125
            )
            d_keys = (
                jnp.einsum("hrk,rhd->kd", d_scores, queries, preferred_element_type=jnp.float32)
                * 0.125
            )
            d_values = jnp.einsum(
                "hrk,rhd->kd",
                soft_probs.astype(jnp.bfloat16),
                d_attended,
                preferred_element_type=jnp.float32,
            )
            current = lax.dynamic_slice_in_dim(d_shared_all, start_row, key_block, 0)
            d_shared_all = lax.dynamic_update_slice_in_dim(
                d_shared_all, current + jnp.concatenate([d_keys, d_values], axis=1), start_row, 0
            )
            return (d_query_rot, d_shared_all)

        d_query_rot, d_shared_all = lax.fori_loop(
            0,
            blocks_used,
            grad_step,
            (jnp.zeros((local_rows, H, HD), jnp.float32), jnp.zeros((seqlen, 2 * HD), jnp.float32)),
        )
        d_shared_mine = lax.psum_scatter(
            d_shared_all.astype(jnp.bfloat16), "seq", scatter_dimension=0, tiled=True
        ).astype(jnp.float32)
        d_shared = jnp.concatenate(
            [rotate(d_shared_mine[:, :HD], cosine, -sine_part), d_shared_mine[:, HD:]], axis=1
        ).astype(jnp.bfloat16)
        d_queries = (
            rotate(d_query_rot, cosine[:, None, :], -sine_part[:, None, :])
            .reshape(local_rows, model_width)
            .astype(jnp.bfloat16)
        )
        grad_w_query = jnp.einsum(
            "rd,re->de", hidden1, d_queries, preferred_element_type=jnp.float32
        )
        grad_w_kv = jnp.einsum("rd,rc->dc", hidden1, d_shared, preferred_element_type=jnp.float32)
        kv_bias_total = kv_bias_total + jnp.sum(d_shared.astype(jnp.float32), axis=0)
        d_normed1 = jnp.einsum(
            "re,de->rd", d_queries, query_back, preferred_element_type=jnp.float32
        ) + jnp.einsum("rc,dc->rd", d_shared, kv_back, preferred_element_type=jnp.float32)
        upstream_sum = jnp.sum(upstream_f, axis=0)
        grad_vectors = jnp.stack(
            [
                jnp.sum(d_normed1 * normed1, axis=0),
                jnp.sum(d_normed1, axis=0),
                jnp.sum(d_normed2 * normed2, axis=0),
                jnp.sum(d_normed2, axis=0),
                jnp.sum(d_queries.astype(jnp.float32), axis=0),
                upstream_sum,
                upstream_sum,
            ]
        )
        input_grads.append(
            upstream_f
            + norm_back(d_normed1, normed1, inverse1, vector_back_f[0])
            + norm_back(d_normed2, normed2, inverse2, vector_back_f[2])
        )
        shares = (
            lax.psum_scatter(grad_w_query, ("dp", "seq"), scatter_dimension=0, tiled=True),
            lax.psum_scatter(grad_w_kv, ("dp", "seq"), scatter_dimension=0, tiled=True),
            lax.psum_scatter(grad_w_out, ("dp", "seq"), scatter_dimension=0, tiled=True),
            lax.psum_scatter(grad_w_up, ("dp", "seq"), scatter_dimension=0, tiled=True),
            lax.psum_scatter(grad_w_down, ("dp", "seq"), scatter_dimension=0, tiled=True),
            lax.psum_scatter(grad_b_up, ("dp", "seq"), scatter_dimension=0, tiled=True),
            lax.psum_scatter(grad_vectors, ("dp", "seq"), scatter_dimension=1, tiled=True),
        )
        totals = shares if totals is None else tree_add(totals, shares)
    kv_bias_grad = lax.psum(kv_bias_total, ("dp", "seq"))
    return (
        jnp.stack(results)[:, None],
        jnp.stack(input_grads)[:, None],
        totals[0],
        totals[1],
        totals[2],
        totals[3],
        totals[4],
        totals[5],
        totals[6],
        kv_bias_grad,
    )


MESH = pl.DeviceIdType.MESH
NT = (((1,), (1,)), ((), ()))
VM = pl.BlockSpec(memory_space=pltpu.VMEM)
HBM = pl.BlockSpec(memory_space=pl.ANY)
GROUP = 6
KEYS = 512
MINI = 256
scale_log2 = 0.125 * 1.4426950408889634


def dot(left, right):
    return jnp.dot(left, right, preferred_element_type=jnp.float32)


def dot_nt(left, right):
    return lax.dot_general(left, right, NT, preferred_element_type=jnp.float32)


def bf(values):
    return values.astype(jnp.bfloat16)


def f32(values):
    return values.astype(jnp.float32)


def rotate_rows(block, cosine, sine_part):
    half_rot = ROT // 2
    first, second = block[:half_rot], block[half_rot:ROT]
    return jnp.concatenate(
        [first * cosine - second * sine_part, second * cosine + first * sine_part, block[ROT:]],
        axis=0,
    )


def here():
    return lax.axis_index("dp"), lax.axis_index("seq")


def greet(targets):
    barrier = pltpu.get_barrier_semaphore()
    for target in targets:
        pl.semaphore_signal(barrier, inc=1, device_id=target, device_id_type=MESH)
    pl.semaphore_wait(barrier, len(targets))


def remote(source, target, send, recv, device):
    return pltpu.make_async_remote_copy(
        src_ref=source,
        dst_ref=target,
        send_sem=send,
        recv_sem=recv,
        device_id=device,
        device_id_type=MESH,
    )


class Gather:
    def __init__(self, shard, slabs, halves, send, recv):
        self.shard, self.slabs, self.halves, self.send, self.recv = shard, slabs, halves, send, recv
        self.dp, self.seq = here()
        self.sent = []

    def index(self, dp_flip, z_flip, core_flip=0):
        return (self.dp ^ dp_flip) * 8 + (self.seq ^ (2 * z_flip + core_flip))

    def part(self, slab, half):
        rows, columns = half
        return self.slabs.at[slab, rows, columns]

    def start(self, number, source, target, device):
        remote(source, target, self.send.at[number], self.recv.at[number], device).start()
        self.sent.append(number)

    def arrived(self, number, target):
        remote(target, target, self.send.at[number], self.recv.at[number], (self.dp, self.seq ^ 1)).wait_recv()

    def along_z(self, flip):
        self.start(flip - 1, self.shard, self.slabs.at[self.index(0, 0)], (self.dp, self.seq ^ (2 * flip)))

    def own(self):
        mine = self.slabs.at[self.index(0, 0)]
        self.start(3, self.shard, mine, (self.dp ^ 1, self.seq))
        self.start(7, self.shard, mine, (self.dp ^ 2, self.seq))
        self.start(19, self.shard, mine, (self.dp, self.seq ^ 1))

    def from_z(self, flip):
        piece = self.slabs.at[self.index(0, flip)]
        self.arrived(flip - 1, piece)
        self.start(3 + flip, piece, piece, (self.dp ^ 1, self.seq))
        self.start(7 + flip, piece, piece, (self.dp ^ 2, self.seq))
        if flip == 2:
            self.start(2, piece, piece, (self.dp, self.seq ^ 2))
        self.start(19 + flip, piece, piece, (self.dp, self.seq ^ 1))

    def from_xy(self, flip):
        for axis, half in ((1, 0), (2, 1)):
            number = 3 if axis == 1 else 7
            slab = self.index(axis, flip)
            piece = self.slabs.at[slab]
            self.arrived(number + flip, piece)
            cut = self.part(slab, self.halves[half])
            self.start(11 + 4 * half + flip, cut, cut, (self.dp ^ (3 - axis), self.seq))
            self.start((23 if axis == 1 else 27) + flip, piece, piece, (self.dp, self.seq ^ 1))

    def from_diagonal(self, flip):
        slab = self.index(3, flip)
        for half in (0, 1):
            self.arrived(11 + 4 * half + flip, self.part(slab, self.halves[half]))
        piece = self.slabs.at[slab]
        self.start(31 + flip, piece, piece, (self.dp, self.seq ^ 1))

    def from_core(self):
        for number, dp_flip in ((19, 0), (23, 1), (27, 2), (31, 3)):
            for flip in range(4):
                self.arrived(number + flip, self.slabs.at[self.index(dp_flip, flip, 1)])

    def finish(self):
        for number in self.sent:
            view = self.part(0, self.halves[(number - 11) // 4]) if 11 <= number < 19 else self.slabs.at[0]
            remote(view, view, self.send.at[number], self.recv.at[number], (self.dp, self.seq ^ 1)).wait_send()


def attend(
    micro, steps, row0, off_ref, q_t, do_t, kv_ref, kv_t, att_t, dq_t, dkv, pair, scaled, score_ref, weight_ref, tick
):
    cols = slice(micro * MINI, (micro + 1) * MINI)
    row_ids = row0 + lax.broadcasted_iota(jnp.int32, (1, MINI), 1)
    begin = row_ids - off_ref[micro]

    def group_step(group, carry):
        heads = [pl.ds(pl.multiple_of((group * GROUP + n) * HD, HD), HD) for n in range(GROUP)]
        for n, head in enumerate(heads):
            pair[n, :HD, :MINI] = q_t[head, cols]
            pair[n, HD:, MINI:] = do_t[head, cols]

        def score_step(step, tops):
            keys = pl.ds(pl.multiple_of(step * KEYS, KEYS), KEYS)
            block = kv_ref[micro, keys, :]
            ids = step * KEYS + lax.broadcasted_iota(jnp.int32, (KEYS, 1), 0)
            allowed = (ids <= row_ids) & (ids >= begin)
            found = []
            for n in range(GROUP):
                both = dot(block, pair[n])
                scores = jnp.where(allowed, both[:, :MINI] * scale_log2, masked_score)
                score_ref[n, keys, :MINI] = scores
                score_ref[n, keys, MINI:] = both[:, MINI:]
                found.append(jnp.maximum(tops[n], jnp.max(scores.reshape(KEYS // 8, 8, MINI), axis=0)))
            return tuple(found)

        tops = lax.fori_loop(
            0, steps, score_step, tuple(jnp.full((8, MINI), masked_score, jnp.float32) for _ in heads)
        )
        tops = [jnp.max(top, axis=0, keepdims=True) for top in tops]
        tick(micro, group, 0)

        def value_step(step, carried):
            keys = pl.ds(pl.multiple_of(step * KEYS, KEYS), KEYS)
            values = kv_t[micro, HD:, keys]
            found = []
            for n in range(GROUP):
                output, total = carried[n]
                weights = jnp.exp2(score_ref[n, keys, :MINI] - tops[n])
                total = total + jnp.sum(weights.reshape(KEYS // 8, 8, MINI), axis=0)
                weight_ref[n, keys, :] = bf(weights)
                found.append((output + dot(values, bf(weights)), total))
            return tuple(found)

        sums = lax.fori_loop(
            0,
            steps,
            value_step,
            tuple((jnp.zeros((HD, MINI), jnp.float32), jnp.zeros((8, MINI), jnp.float32)) for _ in heads),
        )
        tick(micro, group, 1)
        inverses, deltas = [], []
        for n, head in enumerate(heads):
            inverse = 1.0 / jnp.sum(sums[n][1], axis=0, keepdims=True)
            output = sums[n][0] * inverse
            upstream = f32(do_t[head, cols])
            deltas.append(jnp.sum(output * upstream, axis=0, keepdims=True))
            inverses.append(inverse)
            att_t[head, cols] = bf(output)
            scaled[n, :HD, :MINI] = bf(f32(q_t[head, cols]) * inverse)
            scaled[n, HD:, MINI:] = bf(upstream * inverse)

        def grad_step(step, carried):
            keys = pl.ds(pl.multiple_of(step * KEYS, KEYS), KEYS)
            key_block = kv_t[micro, :HD, keys]
            total = dkv[micro, keys, :]
            found = []
            for n in range(GROUP):
                weights = weight_ref[n, keys, :]
                d_scores = bf(f32(weights) * (score_ref[n, keys, MINI:] - deltas[n]))
                found.append(carried[n] + dot(key_block, d_scores))
                total = total + dot_nt(d_scores, scaled[n, :, :MINI])
                total = total + dot_nt(weights, scaled[n, :, MINI:])
            dkv[micro, keys, :] = total
            return tuple(found)

        grads = lax.fori_loop(
            0, steps, grad_step, tuple(jnp.zeros((HD, MINI), jnp.float32) for _ in heads)
        )
        for n, head in enumerate(heads):
            dq_t[head, cols] = grads[n] * (inverses[n] * 0.125)
        tick(micro, group, 2)
        return carry

    lax.fori_loop(0, H // GROUP, group_step, 0)


def spread(slabs):
    lane = lax.broadcasted_iota(jnp.int32, (8, 128), 1)
    row = lax.broadcasted_iota(jnp.int32, (8, 128), 0)
    rows = [jnp.zeros((8, 128), jnp.float32) for _ in range(6)]
    wide = [jnp.zeros((8, 128), jnp.float32) for _ in range(24)]
    for number in range(32):
        for width, target, keep in ((24, rows, row < 7), (96, wide, row == 7)):
            block, shift = divmod(number * width, 128)
            piece = jnp.where(keep, slabs[number], 0.0)
            piece = pltpu.roll(piece, shift, 1) if shift else piece
            target[block] = target[block] + jnp.where(lane >= shift, piece, 0.0)
            if shift + width > 128:
                target[block + 1] = target[block + 1] + jnp.where(lane < shift, piece, 0.0)
    return jnp.concatenate(rows, axis=1), jnp.concatenate(wide, axis=1)


def slab_order(store, block, dp_index, rows):
    for z in range(4):
        for core in range(2):
            first = (2 * z + core) * rows
            store(dp_index, core, z, bf(block[first : first + rows]))


def attention_kernel(
    x_ref, cot_ref, off_ref, wq_ref, wkv_in, wout_ref, vec_in, bup_in, bkv_ref, up_ref, down_ref,
    up_slabs, down_slabs, vec_ref, bup_ref, wkv_ref, cos_ref, sin_ref, attn_ref, dn_ref, dkv_out, grads_ref, dqsum_ref,
    small_ref, pair_ref, extra, slabs, pair_slabs, weights, out_weights, n1t_ref, q_t, do_t, att_t, dq_t, kv_ref, kv_t, dkv, pair, scaled,
    score_ref, weight_ref,
    send_a, recv_a, send_o, recv_o, send_u, recv_u, send_d, recv_d, send_kv, recv_kv, local_sem,
):
    dp, seq = here()

    def halves(shape, axis):
        middle = shape[axis] // 2
        cuts = [slice(0, middle), slice(middle, 2 * middle)]
        return tuple((cut, slice(None)) if axis == 0 else (slice(None), cut) for cut in cuts)

    gather_a = Gather(small_ref, slabs, halves(small_ref.shape, 1), send_a, recv_a)
    gather_o = Gather(pair_ref, pair_slabs, halves(pair_ref.shape, 1), send_o, recv_o)
    gather_u = Gather(up_ref, up_slabs, halves(up_ref.shape, 1), send_u, recv_u)
    gather_d = Gather(down_ref, down_slabs, halves(down_ref.shape, 0), send_d, recv_d)

    def signal():
        barrier = pltpu.get_barrier_semaphore()
        for target in friends:
            pl.semaphore_signal(barrier, inc=1, device_id=target, device_id_type=MESH)

    friends = [(dp, seq ^ 1), (dp, seq ^ 2), (dp, seq ^ 4), (dp, seq ^ 6), (dp ^ 1, seq), (dp ^ 2, seq)]
    signal()
    extra[...] = jnp.zeros_like(extra)
    extra[0:7, 0 : vec_in.shape[1]] = f32(vec_in[...])
    extra[7:8, 0 : bup_in.shape[1]] = f32(bup_in[...])
    small_ref[:, 0:128] = wkv_in[...]
    small_ref[:, 128:256] = bf(extra[...])
    pair_ref[:, 0:768] = wq_ref[...]
    pair_ref[:, 768:1536] = wout_ref[...]
    pl.semaphore_wait(pltpu.get_barrier_semaphore(), len(friends))
    for flip in (1, 2):
        gather_a.along_z(flip)
    gather_a.own()
    gather_o.along_z(1)
    gather_o.own()
    gather_u.own()
    mine = gather_a.index(0, 0)
    local_copies = [
        pltpu.make_async_copy(small_ref, slabs.at[mine], local_sem.at[0]),
        pltpu.make_async_copy(pair_ref, pair_slabs.at[mine], local_sem.at[1]),
        pltpu.make_async_copy(up_ref, up_slabs.at[mine], local_sem.at[2]),
        pltpu.make_async_copy(down_ref, down_slabs.at[mine], local_sem.at[3]),
    ]
    for copy in local_copies:
        copy.start()
    pair[...] = jnp.zeros_like(pair)
    scaled[...] = jnp.zeros_like(scaled)
    dkv[...] = jnp.zeros_like(dkv)
    rank = f32(lax.broadcasted_iota(jnp.int32, (ROT // 2, 1), 0))
    frequency = jnp.exp(rank * (-2.0 / ROT * math.log(10000.0)))
    for micro in range(2):
        cols = slice(micro * MINI, (micro + 1) * MINI)
        angle = (f32(off_ref[micro]) * 0.25) * frequency
        cos_ref[:, cols] = jnp.cos(angle)
        sin_ref[:, cols] = jnp.sin(angle)
    normed, _ = normalize(f32(x_ref[...]))
    for flip in (1, 2, 3):
        gather_a.from_z(flip)
    for flip in range(4):
        gather_a.from_xy(flip)
    gather_o.along_z(2)
    gather_o.from_z(1)
    for flip in range(4):
        gather_a.from_diagonal(flip)
    gather_o.from_xy(0)
    gather_u.along_z(1)
    gather_u.along_z(2)
    gather_a.from_core()
    local_copies[0].wait()

    vectors, wide_row = spread([f32(slabs[number, 0:8, 128:256]) for number in range(32)])
    vec_ref[...] = vectors
    bup_ref[...] = wide_row[7:8]

    def unpack(source, target, columns):
        for number in range(16):
            block = jnp.concatenate(
                [f32(source[2 * number, :, columns]), f32(source[2 * number + 1, :, columns])], axis=0
            )
            target[48 * number : 48 * number + 48, :] = bf(block)

    unpack(slabs, wkv_ref, slice(0, 128))
    hidden = bf(normed * vectors[0:1] + vectors[1:2])
    kv_pre = dot(hidden, wkv_ref[...]) + f32(bkv_ref[...])
    kv_pre_t = kv_pre.T
    cosine, sine_part = cos_ref[...], sin_ref[...]
    shared_t = bf(jnp.concatenate([rotate_rows(kv_pre_t[:HD], cosine, sine_part), kv_pre_t[HD:]], axis=0))
    shared = bf(f32(shared_t).T)
    place = pl.ds(pl.multiple_of(seq * MINI, MINI), MINI)
    kv_copies = []
    for micro in range(2):
        kv_ref[micro, place, :] = shared[micro * MINI : (micro + 1) * MINI]

    def kv_block(micro, flip):
        return kv_ref.at[micro, pl.ds(pl.multiple_of((seq ^ flip) * MINI, MINI), MINI)]

    def kv_send(micro, flip, number, device):
        block = kv_block(micro, flip)
        copy = remote(block, block, send_kv.at[micro, number], recv_kv.at[micro, number], device)
        copy.start()
        kv_copies.append(copy)

    def kv_arrived(micro, flip, number):
        block = kv_block(micro, flip)
        remote(block, block, send_kv.at[micro, number], recv_kv.at[micro, number], (dp, seq ^ 1)).wait_recv()

    def kv_start(micro):
        for flip in (1, 2, 3):
            kv_send(micro, 0, flip - 1, (dp, seq ^ (2 * flip)))
        kv_send(micro, 0, 3, (dp, seq ^ 1))

    def kv_forward(micro):
        for flip in (1, 2, 3):
            kv_arrived(micro, 2 * flip, flip - 1)
            kv_send(micro, 2 * flip, 3 + flip, (dp, seq ^ 1))

    def kv_finish(micro):
        for flip in range(4):
            kv_arrived(micro, 2 * flip + 1, 3 + flip)
        kv_t[micro] = bf(f32(kv_ref[micro]).T)

    kv_start(0)
    gather_o.from_z(2)
    gather_o.from_xy(1)
    gather_o.from_diagonal(0)
    gather_o.from_z(3)
    gather_o.from_xy(2)
    gather_o.from_diagonal(1)
    n1t_ref[...] = bf(f32(hidden).T)
    kv_forward(0)
    gather_o.from_xy(3)
    gather_d.along_z(1)
    gather_d.along_z(2)
    gather_d.own()
    gather_u.from_z(1)
    gather_u.from_xy(0)
    gather_o.from_diagonal(2)
    gather_o.from_diagonal(3)
    kv_start(1)
    kv_finish(0)
    local_copies[1].wait()
    gather_o.from_core()
    unpack(pair_slabs, weights, slice(0, 768))
    unpack(pair_slabs, out_weights, slice(768, 1536))
    query = (dot(hidden, weights[...]) + vectors[4:5]).T
    for head in range(H):
        q_t[head * HD : (head + 1) * HD, :] = bf(
            rotate_rows(query[head * HD : (head + 1) * HD], cosine, sine_part)
        )
    do_t[...] = bf(dot_nt(out_weights[...], cot_ref[...]))

    def each(name, *flips):
        def act():
            for gather in (gather_u, gather_d):
                for flip in flips:
                    getattr(gather, name)(flip)

        return act

    def then(*acts):
        def act():
            for one in acts:
                one()

        return act

    actions = [
        then(lambda: gather_d.from_z(1), lambda: gather_d.from_xy(0)),
        None,
        then(each("from_z", 2), lambda: gather_u.from_diagonal(0)),
        each("from_xy", 1),
        then(lambda: gather_d.from_diagonal(0), each("from_z", 3)),
        each("from_diagonal", 1),
        each("from_xy", 2),
        each("from_diagonal", 2),
        each("from_xy", 3),
        None,
        each("from_diagonal", 3),
        None,
    ]

    def tick(micro, group, part):
        for number in range(H // GROUP):
            act = actions[(micro * (H // GROUP) + number) * 3 + part]
            if act is not None:
                pl.when(group == number)(act)

    kv_forward(1)
    steps = lax.div((seq + 1) * MINI + KEYS - 1, KEYS)
    for micro in range(2):
        if micro == 1:
            kv_finish(1)
        attend(
            micro, steps, seq * MINI, off_ref, q_t, do_t, kv_ref, kv_t, att_t, dq_t, dkv,
            pair, scaled, score_ref, weight_ref, tick,
        )
    for micro in range(2):
        for core in range(2):
            for z in range(4):
                first = (2 * z + core) * MINI
                block = dkv[micro, first : first + MINI, :]
                scale = jnp.where(lax.broadcasted_iota(jnp.int32, (1, 2 * HD), 1) < HD, 0.125, 1.0)
                dkv_out[core, z, micro] = bf(block * scale)
    attn_ref[...] = dot(bf(f32(att_t[...]).T), out_weights[...]) + vectors[5:6]
    for head in range(H):
        dq_t[head * HD : (head + 1) * HD, :] = rotate_rows(
            dq_t[head * HD : (head + 1) * HD, :], cosine, -sine_part
        )
    d_query = bf(dq_t[...].T)
    dqsum_ref[...] = jnp.sum(f32(d_query), axis=0, keepdims=True)
    dn_ref[...] = dot_nt(d_query, weights[...])
    for block in range(4):
        rows = slice(192 * block, 192 * block + 192)

        def put_query(dp_index, core, z, piece):
            grads_ref[dp_index, core, z, :, 0:768] = piece

        def put_out(dp_index, core, z, piece):
            grads_ref[dp_index, core, z, :, 768:1536] = piece

        slab_order(put_query, dot(n1t_ref[rows, :], d_query), block, 24)
        slab_order(put_out, dot(att_t[rows, :], cot_ref[...]), block, 24)
    for gather in (gather_u, gather_d):
        gather.from_core()
    for gather in (gather_a, gather_o, gather_u, gather_d):
        gather.finish()
    for copy in kv_copies:
        copy.wait_send()
    for copy in local_copies[2:]:
        copy.wait()


def attention_call(x, cot, offsets, w_query, w_kv, w_out, vectors, b_up, b_kv, w_up, w_down):
    rows = x.shape[0]
    dma = pltpu.SemaphoreType.DMA
    out = jax.ShapeDtypeStruct
    seqlen = 8 * MINI
    b16 = jnp.bfloat16
    return pl.pallas_call(
        attention_kernel,
        out_shape=(
            out((32,) + w_up.shape, b16),
            out((32,) + w_down.shape, b16),
            out((8, 768), jnp.float32),
            out((1, 3072), jnp.float32),
            out((768, 128), b16),
            out((ROT // 2, rows), jnp.float32),
            out((ROT // 2, rows), jnp.float32),
            out((rows, 768), jnp.float32),
            out((rows, 768), jnp.float32),
            out((2, 4, 2, MINI, 2 * HD), b16),
            out((4, 2, 4, 24, 1536), b16),
            out((1, 768), jnp.float32),
        ),
        in_specs=[VM] * 9 + [HBM] * 2,
        out_specs=(HBM, HBM) + (VM,) * 10,
        scratch_shapes=[
            pltpu.VMEM((24, 256), b16),
            pltpu.VMEM((24, 1536), b16),
            pltpu.VMEM((24, 128), jnp.float32),
            pltpu.VMEM((32, 24, 256), b16),
            pltpu.VMEM((32, 24, 1536), b16),
            pltpu.VMEM((768, 768), b16),
            pltpu.VMEM((768, 768), b16),
            pltpu.VMEM((768, rows), b16),
            pltpu.VMEM((768, rows), b16),
            pltpu.VMEM((768, rows), b16),
            pltpu.VMEM((768, rows), b16),
            pltpu.VMEM((768, rows), jnp.float32),
            pltpu.VMEM((2, seqlen, 2 * HD), b16),
            pltpu.VMEM((2, 2 * HD, seqlen), b16),
            pltpu.VMEM((2, seqlen, 2 * HD), jnp.float32),
            pltpu.VMEM((GROUP, 2 * HD, 2 * MINI), b16),
            pltpu.VMEM((GROUP, 2 * HD, 2 * MINI), b16),
            pltpu.VMEM((GROUP, seqlen, 2 * MINI), jnp.float32),
            pltpu.VMEM((GROUP, seqlen, MINI), b16),
        ]
        + [dma((35,))] * 8
        + [dma((2, 7))] * 2
        + [dma((4,))],
        compiler_params=pltpu.CompilerParams(
            collective_id=0, has_side_effects=True, vmem_limit_bytes=60 << 20
        ),
        name="attention",
    )(x, cot, offsets, w_query, w_kv, w_out, vectors, b_up, b_kv, w_up, w_down)


def packed_on_device(inputs, offsets, w_query, w_kv, w_out, w_up, w_down, b_up, vectors, b_kv, cotangent):
    rows = 2 * MINI
    x = inputs.reshape(rows, 768)
    cot = cotangent.reshape(rows, 768)
    up_slabs, down_slabs, vec, bup, wkv, cosine, sine_part, attn, dn1, dkv, grads_a, dq_sum = attention_call(
        x, cot, offsets, w_query, w_kv, w_out, vectors, b_up.reshape(1, -1), b_kv.reshape(1, -1), w_up, w_down
    )
    return feed_forward(x, cot, cosine, sine_part, up_slabs, down_slabs, vec, bup, wkv, attn, dn1, dkv, grads_a, dq_sum)


class Scatter:
    def __init__(self, slabs, from_core, from_diagonal, from_xy, from_z, send, recv):
        self.slabs, self.from_core, self.from_diagonal = slabs, from_core, from_diagonal
        self.from_xy, self.from_z, self.send, self.recv = from_xy, from_z, send, recv
        self.dp, self.seq = here()
        self.core = lax.rem(self.seq, 2)
        self.z = lax.div(self.seq, 2)
        self.sent = []

    def start(self, number, source, target, device):
        copy = remote(source, target, self.send.at[number], self.recv.at[number], device)
        copy.start()
        self.sent.append(copy)

    def arrived(self, number, target):
        remote(target, target, self.send.at[number], self.recv.at[number], (self.dp, self.seq ^ 1)).wait_recv()

    def block(self, flip):
        return self.slabs.at[self.dp ^ flip, self.core]

    def to_core(self, flip):
        other = self.slabs.at[self.dp ^ flip, 1 - self.core]
        self.start(flip, other, self.from_core.at[flip], (self.dp, self.seq ^ 1))

    def add(self, block, z, terms):
        total = f32(block[z])
        for term in terms:
            total = total + f32(term)
        block[z] = bf(total)

    def diagonal(self):
        block = self.block(3)
        self.arrived(3, self.from_core.at[3])
        for half in (0, 1):
            for z in (2 * half, 2 * half + 1):
                self.add(block, z, [self.from_core[3, z]])
            self.start(4 + half, block.at[pl.ds(2 * half, 2)], self.from_diagonal.at[half], (self.dp ^ (1 + half), self.seq))

    def beside(self, axis):
        half = 2 - axis
        block = self.block(axis)
        self.arrived(axis, self.from_core.at[axis])
        self.arrived(4 + half, self.from_diagonal.at[half])
        for z in range(4):
            terms = [self.from_core[axis, z]]
            if z // 2 == half:
                terms.append(self.from_diagonal[half, z % 2])
            self.add(block, z, terms)
        self.start(5 + axis, block, self.from_xy.at[axis - 1], (self.dp ^ axis, self.seq))

    def own(self):
        block = self.block(0)
        self.arrived(0, self.from_core.at[0])
        for axis in (1, 2):
            self.arrived(5 + axis, self.from_xy.at[axis - 1])
        for z in range(4):
            self.add(block, z, [self.from_core[0, z], self.from_xy[0, z], self.from_xy[1, z]])
        for flip in (1, 2, 3):
            self.start(7 + flip, block.at[self.z ^ flip], self.from_z.at[flip - 1], (self.dp, self.seq ^ (2 * flip)))

    def total(self):
        value = f32(self.slabs[self.dp, self.core, self.z])
        for flip in (1, 2, 3):
            self.arrived(7 + flip, self.from_z.at[flip - 1])
            value = value + f32(self.from_z[flip - 1])
        return value

    def finish(self):
        for copy in self.sent:
            copy.wait_send()


def feed_kernel(
    x_ref, cot_ref, cos_ref, sin_ref, vec_ref, bup_ref, wkv_ref, attn_ref, dn_ref, dqsum_ref, dkv_in, grads_a, up_hbm, down_hbm,
    out_ref, gin_ref, gq_ref, go_ref, gu_ref, gkv_ref, gd_ref, small_out,
    up_ref, down_ref, n1t_ref, n2_ref, n2t_ref, act_ref, dh_ref, mlp_ref, dshared_ref, stats,
    a_slabs, d_slabs, u_slabs, v_slabs,
    a_core, a_diag, a_xy, a_z, d_core, d_diag, d_xy, d_z, u_core, u_diag, u_xy, u_z, v_core, v_diag, v_xy, v_z,
    dkv, dkv_core, dkv_z, small, small_in,
    send_s, recv_s, send_k, recv_k, send_m, recv_m, load_sem,
):
    dp, seq = here()
    core, z = lax.rem(seq, 2), lax.div(seq, 2)
    loads = [
        pltpu.make_async_copy(dkv_in, dkv, load_sem.at[2]),
        pltpu.make_async_copy(grads_a, a_slabs, load_sem.at[3]),
        pltpu.make_async_copy(up_hbm, up_ref, load_sem.at[0]),
        pltpu.make_async_copy(down_hbm, down_ref, load_sem.at[1]),
    ]
    for copy in loads:
        copy.start()
    greet(
        [(dp, seq ^ 1), (dp, seq ^ 2), (dp, seq ^ 4), (dp, seq ^ 6), (dp ^ 1, seq), (dp ^ 2, seq)]
    )
    scatter_a = Scatter(a_slabs, a_core, a_diag, a_xy, a_z, send_s.at[0], recv_s.at[0])
    scatter_d = Scatter(d_slabs, d_core, d_diag, d_xy, d_z, send_s.at[1], recv_s.at[1])
    scatter_u = Scatter(u_slabs, u_core, u_diag, u_xy, u_z, send_s.at[2], recv_s.at[2])
    scatter_v = Scatter(v_slabs, v_core, v_diag, v_xy, v_z, send_s.at[3], recv_s.at[3])
    kv_sent = []

    def kv_start(number, source, target, device):
        copy = remote(source, target, send_k.at[number], recv_k.at[number], device)
        copy.start()
        kv_sent.append(copy)

    def kv_arrived(number, target):
        remote(target, target, send_k.at[number], recv_k.at[number], (dp, seq ^ 1)).wait_recv()

    loads[1].wait()
    for flip in (3, 1, 2, 0):
        scatter_a.to_core(flip)
    loads[0].wait()
    kv_start(0, dkv.at[1 - core], dkv_core, (dp, seq ^ 1))
    scatter_a.diagonal()

    vectors = vec_ref[...]
    for start in range(0, 2 * MINI, MINI):
        rows = slice(start, start + MINI)
        normed, inverse = normalize(f32(x_ref[rows, :]))
        stats[rows, :] = jnp.broadcast_to(inverse, (MINI, 128))
        n1t_ref[:, rows] = bf((normed * vectors[0:1] + vectors[1:2]).T)
        second = normed * vectors[2:3] + vectors[3:4]
        n2_ref[rows, :] = bf(second)
        n2t_ref[:, rows] = bf(second.T)
    kv_arrived(0, dkv_core)
    for index in range(4):
        for micro in range(2):
            dkv[core, index, micro] = bf(f32(dkv[core, index, micro]) + f32(dkv_core[index, micro]))
    for flip in (1, 2, 3):
        kv_start(flip, dkv.at[core, z ^ flip], dkv_z.at[flip - 1], (dp, seq ^ (2 * flip)))
    scatter_a.beside(1)
    scatter_a.beside(2)
    loads[2].wait()
    loads[3].wait()

    def chunk(flip, first):
        base = (dp ^ flip) * 768

        def tile(number, carry):
            columns = pl.ds(pl.multiple_of(base + number * 256, 256), 256)
            hidden = dot(n2_ref[...], up_ref[:, columns]) + bup_ref[0:1, columns]
            d_act = dot_nt(cot_ref[...], down_ref[columns, :])
            normal = 0.5 + 0.5 * lax.erf(hidden * root_half)
            density = density_scale * jnp.exp(-0.5 * hidden * hidden)
            d_hidden = bf(d_act * (normal + hidden * density))
            act_ref[:, pl.ds(pl.multiple_of(number * 256, 256), 256)] = bf(hidden * normal)
            dh_ref[:, columns] = d_hidden
            return carry

        lax.fori_loop(0, 3, tile, 0)
        down_rows = pl.ds(pl.multiple_of(base, 768), 768)
        part = dot(act_ref[...], down_ref[down_rows, :])
        mlp_ref[...] = part if first else mlp_ref[...] + part

        grad_t = bf(f32(act_ref[...]).T)
        for number in range(4):
            grad = dot(grad_t[192 * number : 192 * number + 192], cot_ref[...])
            for half in range(2):
                d_slabs[dp ^ flip, half, number] = bf(grad[96 * half : 96 * half + 96])
        scatter_d.to_core(flip)

    def put(store, block, flip, rows):
        for index in range(4):
            for half in range(2):
                first = (2 * index + half) * rows
                store(dp ^ flip, half, index, bf(block[first : first + rows]))

    def up_block(flip, left):
        rows = pl.ds(pl.multiple_of((dp ^ flip) * 192, 192), 192)
        if left:

            def put_left(target, half, index, piece):
                u_slabs[target, half, index, :, 0:1536] = piece

            def put_kv(target, half, index, piece):
                u_slabs[target, half, index, :, 1536:1664] = piece

            put(put_left, dot(n2t_ref[rows, :], dh_ref[:, 0:1536]), flip, 24)
            put(put_kv, dot(n1t_ref[rows, :], dshared_ref[...]), flip, 24)
            scatter_u.to_core(flip)
        else:

            def put_right(target, half, index, piece):
                v_slabs[target, half, index] = piece

            put(put_right, dot(n2t_ref[rows, :], dh_ref[:, 1536:3072]), flip, 24)
            scatter_v.to_core(flip)

    chunk(3, True)
    scatter_d.diagonal()
    chunk(1, False)
    scatter_a.own()
    scatter_d.beside(1)
    for flip in (1, 2, 3):
        kv_arrived(flip, dkv_z.at[flip - 1])
    cosine, sine_part = cos_ref[...], sin_ref[...]
    for micro in range(2):
        cols = slice(micro * MINI, (micro + 1) * MINI)
        total = f32(dkv[core, z, micro])
        for flip in (1, 2, 3):
            total = total + f32(dkv_z[flip - 1, micro])
        total_t = total.T
        total_t = jnp.concatenate(
            [rotate_rows(total_t[:HD], cosine[:, cols], -sine_part[:, cols]), total_t[HD:]], axis=0
        )
        dshared_ref[cols, :] = bf(total_t.T)
    chunk(2, False)
    scatter_d.beside(2)
    chunk(0, False)
    up_block(3, True)
    up_block(1, True)
    scatter_u.diagonal()
    up_block(2, True)
    up_block(0, True)
    scatter_d.own()
    up_block(3, False)
    up_block(1, False)
    scatter_u.beside(1)
    scatter_u.beside(2)
    scatter_v.diagonal()
    up_block(2, False)
    up_block(0, False)
    zero = jnp.zeros((1, 768), jnp.float32)
    sums = [zero] * 5
    for start in range(0, 2 * MINI, 128):
        rows = slice(start, start + 128)
        values = f32(x_ref[rows, :])
        upstream = f32(cot_ref[rows, :])
        inverse = stats[rows, 0:1]
        normed = (values - jnp.mean(values, axis=-1, keepdims=True)) * inverse
        out_ref[rows, :] = bf(values + attn_ref[rows, :] + mlp_ref[rows, :] + vectors[6:7])
        first = dn_ref[rows, :] + dot_nt(dshared_ref[rows, :], wkv_ref[...])
        second = dot_nt(dh_ref[rows, :], up_ref[...])
        gin_ref[rows, :] = (
            upstream
            + norm_back(first, normed, inverse, vectors[0:1])
            + norm_back(second, normed, inverse, vectors[2:3])
        )
        news = (first * normed, first, second * normed, second, upstream)
        sums = [total + jnp.sum(new, axis=0, keepdims=True) for total, new in zip(sums, news)]
    b_up_sum = jnp.sum(f32(dh_ref[...]), axis=0, keepdims=True)
    kv_sum = jnp.sum(f32(dshared_ref[...]), axis=0, keepdims=True)
    small[0] = jnp.concatenate(
        sums[:4]
        + [dqsum_ref[...], sums[4], sums[4], zero]
        + [b_up_sum[:, 768 * n : 768 * n + 768] for n in range(4)]
        + [jnp.concatenate([kv_sum, zero[:, 128:]], axis=1)]
        + [zero] * 3,
        axis=0,
    )
    partners = [(dp, seq ^ 1), (dp, seq ^ 2), (dp, seq ^ 4), (dp ^ 1, seq), (dp ^ 2, seq)]
    small_sent = []

    def small_start(number):
        copy = remote(small.at[number], small_in.at[number], send_m.at[number], recv_m.at[number], partners[number])
        copy.start()
        small_sent.append(copy)

    def small_end(number):
        small_sent[number].wait_recv()
        small[number + 1] = small[number] + small_in[number]

    total = scatter_a.total()
    gq_ref[...] = total[:, :768]
    go_ref[...] = total[:, 768:]
    small_start(0)
    scatter_v.beside(1)
    scatter_v.beside(2)
    small_end(0)
    small_start(1)
    scatter_u.own()
    small_end(1)
    small_start(2)
    gd_ref[...] = scatter_d.total()
    scatter_v.own()
    small_end(2)
    small_start(3)
    total = scatter_u.total()
    gu_ref[:, 0:1536] = total[:, 0:1536]
    gkv_ref[...] = total[:, 1536:1664]
    small_end(3)
    small_start(4)
    small_end(4)
    small_out[...] = small[5]
    gu_ref[:, 1536:3072] = scatter_v.total()
    for scatter in (scatter_a, scatter_d, scatter_u, scatter_v):
        scatter.finish()
    for copy in kv_sent + small_sent:
        copy.wait_send()


def place_kernel(small, *refs):
    wholes, results = refs[:7], refs[7:17]
    for source, target in zip(wholes, results):
        target[...] = source[...]
    dp, seq = here()
    rows = small[0:8, :]
    shift = lax.rem(768 - 24 * (8 * dp + seq), 768)
    results[7][...] = pltpu.roll(rows, shift, 1)[0:7, 0:24]
    wide = jnp.broadcast_to(small[pl.ds(8 + dp, 1), :], (8, 768))
    shift = lax.rem(768 - 96 * seq, 768)
    results[8][...] = pltpu.roll(wide, shift, 1)[0:1, 0:96]
    results[9][...] = small[12:13, 0 : 2 * HD]


def feed_forward(x, cot, cosine, sine_part, up_slabs, down_slabs, vec, bup, wkv, attn, dn1, dkv, grads_a, dq_sum):
    rows = x.shape[0]
    dma = pltpu.SemaphoreType.DMA
    out = jax.ShapeDtypeStruct
    b16 = jnp.bfloat16
    shapes = ((24, 1536), (96, 768), (24, 1664), (24, 1536))
    buffers = [pltpu.VMEM((4, 2, 4) + shape, b16) for shape in shapes]
    for shape in shapes:
        for lead in ((4, 4), (2, 2), (2, 4), (3,)):
            buffers.append(pltpu.VMEM(lead + shape, b16))
    out_rows, g_in, g_query, g_out, g_up, g_kv, g_down, small = pl.pallas_call(
        feed_kernel,
        out_shape=(
            out((rows, 768), b16),
            out((rows, 768), jnp.float32),
            out((24, 768), jnp.float32),
            out((24, 768), jnp.float32),
            out((24, 3072), jnp.float32),
            out((24, 128), jnp.float32),
            out((96, 768), jnp.float32),
            out((16, 768), jnp.float32),
        ),
        in_specs=[VM] * 10 + [HBM] * 4,
        out_specs=(VM,) * 8,
        scratch_shapes=[
            pltpu.VMEM((768, 3072), b16),
            pltpu.VMEM((3072, 768), b16),
            pltpu.VMEM((768, rows), b16),
            pltpu.VMEM((rows, 768), b16),
            pltpu.VMEM((768, rows), b16),
            pltpu.VMEM((rows, 768), b16),
            pltpu.VMEM((rows, 3072), b16),
            pltpu.VMEM((rows, 768), jnp.float32),
            pltpu.VMEM((rows, 2 * HD), b16),
            pltpu.VMEM((rows, 128), jnp.float32),
        ]
        + buffers
        + [
            pltpu.VMEM((2, 4, 2, MINI, 2 * HD), b16),
            pltpu.VMEM((4, 2, MINI, 2 * HD), b16),
            pltpu.VMEM((3, 2, MINI, 2 * HD), b16),
            pltpu.VMEM((6, 16, 768), jnp.float32),
            pltpu.VMEM((5, 16, 768), jnp.float32),
            dma((4, 11)),
            dma((4, 11)),
            dma((4,)),
            dma((4,)),
            dma((5,)),
            dma((5,)),
            dma((4,)),
        ],
        compiler_params=pltpu.CompilerParams(
            collective_id=1, has_side_effects=True, vmem_limit_bytes=63 << 20
        ),
        name="feed_forward",
    )(
        x, cot, cosine, sine_part, vec, bup, wkv, attn, dn1, dq_sum, dkv, grads_a,
        up_slabs.reshape(768, 3072), down_slabs.reshape(3072, 768),
    )
    wholes = (out_rows, g_in, g_query, g_kv, g_out, g_up, g_down)
    like = tuple(out(one.shape, one.dtype) for one in wholes)
    results = pl.pallas_call(
        place_kernel,
        out_shape=like + (out((7, 24), jnp.float32), out((1, 96), jnp.float32), out((1, 2 * HD), jnp.float32)),
        in_specs=[VM] * (1 + len(wholes)),
        out_specs=(VM,) * (3 + len(wholes)),
        compiler_params=pltpu.CompilerParams(vmem_limit_bytes=62 << 20),
        name="place",
    )(small, *wholes)
    out_rows, g_in, g_query, g_kv, g_out, g_up, g_down, g_vectors, g_b_up, g_b_kv = results
    return (
        out_rows.reshape(2, 1, MINI, 768), g_in.reshape(2, 1, MINI, 768), g_query, g_kv, g_out,
        g_up, g_down, g_b_up.reshape(-1), g_vectors, g_b_kv.reshape(-1),
    )


def solution(mesh):
    packed = mesh.shape["dp"] == 4 and mesh.shape["seq"] == 8
    on_device = packed_on_device if packed else plain_on_device

    in_specs = (
        P(None, "dp", "seq", None),
        P(None, "dp", "seq"),
        P(("dp", "seq"), None),
        P(("dp", "seq"), None),
        P(("dp", "seq"), None),
        P(("dp", "seq"), None),
        P(("dp", "seq"), None),
        P(("dp", "seq")),
        P(None, ("dp", "seq")),
        P(),
        P(None, "dp", "seq", None),
    )
    out_specs = (
        P(None, "dp", "seq", None),
        P(None, "dp", "seq", None),
        P(("dp", "seq"), None),
        P(("dp", "seq"), None),
        P(("dp", "seq"), None),
        P(("dp", "seq"), None),
        P(("dp", "seq"), None),
        P(("dp", "seq")),
        P(None, ("dp", "seq")),
        P(),
    )
    return jax.shard_map(
        on_device, mesh=mesh, in_specs=in_specs, out_specs=out_specs, check_vma=False
    )
```

```python
import functools
import math

import jax
import jax.numpy as jnp
from jax import lax
from jax.experimental import pallas as pl
from jax.experimental.pallas import tpu as pltpu
from jax.sharding import PartitionSpec as P

H = 12
HD = 64
ROT = 16


epsilon = 1e-05
root_half = 0.7071067811865476
density_scale = 0.3989422804014327
masked_score = -1e30


def normalize(values):
    average = jnp.mean(values, axis=-1, keepdims=True)
    centered = values - average
    inverse = lax.rsqrt(jnp.mean(centered * centered, axis=-1, keepdims=True) + epsilon)
    return (centered * inverse, inverse)


def norm_back(grad_out, normed, inverse, gain_row):
    scaled = grad_out * gain_row
    first_mean = jnp.mean(scaled, axis=-1, keepdims=True)
    second_mean = jnp.mean(scaled * normed, axis=-1, keepdims=True)
    return inverse * (scaled - first_mean - normed * second_mean)


def rotate(values, cosine, sine_part):
    half_rot = ROT // 2
    first_part = values[..., :half_rot]
    second = values[..., half_rot:ROT]
    return jnp.concatenate(
        [
            first_part * cosine - second * sine_part,
            second * cosine + first_part * sine_part,
            values[..., ROT:],
        ],
        axis=-1,
    )


def gelu_slope(hidden):
    return 0.5 * (1.0 + lax.erf(hidden * root_half)) + hidden * density_scale * jnp.exp(
        -0.5 * hidden * hidden
    )


def tree_add(left_tree, right_tree):
    return tuple((left_item + right_item for left_item, right_item in zip(left_tree, right_tree)))


def plain_on_device(inputs, offsets, w_query, w_kv, w_out, w_up, w_down, b_up, vectors, b_kv, cotangent):
    micro_count = inputs.shape[0]
    local_rows = inputs.shape[2]
    model_width = inputs.shape[3]
    seqlen = local_rows * lax.axis_size("seq")
    key_block = math.gcd(seqlen, 512)
    first_row = lax.axis_index("seq") * local_rows
    blocks_used = (first_row + local_rows + key_block - 1) // key_block
    row_ids = first_row + jnp.arange(local_rows, dtype=jnp.int32)
    half_rot = ROT // 2
    frequency = jnp.power(10000.0, -jnp.arange(half_rot, dtype=jnp.float32) * (2.0 / ROT))
    kv_bias = b_kv.astype(jnp.float32)
    results = []
    input_grads = []
    totals = None
    kv_bias_total = jnp.zeros(b_kv.shape, jnp.float32)
    for micro_index in range(micro_count):
        values_in = inputs[micro_index, 0].astype(jnp.float32)
        row_offsets = offsets[micro_index, 0]
        upstream = cotangent[micro_index, 0]
        upstream_f = upstream.astype(jnp.float32)
        angle = (row_offsets.astype(jnp.float32) * 0.25)[:, None] * frequency[None, :]
        cosine = jnp.cos(angle)
        sine_part = jnp.sin(angle)
        gathered = (
            lax.all_gather(w_query, ("dp", "seq"), axis=0, tiled=True),
            lax.all_gather(w_kv, ("dp", "seq"), axis=0, tiled=True),
            lax.all_gather(w_out, ("dp", "seq"), axis=0, tiled=True),
            lax.all_gather(w_up, ("dp", "seq"), axis=0, tiled=True),
            lax.all_gather(w_down, ("dp", "seq"), axis=0, tiled=True),
            lax.all_gather(b_up, ("dp", "seq"), axis=0, tiled=True),
            lax.all_gather(vectors, ("dp", "seq"), axis=1, tiled=True),
        )
        query_full, kv_full, out_full, up_full, down_full, up_bias, vector_full = gathered
        vector_f = vector_full.astype(jnp.float32)
        normed1, inverse1 = normalize(values_in)
        hidden1 = (normed1 * vector_f[0] + vector_f[1]).astype(jnp.bfloat16)
        query_pre = jnp.dot(hidden1, query_full, preferred_element_type=jnp.float32) + vector_f[4]
        kv_pre = jnp.dot(hidden1, kv_full, preferred_element_type=jnp.float32) + kv_bias
        queries = rotate(
            query_pre.reshape(local_rows, H, HD), cosine[:, None, :], sine_part[:, None, :]
        ).astype(jnp.bfloat16)
        shared_local = jnp.concatenate(
            [rotate(kv_pre[:, :HD], cosine, sine_part), kv_pre[:, HD:]], axis=1
        ).astype(jnp.bfloat16)
        shared = lax.all_gather(shared_local, "seq", axis=0, tiled=True)

        def block_scores(number):
            start_row = number * key_block
            key_piece = lax.dynamic_slice_in_dim(shared, start_row, key_block, 0)
            columns = start_row + jnp.arange(key_block, dtype=jnp.int32)
            allowed = (columns[None, :] <= row_ids[:, None]) & (
                row_ids[:, None] - columns[None, :] <= row_offsets[:, None]
            )
            scores = (
                jnp.einsum(
                    "rhd,kd->hrk", queries, key_piece[:, :HD], preferred_element_type=jnp.float32
                )
                * 0.125
            )
            return (jnp.where(allowed[None], scores, masked_score), key_piece)

        def max_step(number, state_pair):
            running_top, denominator = state_pair
            scores, key_piece = block_scores(number)
            new_top = jnp.maximum(running_top, jnp.max(scores, axis=-1))
            denominator = denominator * jnp.exp(running_top - new_top) + jnp.sum(
                jnp.exp(scores - new_top[..., None]), axis=-1
            )
            return (new_top, denominator)

        start_top = jnp.full((H, local_rows), masked_score, jnp.float32)
        running_top, denominator = lax.fori_loop(
            0, blocks_used, max_step, (start_top, jnp.zeros((H, local_rows), jnp.float32))
        )
        log_total = running_top + jnp.log(denominator)

        def value_step(number, accumulated):
            scores, key_piece = block_scores(number)
            soft_weights = jnp.exp(scores - log_total[..., None]).astype(jnp.bfloat16)
            return accumulated + jnp.einsum(
                "hrk,kd->rhd", soft_weights, key_piece[:, HD:], preferred_element_type=jnp.float32
            )

        attended_f = lax.fori_loop(
            0, blocks_used, value_step, jnp.zeros((local_rows, H, HD), jnp.float32)
        )
        attended = attended_f.reshape(local_rows, model_width).astype(jnp.bfloat16)
        attn_out = jnp.dot(attended, out_full, preferred_element_type=jnp.float32) + vector_f[5]
        normed2, inverse2 = normalize(values_in)
        hidden2 = (normed2 * vector_f[2] + vector_f[3]).astype(jnp.bfloat16)
        hidden_up = jnp.dot(hidden2, up_full, preferred_element_type=jnp.float32) + up_bias.astype(
            jnp.float32
        )
        activated = jax.nn.gelu(hidden_up, approximate=False).astype(jnp.bfloat16)
        mlp_out = jnp.dot(activated, down_full, preferred_element_type=jnp.float32) + vector_f[6]
        results.append((values_in + attn_out + mlp_out).astype(jnp.bfloat16))
        regathered = (
            lax.all_gather(w_query, ("dp", "seq"), axis=0, tiled=True),
            lax.all_gather(w_kv, ("dp", "seq"), axis=0, tiled=True),
            lax.all_gather(w_out, ("dp", "seq"), axis=0, tiled=True),
            lax.all_gather(w_up, ("dp", "seq"), axis=0, tiled=True),
            lax.all_gather(w_down, ("dp", "seq"), axis=0, tiled=True),
            lax.all_gather(b_up, ("dp", "seq"), axis=0, tiled=True),
            lax.all_gather(vectors, ("dp", "seq"), axis=1, tiled=True),
        )
        query_back, kv_back, out_back, up_back, down_back, up_bias_back, vector_back = regathered
        vector_back_f = vector_back.astype(jnp.float32)
        grad_w_down = jnp.einsum(
            "rf,rd->fd", activated, upstream, preferred_element_type=jnp.float32
        )
        d_act = jnp.einsum("rd,fd->rf", upstream, down_back, preferred_element_type=jnp.float32)
        d_hidden = (d_act * gelu_slope(hidden_up)).astype(jnp.bfloat16)
        grad_w_up = jnp.einsum("rd,rf->df", hidden2, d_hidden, preferred_element_type=jnp.float32)
        grad_b_up = jnp.sum(d_hidden.astype(jnp.float32), axis=0)
        d_normed2 = jnp.einsum("rf,df->rd", d_hidden, up_back, preferred_element_type=jnp.float32)
        grad_w_out = jnp.einsum("rd,re->de", attended, upstream, preferred_element_type=jnp.float32)
        d_attended = (
            jnp.einsum("re,de->rd", upstream, out_back, preferred_element_type=jnp.float32)
            .astype(jnp.bfloat16)
            .reshape(local_rows, H, HD)
        )

        def delta_step(number, accumulated):
            scores, key_piece = block_scores(number)
            soft_probs = jnp.exp(scores - log_total[..., None])
            d_probs = jnp.einsum(
                "rhd,kd->hrk", d_attended, key_piece[:, HD:], preferred_element_type=jnp.float32
            )
            return accumulated + jnp.sum(soft_probs * d_probs, axis=-1)

        delta = lax.fori_loop(0, blocks_used, delta_step, jnp.zeros((H, local_rows), jnp.float32))

        def grad_step(number, state_pair):
            d_query_rot, d_shared_all = state_pair
            start_row = number * key_block
            scores, key_piece = block_scores(number)
            soft_probs = jnp.exp(scores - log_total[..., None])
            d_probs = jnp.einsum(
                "rhd,kd->hrk", d_attended, key_piece[:, HD:], preferred_element_type=jnp.float32
            )
            d_scores = (soft_probs * (d_probs - delta[..., None])).astype(jnp.bfloat16)
            d_query_rot = (
                d_query_rot
                + jnp.einsum(
                    "hrk,kd->rhd", d_scores, key_piece[:, :HD], preferred_element_type=jnp.float32
                )
                * 0.125
            )
            d_keys = (
                jnp.einsum("hrk,rhd->kd", d_scores, queries, preferred_element_type=jnp.float32)
                * 0.125
            )
            d_values = jnp.einsum(
                "hrk,rhd->kd",
                soft_probs.astype(jnp.bfloat16),
                d_attended,
                preferred_element_type=jnp.float32,
            )
            current = lax.dynamic_slice_in_dim(d_shared_all, start_row, key_block, 0)
            d_shared_all = lax.dynamic_update_slice_in_dim(
                d_shared_all, current + jnp.concatenate([d_keys, d_values], axis=1), start_row, 0
            )
            return (d_query_rot, d_shared_all)

        d_query_rot, d_shared_all = lax.fori_loop(
            0,
            blocks_used,
            grad_step,
            (jnp.zeros((local_rows, H, HD), jnp.float32), jnp.zeros((seqlen, 2 * HD), jnp.float32)),
        )
        d_shared_mine = lax.psum_scatter(
            d_shared_all.astype(jnp.bfloat16), "seq", scatter_dimension=0, tiled=True
        ).astype(jnp.float32)
        d_shared = jnp.concatenate(
            [rotate(d_shared_mine[:, :HD], cosine, -sine_part), d_shared_mine[:, HD:]], axis=1
        ).astype(jnp.bfloat16)
        d_queries = (
            rotate(d_query_rot, cosine[:, None, :], -sine_part[:, None, :])
            .reshape(local_rows, model_width)
            .astype(jnp.bfloat16)
        )
        grad_w_query = jnp.einsum(
            "rd,re->de", hidden1, d_queries, preferred_element_type=jnp.float32
        )
        grad_w_kv = jnp.einsum("rd,rc->dc", hidden1, d_shared, preferred_element_type=jnp.float32)
        kv_bias_total = kv_bias_total + jnp.sum(d_shared.astype(jnp.float32), axis=0)
        d_normed1 = jnp.einsum(
            "re,de->rd", d_queries, query_back, preferred_element_type=jnp.float32
        ) + jnp.einsum("rc,dc->rd", d_shared, kv_back, preferred_element_type=jnp.float32)
        upstream_sum = jnp.sum(upstream_f, axis=0)
        grad_vectors = jnp.stack(
            [
                jnp.sum(d_normed1 * normed1, axis=0),
                jnp.sum(d_normed1, axis=0),
                jnp.sum(d_normed2 * normed2, axis=0),
                jnp.sum(d_normed2, axis=0),
                jnp.sum(d_queries.astype(jnp.float32), axis=0),
                upstream_sum,
                upstream_sum,
            ]
        )
        input_grads.append(
            upstream_f
            + norm_back(d_normed1, normed1, inverse1, vector_back_f[0])
            + norm_back(d_normed2, normed2, inverse2, vector_back_f[2])
        )
        shares = (
            lax.psum_scatter(grad_w_query, ("dp", "seq"), scatter_dimension=0, tiled=True),
            lax.psum_scatter(grad_w_kv, ("dp", "seq"), scatter_dimension=0, tiled=True),
            lax.psum_scatter(grad_w_out, ("dp", "seq"), scatter_dimension=0, tiled=True),
            lax.psum_scatter(grad_w_up, ("dp", "seq"), scatter_dimension=0, tiled=True),
            lax.psum_scatter(grad_w_down, ("dp", "seq"), scatter_dimension=0, tiled=True),
            lax.psum_scatter(grad_b_up, ("dp", "seq"), scatter_dimension=0, tiled=True),
            lax.psum_scatter(grad_vectors, ("dp", "seq"), scatter_dimension=1, tiled=True),
        )
        totals = shares if totals is None else tree_add(totals, shares)
    kv_bias_grad = lax.psum(kv_bias_total, ("dp", "seq"))
    return (
        jnp.stack(results)[:, None],
        jnp.stack(input_grads)[:, None],
        totals[0],
        totals[1],
        totals[2],
        totals[3],
        totals[4],
        totals[5],
        totals[6],
        kv_bias_grad,
    )


MESH = pl.DeviceIdType.MESH
NT = (((1,), (1,)), ((), ()))
VM = pl.BlockSpec(memory_space=pltpu.VMEM)
HBM = pl.BlockSpec(memory_space=pl.ANY)
GROUP = 6
KEYS = 512
MINI = 256
scale_log2 = 0.125 * 1.4426950408889634


def dot(left, right):
    return jnp.dot(left, right, preferred_element_type=jnp.float32)


def dot_nt(left, right):
    return lax.dot_general(left, right, NT, preferred_element_type=jnp.float32)


def bf(values):
    return values.astype(jnp.bfloat16)


def f32(values):
    return values.astype(jnp.float32)


def rotate_rows(block, cosine, sine_part):
    half_rot = ROT // 2
    first, second = block[:half_rot], block[half_rot:ROT]
    return jnp.concatenate(
        [first * cosine - second * sine_part, second * cosine + first * sine_part, block[ROT:]],
        axis=0,
    )


def here():
    return lax.axis_index("dp"), lax.axis_index("seq")


def greet(targets):
    barrier = pltpu.get_barrier_semaphore()
    for target in targets:
        pl.semaphore_signal(barrier, inc=1, device_id=target, device_id_type=MESH)
    pl.semaphore_wait(barrier, len(targets))


def remote(source, target, send, recv, device):
    return pltpu.make_async_remote_copy(
        src_ref=source,
        dst_ref=target,
        send_sem=send,
        recv_sem=recv,
        device_id=device,
        device_id_type=MESH,
    )


class Gather:
    def __init__(self, shard, slabs, halves, send, recv):
        self.shard, self.slabs, self.halves, self.send, self.recv = shard, slabs, halves, send, recv
        self.dp, self.seq = here()
        self.sent = []

    def index(self, dp_flip, z_flip, core_flip=0):
        return (self.dp ^ dp_flip) * 8 + (self.seq ^ (2 * z_flip + core_flip))

    def part(self, slab, half):
        rows, columns = half
        return self.slabs.at[slab, rows, columns]

    def start(self, number, source, target, device):
        remote(source, target, self.send.at[number], self.recv.at[number], device).start()
        self.sent.append(number)

    def arrived(self, number, target):
        remote(target, target, self.send.at[number], self.recv.at[number], (self.dp, self.seq ^ 1)).wait_recv()

    def along_z(self, flip):
        self.start(flip - 1, self.shard, self.slabs.at[self.index(0, 0)], (self.dp, self.seq ^ (2 * flip)))

    def own(self):
        mine = self.slabs.at[self.index(0, 0)]
        self.start(3, self.shard, mine, (self.dp ^ 1, self.seq))
        self.start(7, self.shard, mine, (self.dp ^ 2, self.seq))
        self.start(19, self.shard, mine, (self.dp, self.seq ^ 1))

    def from_z(self, flip):
        piece = self.slabs.at[self.index(0, flip)]
        self.arrived(flip - 1, piece)
        self.start(3 + flip, piece, piece, (self.dp ^ 1, self.seq))
        self.start(7 + flip, piece, piece, (self.dp ^ 2, self.seq))
        if flip == 2:
            self.start(2, piece, piece, (self.dp, self.seq ^ 2))
        self.start(19 + flip, piece, piece, (self.dp, self.seq ^ 1))

    def from_xy(self, flip):
        for axis, half in ((1, 0), (2, 1)):
            number = 3 if axis == 1 else 7
            slab = self.index(axis, flip)
            piece = self.slabs.at[slab]
            self.arrived(number + flip, piece)
            cut = self.part(slab, self.halves[half])
            self.start(11 + 4 * half + flip, cut, cut, (self.dp ^ (3 - axis), self.seq))
            self.start((23 if axis == 1 else 27) + flip, piece, piece, (self.dp, self.seq ^ 1))

    def from_diagonal(self, flip):
        slab = self.index(3, flip)
        for half in (0, 1):
            self.arrived(11 + 4 * half + flip, self.part(slab, self.halves[half]))
        piece = self.slabs.at[slab]
        self.start(31 + flip, piece, piece, (self.dp, self.seq ^ 1))

    def from_core(self):
        for number, dp_flip in ((19, 0), (23, 1), (27, 2), (31, 3)):
            for flip in range(4):
                self.arrived(number + flip, self.slabs.at[self.index(dp_flip, flip, 1)])

    def finish(self):
        for number in self.sent:
            view = self.part(0, self.halves[(number - 11) // 4]) if 11 <= number < 19 else self.slabs.at[0]
            remote(view, view, self.send.at[number], self.recv.at[number], (self.dp, self.seq ^ 1)).wait_send()


def attend(
    micro, steps, row0, off_ref, q_t, do_t, kv_ref, kv_t, att_t, dq_t, dkv, pair, scaled, score_ref, weight_ref, tick
):
    cols = slice(micro * MINI, (micro + 1) * MINI)
    row_ids = row0 + lax.broadcasted_iota(jnp.int32, (1, MINI), 1)
    begin = row_ids - off_ref[micro]

    def group_step(group, carry):
        heads = [pl.ds(pl.multiple_of((group * GROUP + n) * HD, HD), HD) for n in range(GROUP)]
        for n, head in enumerate(heads):
            pair[n, :HD, :MINI] = q_t[head, cols]
            pair[n, HD:, MINI:] = do_t[head, cols]

        def score_step(step, tops):
            keys = pl.ds(pl.multiple_of(step * KEYS, KEYS), KEYS)
            block = kv_ref[micro, keys, :]
            ids = step * KEYS + lax.broadcasted_iota(jnp.int32, (KEYS, 1), 0)
            allowed = (ids <= row_ids) & (ids >= begin)
            found = []
            for n in range(GROUP):
                both = dot(block, pair[n])
                scores = jnp.where(allowed, both[:, :MINI] * scale_log2, masked_score)
                score_ref[n, keys, :MINI] = scores
                score_ref[n, keys, MINI:] = both[:, MINI:]
                found.append(jnp.maximum(tops[n], jnp.max(scores.reshape(KEYS // 8, 8, MINI), axis=0)))
            return tuple(found)

        tops = lax.fori_loop(
            0, steps, score_step, tuple(jnp.full((8, MINI), masked_score, jnp.float32) for _ in heads)
        )
        tops = [jnp.max(top, axis=0, keepdims=True) for top in tops]
        tick(micro, group, 0)

        def value_step(step, carried):
            keys = pl.ds(pl.multiple_of(step * KEYS, KEYS), KEYS)
            values = kv_t[micro, HD:, keys]
            found = []
            for n in range(GROUP):
                output, total = carried[n]
                weights = jnp.exp2(score_ref[n, keys, :MINI] - tops[n])
                total = total + jnp.sum(weights.reshape(KEYS // 8, 8, MINI), axis=0)
                weight_ref[n, keys, :] = bf(weights)
                found.append((output + dot(values, bf(weights)), total))
            return tuple(found)

        sums = lax.fori_loop(
            0,
            steps,
            value_step,
            tuple((jnp.zeros((HD, MINI), jnp.float32), jnp.zeros((8, MINI), jnp.float32)) for _ in heads),
        )
        tick(micro, group, 1)
        inverses, deltas = [], []
        for n, head in enumerate(heads):
            inverse = 1.0 / jnp.sum(sums[n][1], axis=0, keepdims=True)
            output = sums[n][0] * inverse
            upstream = f32(do_t[head, cols])
            deltas.append(jnp.sum(output * upstream, axis=0, keepdims=True))
            inverses.append(inverse)
            att_t[head, cols] = bf(output)
            scaled[n, :HD, :MINI] = bf(f32(q_t[head, cols]) * inverse)
            scaled[n, HD:, MINI:] = bf(upstream * inverse)

        def grad_step(step, carried):
            keys = pl.ds(pl.multiple_of(step * KEYS, KEYS), KEYS)
            key_block = kv_t[micro, :HD, keys]
            total = dkv[micro, keys, :]
            found = []
            for n in range(GROUP):
                weights = weight_ref[n, keys, :]
                d_scores = bf(f32(weights) * (score_ref[n, keys, MINI:] - deltas[n]))
                found.append(carried[n] + dot(key_block, d_scores))
                total = total + dot_nt(d_scores, scaled[n, :, :MINI])
                total = total + dot_nt(weights, scaled[n, :, MINI:])
            dkv[micro, keys, :] = total
            return tuple(found)

        grads = lax.fori_loop(
            0, steps, grad_step, tuple(jnp.zeros((HD, MINI), jnp.float32) for _ in heads)
        )
        for n, head in enumerate(heads):
            dq_t[head, cols] = grads[n] * (inverses[n] * 0.125)
        tick(micro, group, 2)
        return carry

    lax.fori_loop(0, H // GROUP, group_step, 0)


def spread(slabs):
    lane = lax.broadcasted_iota(jnp.int32, (8, 128), 1)
    row = lax.broadcasted_iota(jnp.int32, (8, 128), 0)
    rows = [jnp.zeros((8, 128), jnp.float32) for _ in range(6)]
    wide = [jnp.zeros((8, 128), jnp.float32) for _ in range(24)]
    for number in range(32):
        for width, target, keep in ((24, rows, row < 7), (96, wide, row == 7)):
            block, shift = divmod(number * width, 128)
            piece = jnp.where(keep, slabs[number], 0.0)
            piece = pltpu.roll(piece, shift, 1) if shift else piece
            target[block] = target[block] + jnp.where(lane >= shift, piece, 0.0)
            if shift + width > 128:
                target[block + 1] = target[block + 1] + jnp.where(lane < shift, piece, 0.0)
    return jnp.concatenate(rows, axis=1), jnp.concatenate(wide, axis=1)


def slab_order(store, block, dp_index, rows):
    for z in range(4):
        for core in range(2):
            first = (2 * z + core) * rows
            store(dp_index, core, z, bf(block[first : first + rows]))


def attention_kernel(
    x_ref, cot_ref, off_ref, wq_ref, wkv_in, wout_ref, vec_in, bup_in, bkv_ref, up_ref, down_ref,
    up_slabs, down_slabs, vec_ref, bup_ref, wkv_ref, cos_ref, sin_ref, attn_ref, dn_ref, dkv_out, grads_ref, dqsum_ref,
    small_ref, pair_ref, extra, slabs, pair_slabs, weights, out_weights, n1t_ref, q_t, do_t, att_t, dq_t, kv_ref, kv_t, dkv, pair, scaled,
    score_ref, weight_ref,
    send_a, recv_a, send_o, recv_o, send_u, recv_u, send_d, recv_d, send_kv, recv_kv, local_sem,
):
    dp, seq = here()

    def halves(shape, axis):
        middle = shape[axis] // 2
        cuts = [slice(0, middle), slice(middle, 2 * middle)]
        return tuple((cut, slice(None)) if axis == 0 else (slice(None), cut) for cut in cuts)

    gather_a = Gather(small_ref, slabs, halves(small_ref.shape, 1), send_a, recv_a)
    gather_o = Gather(pair_ref, pair_slabs, halves(pair_ref.shape, 1), send_o, recv_o)
    gather_u = Gather(up_ref, up_slabs, halves(up_ref.shape, 1), send_u, recv_u)
    gather_d = Gather(down_ref, down_slabs, halves(down_ref.shape, 0), send_d, recv_d)

    def signal():
        barrier = pltpu.get_barrier_semaphore()
        for target in friends:
            pl.semaphore_signal(barrier, inc=1, device_id=target, device_id_type=MESH)

    friends = [(dp, seq ^ 1), (dp, seq ^ 2), (dp, seq ^ 4), (dp, seq ^ 6), (dp ^ 1, seq), (dp ^ 2, seq)]
    signal()
    extra[...] = jnp.zeros_like(extra)
    extra[0:7, 0 : vec_in.shape[1]] = f32(vec_in[...])
    extra[7:8, 0 : bup_in.shape[1]] = f32(bup_in[...])
    small_ref[:, 0:128] = wkv_in[...]
    small_ref[:, 128:256] = bf(extra[...])
    pair_ref[:, 0:768] = wq_ref[...]
    pair_ref[:, 768:1536] = wout_ref[...]
    pl.semaphore_wait(pltpu.get_barrier_semaphore(), len(friends))
    for flip in (1, 2):
        gather_a.along_z(flip)
    gather_a.own()
    gather_o.along_z(1)
    gather_o.own()
    gather_u.own()
    mine = gather_a.index(0, 0)
    local_copies = [
        pltpu.make_async_copy(small_ref, slabs.at[mine], local_sem.at[0]),
        pltpu.make_async_copy(pair_ref, pair_slabs.at[mine], local_sem.at[1]),
        pltpu.make_async_copy(up_ref, up_slabs.at[mine], local_sem.at[2]),
        pltpu.make_async_copy(down_ref, down_slabs.at[mine], local_sem.at[3]),
    ]
    for copy in local_copies:
        copy.start()
    pair[...] = jnp.zeros_like(pair)
    scaled[...] = jnp.zeros_like(scaled)
    dkv[...] = jnp.zeros_like(dkv)
    rank = f32(lax.broadcasted_iota(jnp.int32, (ROT // 2, 1), 0))
    frequency = jnp.exp(rank * (-2.0 / ROT * math.log(10000.0)))
    for micro in range(2):
        cols = slice(micro * MINI, (micro + 1) * MINI)
        angle = (f32(off_ref[micro]) * 0.25) * frequency
        cos_ref[:, cols] = jnp.cos(angle)
        sin_ref[:, cols] = jnp.sin(angle)
    normed, _ = normalize(f32(x_ref[...]))
    for flip in (1, 2, 3):
        gather_a.from_z(flip)
    for flip in range(4):
        gather_a.from_xy(flip)
    gather_o.along_z(2)
    gather_o.from_z(1)
    for flip in range(4):
        gather_a.from_diagonal(flip)
    gather_o.from_xy(0)
    gather_u.along_z(1)
    gather_u.along_z(2)
    gather_a.from_core()
    local_copies[0].wait()

    vectors, wide_row = spread([f32(slabs[number, 0:8, 128:256]) for number in range(32)])
    vec_ref[...] = vectors
    bup_ref[...] = wide_row[7:8]

    def unpack(source, target, columns):
        for number in range(16):
            block = jnp.concatenate(
                [f32(source[2 * number, :, columns]), f32(source[2 * number + 1, :, columns])], axis=0
            )
            target[48 * number : 48 * number + 48, :] = bf(block)

    unpack(slabs, wkv_ref, slice(0, 128))
    hidden = bf(normed * vectors[0:1] + vectors[1:2])
    kv_pre = dot(hidden, wkv_ref[...]) + f32(bkv_ref[...])
    kv_pre_t = kv_pre.T
    cosine, sine_part = cos_ref[...], sin_ref[...]
    shared_t = bf(jnp.concatenate([rotate_rows(kv_pre_t[:HD], cosine, sine_part), kv_pre_t[HD:]], axis=0))
    shared = bf(f32(shared_t).T)
    place = pl.ds(pl.multiple_of(seq * MINI, MINI), MINI)
    kv_copies = []
    for micro in range(2):
        kv_ref[micro, place, :] = shared[micro * MINI : (micro + 1) * MINI]

    def kv_block(micro, flip):
        return kv_ref.at[micro, pl.ds(pl.multiple_of((seq ^ flip) * MINI, MINI), MINI)]

    def kv_send(micro, flip, number, device):
        block = kv_block(micro, flip)
        copy = remote(block, block, send_kv.at[micro, number], recv_kv.at[micro, number], device)
        copy.start()
        kv_copies.append(copy)

    def kv_arrived(micro, flip, number):
        block = kv_block(micro, flip)
        remote(block, block, send_kv.at[micro, number], recv_kv.at[micro, number], (dp, seq ^ 1)).wait_recv()

    def kv_start(micro):
        for flip in (1, 2, 3):
            kv_send(micro, 0, flip - 1, (dp, seq ^ (2 * flip)))
        kv_send(micro, 0, 3, (dp, seq ^ 1))

    def kv_forward(micro):
        for flip in (1, 2, 3):
            kv_arrived(micro, 2 * flip, flip - 1)
            kv_send(micro, 2 * flip, 3 + flip, (dp, seq ^ 1))

    def kv_finish(micro):
        for flip in range(4):
            kv_arrived(micro, 2 * flip + 1, 3 + flip)
        kv_t[micro] = bf(f32(kv_ref[micro]).T)

    kv_start(0)
    gather_o.from_z(2)
    gather_o.from_xy(1)
    gather_o.from_diagonal(0)
    gather_o.from_z(3)
    gather_o.from_xy(2)
    gather_o.from_diagonal(1)
    n1t_ref[...] = bf(f32(hidden).T)
    kv_forward(0)
    gather_o.from_xy(3)
    gather_d.along_z(1)
    gather_d.along_z(2)
    gather_d.own()
    gather_u.from_z(1)
    gather_u.from_xy(0)
    gather_o.from_diagonal(2)
    gather_o.from_diagonal(3)
    kv_start(1)
    kv_finish(0)
    local_copies[1].wait()
    gather_o.from_core()
    unpack(pair_slabs, weights, slice(0, 768))
    unpack(pair_slabs, out_weights, slice(768, 1536))
    query = (dot(hidden, weights[...]) + vectors[4:5]).T
    for head in range(H):
        q_t[head * HD : (head + 1) * HD, :] = bf(
            rotate_rows(query[head * HD : (head + 1) * HD], cosine, sine_part)
        )
    do_t[...] = bf(dot_nt(out_weights[...], cot_ref[...]))

    def each(name, *flips):
        def act():
            for gather in (gather_u, gather_d):
                for flip in flips:
                    getattr(gather, name)(flip)

        return act

    def then(*acts):
        def act():
            for one in acts:
                one()

        return act

    actions = [
        then(lambda: gather_d.from_z(1), lambda: gather_d.from_xy(0)),
        None,
        then(each("from_z", 2), lambda: gather_u.from_diagonal(0)),
        each("from_xy", 1),
        then(lambda: gather_d.from_diagonal(0), each("from_z", 3)),
        each("from_diagonal", 1),
        each("from_xy", 2),
        each("from_diagonal", 2),
        each("from_xy", 3),
        None,
        each("from_diagonal", 3),
        None,
    ]

    def tick(micro, group, part):
        for number in range(H // GROUP):
            act = actions[(micro * (H // GROUP) + number) * 3 + part]
            if act is not None:
                pl.when(group == number)(act)

    kv_forward(1)
    steps = lax.div((seq + 1) * MINI + KEYS - 1, KEYS)
    for micro in range(2):
        if micro == 1:
            kv_finish(1)
        attend(
            micro, steps, seq * MINI, off_ref, q_t, do_t, kv_ref, kv_t, att_t, dq_t, dkv,
            pair, scaled, score_ref, weight_ref, tick,
        )
    for micro in range(2):
        for core in range(2):
            for z in range(4):
                first = (2 * z + core) * MINI
                block = dkv[micro, first : first + MINI, :]
                scale = jnp.where(lax.broadcasted_iota(jnp.int32, (1, 2 * HD), 1) < HD, 0.125, 1.0)
                dkv_out[core, z, micro] = bf(block * scale)
    attn_ref[...] = dot(bf(f32(att_t[...]).T), out_weights[...]) + vectors[5:6]
    for head in range(H):
        dq_t[head * HD : (head + 1) * HD, :] = rotate_rows(
            dq_t[head * HD : (head + 1) * HD, :], cosine, -sine_part
        )
    d_query = bf(dq_t[...].T)
    dqsum_ref[...] = jnp.sum(f32(d_query), axis=0, keepdims=True)
    dn_ref[...] = dot_nt(d_query, weights[...])
    for block in range(4):
        rows = slice(192 * block, 192 * block + 192)

        def put_query(dp_index, core, z, piece):
            grads_ref[dp_index, core, z, :, 0:768] = piece

        def put_out(dp_index, core, z, piece):
            grads_ref[dp_index, core, z, :, 768:1536] = piece

        slab_order(put_query, dot(n1t_ref[rows, :], d_query), block, 24)
        slab_order(put_out, dot(att_t[rows, :], cot_ref[...]), block, 24)
    for gather in (gather_u, gather_d):
        gather.from_core()
    for gather in (gather_a, gather_o, gather_u, gather_d):
        gather.finish()
    for copy in kv_copies:
        copy.wait_send()
    for copy in local_copies[2:]:
        copy.wait()


def attention_call(x, cot, offsets, w_query, w_kv, w_out, vectors, b_up, b_kv, w_up, w_down):
    rows = x.shape[0]
    dma = pltpu.SemaphoreType.DMA
    out = jax.ShapeDtypeStruct
    seqlen = 8 * MINI
    b16 = jnp.bfloat16
    return pl.pallas_call(
        attention_kernel,
        out_shape=(
            out((32,) + w_up.shape, b16),
            out((32,) + w_down.shape, b16),
            out((8, 768), jnp.float32),
            out((1, 3072), jnp.float32),
            out((768, 128), b16),
            out((ROT // 2, rows), jnp.float32),
            out((ROT // 2, rows), jnp.float32),
            out((rows, 768), jnp.float32),
            out((rows, 768), jnp.float32),
            out((2, 4, 2, MINI, 2 * HD), b16),
            out((4, 2, 4, 24, 1536), b16),
            out((1, 768), jnp.float32),
        ),
        in_specs=[VM] * 9 + [HBM] * 2,
        out_specs=(HBM, HBM) + (VM,) * 10,
        scratch_shapes=[
            pltpu.VMEM((24, 256), b16),
            pltpu.VMEM((24, 1536), b16),
            pltpu.VMEM((24, 128), jnp.float32),
            pltpu.VMEM((32, 24, 256), b16),
            pltpu.VMEM((32, 24, 1536), b16),
            pltpu.VMEM((768, 768), b16),
            pltpu.VMEM((768, 768), b16),
            pltpu.VMEM((768, rows), b16),
            pltpu.VMEM((768, rows), b16),
            pltpu.VMEM((768, rows), b16),
            pltpu.VMEM((768, rows), b16),
            pltpu.VMEM((768, rows), jnp.float32),
            pltpu.VMEM((2, seqlen, 2 * HD), b16),
            pltpu.VMEM((2, 2 * HD, seqlen), b16),
            pltpu.VMEM((2, seqlen, 2 * HD), jnp.float32),
            pltpu.VMEM((GROUP, 2 * HD, 2 * MINI), b16),
            pltpu.VMEM((GROUP, 2 * HD, 2 * MINI), b16),
            pltpu.VMEM((GROUP, seqlen, 2 * MINI), jnp.float32),
            pltpu.VMEM((GROUP, seqlen, MINI), b16),
        ]
        + [dma((35,))] * 8
        + [dma((2, 7))] * 2
        + [dma((4,))],
        compiler_params=pltpu.CompilerParams(
            collective_id=0, has_side_effects=True, vmem_limit_bytes=60 << 20
        ),
        name="attention",
    )(x, cot, offsets, w_query, w_kv, w_out, vectors, b_up, b_kv, w_up, w_down)


def packed_on_device(inputs, offsets, w_query, w_kv, w_out, w_up, w_down, b_up, vectors, b_kv, cotangent):
    rows = 2 * MINI
    x = inputs.reshape(rows, 768)
    cot = cotangent.reshape(rows, 768)
    up_slabs, down_slabs, vec, bup, wkv, cosine, sine_part, attn, dn1, dkv, grads_a, dq_sum = attention_call(
        x, cot, offsets, w_query, w_kv, w_out, vectors, b_up.reshape(1, -1), b_kv.reshape(1, -1), w_up, w_down
    )
    return feed_forward(x, cot, cosine, sine_part, up_slabs, down_slabs, vec, bup, wkv, attn, dn1, dkv, grads_a, dq_sum)


class Scatter:
    def __init__(self, slabs, from_core, from_diagonal, from_xy, from_z, send, recv):
        self.slabs, self.from_core, self.from_diagonal = slabs, from_core, from_diagonal
        self.from_xy, self.from_z, self.send, self.recv = from_xy, from_z, send, recv
        self.dp, self.seq = here()
        self.core = lax.rem(self.seq, 2)
        self.z = lax.div(self.seq, 2)
        self.sent = []

    def start(self, number, source, target, device):
        copy = remote(source, target, self.send.at[number], self.recv.at[number], device)
        copy.start()
        self.sent.append(copy)

    def arrived(self, number, target):
        remote(target, target, self.send.at[number], self.recv.at[number], (self.dp, self.seq ^ 1)).wait_recv()

    def block(self, flip):
        return self.slabs.at[self.dp ^ flip, self.core]

    def to_core(self, flip):
        other = self.slabs.at[self.dp ^ flip, 1 - self.core]
        self.start(flip, other, self.from_core.at[flip], (self.dp, self.seq ^ 1))

    def add(self, block, z, terms):
        total = f32(block[z])
        for term in terms:
            total = total + f32(term)
        block[z] = bf(total)

    def diagonal(self):
        block = self.block(3)
        self.arrived(3, self.from_core.at[3])
        for half in (0, 1):
            for z in (2 * half, 2 * half + 1):
                self.add(block, z, [self.from_core[3, z]])
            self.start(4 + half, block.at[pl.ds(2 * half, 2)], self.from_diagonal.at[half], (self.dp ^ (1 + half), self.seq))

    def beside(self, axis):
        half = 2 - axis
        block = self.block(axis)
        self.arrived(axis, self.from_core.at[axis])
        self.arrived(4 + half, self.from_diagonal.at[half])
        for z in range(4):
            terms = [self.from_core[axis, z]]
            if z // 2 == half:
                terms.append(self.from_diagonal[half, z % 2])
            self.add(block, z, terms)
        self.start(5 + axis, block, self.from_xy.at[axis - 1], (self.dp ^ axis, self.seq))

    def own(self):
        block = self.block(0)
        self.arrived(0, self.from_core.at[0])
        for axis in (1, 2):
            self.arrived(5 + axis, self.from_xy.at[axis - 1])
        for z in range(4):
            self.add(block, z, [self.from_core[0, z], self.from_xy[0, z], self.from_xy[1, z]])
        for flip in (1, 2, 3):
            self.start(7 + flip, block.at[self.z ^ flip], self.from_z.at[flip - 1], (self.dp, self.seq ^ (2 * flip)))

    def total(self):
        value = f32(self.slabs[self.dp, self.core, self.z])
        for flip in (1, 2, 3):
            self.arrived(7 + flip, self.from_z.at[flip - 1])
            value = value + f32(self.from_z[flip - 1])
        return value

    def finish(self):
        for copy in self.sent:
            copy.wait_send()


def feed_kernel(
    x_ref, cot_ref, cos_ref, sin_ref, vec_ref, bup_ref, wkv_ref, attn_ref, dn_ref, dqsum_ref, dkv_in, grads_a, up_hbm, down_hbm,
    out_ref, gin_ref, gq_ref, go_ref, gu_ref, gkv_ref, gd_ref, small_out,
    up_ref, down_ref, n1t_ref, n2_ref, n2t_ref, act_ref, dh_ref, mlp_ref, dshared_ref, stats,
    a_slabs, d_slabs, u_slabs, v_slabs,
    a_core, a_diag, a_xy, a_z, d_core, d_diag, d_xy, d_z, u_core, u_diag, u_xy, u_z, v_core, v_diag, v_xy, v_z,
    dkv, dkv_core, dkv_z, small, small_in,
    send_s, recv_s, send_k, recv_k, send_m, recv_m, load_sem,
):
    dp, seq = here()
    core, z = lax.rem(seq, 2), lax.div(seq, 2)
    loads = [
        pltpu.make_async_copy(dkv_in, dkv, load_sem.at[2]),
        pltpu.make_async_copy(grads_a, a_slabs, load_sem.at[3]),
        pltpu.make_async_copy(up_hbm, up_ref, load_sem.at[0]),
        pltpu.make_async_copy(down_hbm, down_ref, load_sem.at[1]),
    ]
    for copy in loads:
        copy.start()
    greet(
        [(dp, seq ^ 1), (dp, seq ^ 2), (dp, seq ^ 4), (dp, seq ^ 6), (dp ^ 1, seq), (dp ^ 2, seq)]
    )
    scatter_a = Scatter(a_slabs, a_core, a_diag, a_xy, a_z, send_s.at[0], recv_s.at[0])
    scatter_d = Scatter(d_slabs, d_core, d_diag, d_xy, d_z, send_s.at[1], recv_s.at[1])
    scatter_u = Scatter(u_slabs, u_core, u_diag, u_xy, u_z, send_s.at[2], recv_s.at[2])
    scatter_v = Scatter(v_slabs, v_core, v_diag, v_xy, v_z, send_s.at[3], recv_s.at[3])
    kv_sent = []

    def kv_start(number, source, target, device):
        copy = remote(source, target, send_k.at[number], recv_k.at[number], device)
        copy.start()
        kv_sent.append(copy)

    def kv_arrived(number, target):
        remote(target, target, send_k.at[number], recv_k.at[number], (dp, seq ^ 1)).wait_recv()

    loads[1].wait()
    for flip in (3, 1, 2, 0):
        scatter_a.to_core(flip)
    loads[0].wait()
    kv_start(0, dkv.at[1 - core], dkv_core, (dp, seq ^ 1))
    scatter_a.diagonal()

    vectors = vec_ref[...]
    for start in range(0, 2 * MINI, MINI):
        rows = slice(start, start + MINI)
        normed, inverse = normalize(f32(x_ref[rows, :]))
        stats[rows, :] = jnp.broadcast_to(inverse, (MINI, 128))
        n1t_ref[:, rows] = bf((normed * vectors[0:1] + vectors[1:2]).T)
        second = normed * vectors[2:3] + vectors[3:4]
        n2_ref[rows, :] = bf(second)
        n2t_ref[:, rows] = bf(second.T)
    kv_arrived(0, dkv_core)
    for index in range(4):
        for micro in range(2):
            dkv[core, index, micro] = bf(f32(dkv[core, index, micro]) + f32(dkv_core[index, micro]))
    for flip in (1, 2, 3):
        kv_start(flip, dkv.at[core, z ^ flip], dkv_z.at[flip - 1], (dp, seq ^ (2 * flip)))
    scatter_a.beside(1)
    scatter_a.beside(2)
    loads[2].wait()
    loads[3].wait()

    def chunk(flip, first):
        base = (dp ^ flip) * 768

        def tile(number, carry):
            columns = pl.ds(pl.multiple_of(base + number * 256, 256), 256)
            hidden = dot(n2_ref[...], up_ref[:, columns]) + bup_ref[0:1, columns]
            d_act = dot_nt(cot_ref[...], down_ref[columns, :])
            normal = 0.5 + 0.5 * lax.erf(hidden * root_half)
            density = density_scale * jnp.exp(-0.5 * hidden * hidden)
            d_hidden = bf(d_act * (normal + hidden * density))
            act_ref[:, pl.ds(pl.multiple_of(number * 256, 256), 256)] = bf(hidden * normal)
            dh_ref[:, columns] = d_hidden
            return carry

        lax.fori_loop(0, 3, tile, 0)
        down_rows = pl.ds(pl.multiple_of(base, 768), 768)
        part = dot(act_ref[...], down_ref[down_rows, :])
        mlp_ref[...] = part if first else mlp_ref[...] + part

        grad_t = bf(f32(act_ref[...]).T)
        for number in range(4):
            grad = dot(grad_t[192 * number : 192 * number + 192], cot_ref[...])
            for half in range(2):
                d_slabs[dp ^ flip, half, number] = bf(grad[96 * half : 96 * half + 96])
        scatter_d.to_core(flip)

    def put(store, block, flip, rows):
        for index in range(4):
            for half in range(2):
                first = (2 * index + half) * rows
                store(dp ^ flip, half, index, bf(block[first : first + rows]))

    def up_block(flip, left):
        rows = pl.ds(pl.multiple_of((dp ^ flip) * 192, 192), 192)
        if left:

            def put_left(target, half, index, piece):
                u_slabs[target, half, index, :, 0:1536] = piece

            def put_kv(target, half, index, piece):
                u_slabs[target, half, index, :, 1536:1664] = piece

            put(put_left, dot(n2t_ref[rows, :], dh_ref[:, 0:1536]), flip, 24)
            put(put_kv, dot(n1t_ref[rows, :], dshared_ref[...]), flip, 24)
            scatter_u.to_core(flip)
        else:

            def put_right(target, half, index, piece):
                v_slabs[target, half, index] = piece

            put(put_right, dot(n2t_ref[rows, :], dh_ref[:, 1536:3072]), flip, 24)
            scatter_v.to_core(flip)

    chunk(3, True)
    scatter_d.diagonal()
    chunk(1, False)
    scatter_d.beside(1)
    scatter_a.own()
    for flip in (1, 2, 3):
        kv_arrived(flip, dkv_z.at[flip - 1])
    cosine, sine_part = cos_ref[...], sin_ref[...]
    for micro in range(2):
        cols = slice(micro * MINI, (micro + 1) * MINI)
        total = f32(dkv[core, z, micro])
        for flip in (1, 2, 3):
            total = total + f32(dkv_z[flip - 1, micro])
        total_t = total.T
        total_t = jnp.concatenate(
            [rotate_rows(total_t[:HD], cosine[:, cols], -sine_part[:, cols]), total_t[HD:]], axis=0
        )
        dshared_ref[cols, :] = bf(total_t.T)
    chunk(2, False)
    scatter_d.beside(2)
    chunk(0, False)
    up_block(3, True)
    up_block(1, True)
    scatter_u.diagonal()
    up_block(2, True)
    up_block(0, True)
    scatter_d.own()
    up_block(3, False)
    up_block(1, False)
    scatter_u.beside(1)
    scatter_u.beside(2)
    scatter_v.diagonal()
    up_block(2, False)
    up_block(0, False)
    zero = jnp.zeros((1, 768), jnp.float32)
    sums = [zero] * 5
    for start in range(0, 2 * MINI, 128):
        rows = slice(start, start + 128)
        values = f32(x_ref[rows, :])
        upstream = f32(cot_ref[rows, :])
        inverse = stats[rows, 0:1]
        normed = (values - jnp.mean(values, axis=-1, keepdims=True)) * inverse
        out_ref[rows, :] = bf(values + attn_ref[rows, :] + mlp_ref[rows, :] + vectors[6:7])
        first = dn_ref[rows, :] + dot_nt(dshared_ref[rows, :], wkv_ref[...])
        second = dot_nt(dh_ref[rows, :], up_ref[...])
        gin_ref[rows, :] = (
            upstream
            + norm_back(first, normed, inverse, vectors[0:1])
            + norm_back(second, normed, inverse, vectors[2:3])
        )
        news = (first * normed, first, second * normed, second, upstream)
        sums = [total + jnp.sum(new, axis=0, keepdims=True) for total, new in zip(sums, news)]
    b_up_sum = jnp.sum(f32(dh_ref[...]), axis=0, keepdims=True)
    kv_sum = jnp.sum(f32(dshared_ref[...]), axis=0, keepdims=True)
    small[0] = jnp.concatenate(
        sums[:4]
        + [dqsum_ref[...], sums[4], sums[4], zero]
        + [b_up_sum[:, 768 * n : 768 * n + 768] for n in range(4)]
        + [jnp.concatenate([kv_sum, zero[:, 128:]], axis=1)]
        + [zero] * 3,
        axis=0,
    )
    partners = [(dp, seq ^ 1), (dp, seq ^ 2), (dp, seq ^ 4), (dp ^ 1, seq), (dp ^ 2, seq)]
    small_sent = []

    def small_start(number):
        copy = remote(small.at[number], small_in.at[number], send_m.at[number], recv_m.at[number], partners[number])
        copy.start()
        small_sent.append(copy)

    def small_end(number):
        small_sent[number].wait_recv()
        small[number + 1] = small[number] + small_in[number]

    total = scatter_a.total()
    gq_ref[...] = total[:, :768]
    go_ref[...] = total[:, 768:]
    small_start(0)
    scatter_v.beside(1)
    scatter_v.beside(2)
    small_end(0)
    small_start(1)
    scatter_u.own()
    small_end(1)
    small_start(2)
    gd_ref[...] = scatter_d.total()
    scatter_v.own()
    small_end(2)
    small_start(3)
    total = scatter_u.total()
    gu_ref[:, 0:1536] = total[:, 0:1536]
    gkv_ref[...] = total[:, 1536:1664]
    small_end(3)
    small_start(4)
    small_end(4)
    small_out[...] = small[5]
    gu_ref[:, 1536:3072] = scatter_v.total()
    for scatter in (scatter_a, scatter_d, scatter_u, scatter_v):
        scatter.finish()
    for copy in kv_sent + small_sent:
        copy.wait_send()


def place_kernel(small, *refs):
    wholes, results = refs[:7], refs[7:17]
    for source, target in zip(wholes, results):
        target[...] = source[...]
    dp, seq = here()
    rows = small[0:8, :]
    shift = lax.rem(768 - 24 * (8 * dp + seq), 768)
    results[7][...] = pltpu.roll(rows, shift, 1)[0:7, 0:24]
    wide = jnp.broadcast_to(small[pl.ds(8 + dp, 1), :], (8, 768))
    shift = lax.rem(768 - 96 * seq, 768)
    results[8][...] = pltpu.roll(wide, shift, 1)[0:1, 0:96]
    results[9][...] = small[12:13, 0 : 2 * HD]


def feed_forward(x, cot, cosine, sine_part, up_slabs, down_slabs, vec, bup, wkv, attn, dn1, dkv, grads_a, dq_sum):
    rows = x.shape[0]
    dma = pltpu.SemaphoreType.DMA
    out = jax.ShapeDtypeStruct
    b16 = jnp.bfloat16
    shapes = ((24, 1536), (96, 768), (24, 1664), (24, 1536))
    buffers = [pltpu.VMEM((4, 2, 4) + shape, b16) for shape in shapes]
    for shape in shapes:
        for lead in ((4, 4), (2, 2), (2, 4), (3,)):
            buffers.append(pltpu.VMEM(lead + shape, b16))
    out_rows, g_in, g_query, g_out, g_up, g_kv, g_down, small = pl.pallas_call(
        feed_kernel,
        out_shape=(
            out((rows, 768), b16),
            out((rows, 768), jnp.float32),
            out((24, 768), jnp.float32),
            out((24, 768), jnp.float32),
            out((24, 3072), jnp.float32),
            out((24, 128), jnp.float32),
            out((96, 768), jnp.float32),
            out((16, 768), jnp.float32),
        ),
        in_specs=[VM] * 10 + [HBM] * 4,
        out_specs=(VM,) * 8,
        scratch_shapes=[
            pltpu.VMEM((768, 3072), b16),
            pltpu.VMEM((3072, 768), b16),
            pltpu.VMEM((768, rows), b16),
            pltpu.VMEM((rows, 768), b16),
            pltpu.VMEM((768, rows), b16),
            pltpu.VMEM((rows, 768), b16),
            pltpu.VMEM((rows, 3072), b16),
            pltpu.VMEM((rows, 768), jnp.float32),
            pltpu.VMEM((rows, 2 * HD), b16),
            pltpu.VMEM((rows, 128), jnp.float32),
        ]
        + buffers
        + [
            pltpu.VMEM((2, 4, 2, MINI, 2 * HD), b16),
            pltpu.VMEM((4, 2, MINI, 2 * HD), b16),
            pltpu.VMEM((3, 2, MINI, 2 * HD), b16),
            pltpu.VMEM((6, 16, 768), jnp.float32),
            pltpu.VMEM((5, 16, 768), jnp.float32),
            dma((4, 11)),
            dma((4, 11)),
            dma((4,)),
            dma((4,)),
            dma((5,)),
            dma((5,)),
            dma((4,)),
        ],
        compiler_params=pltpu.CompilerParams(
            collective_id=1, has_side_effects=True, vmem_limit_bytes=63 << 20
        ),
        name="feed_forward",
    )(
        x, cot, cosine, sine_part, vec, bup, wkv, attn, dn1, dq_sum, dkv, grads_a,
        up_slabs.reshape(768, 3072), down_slabs.reshape(3072, 768),
    )
    wholes = (out_rows, g_in, g_query, g_kv, g_out, g_up, g_down)
    like = tuple(out(one.shape, one.dtype) for one in wholes)
    results = pl.pallas_call(
        place_kernel,
        out_shape=like + (out((7, 24), jnp.float32), out((1, 96), jnp.float32), out((1, 2 * HD), jnp.float32)),
        in_specs=[VM] * (1 + len(wholes)),
        out_specs=(VM,) * (3 + len(wholes)),
        compiler_params=pltpu.CompilerParams(vmem_limit_bytes=62 << 20),
        name="place",
    )(small, *wholes)
    out_rows, g_in, g_query, g_kv, g_out, g_up, g_down, g_vectors, g_b_up, g_b_kv = results
    return (
        out_rows.reshape(2, 1, MINI, 768), g_in.reshape(2, 1, MINI, 768), g_query, g_kv, g_out,
        g_up, g_down, g_b_up.reshape(-1), g_vectors, g_b_kv.reshape(-1),
    )


def solution(mesh):
    packed = mesh.shape["dp"] == 4 and mesh.shape["seq"] == 8
    on_device = packed_on_device if packed else plain_on_device

    in_specs = (
        P(None, "dp", "seq", None),
        P(None, "dp", "seq"),
        P(("dp", "seq"), None),
        P(("dp", "seq"), None),
        P(("dp", "seq"), None),
        P(("dp", "seq"), None),
        P(("dp", "seq"), None),
        P(("dp", "seq")),
        P(None, ("dp", "seq")),
        P(),
        P(None, "dp", "seq", None),
    )
    out_specs = (
        P(None, "dp", "seq", None),
        P(None, "dp", "seq", None),
        P(("dp", "seq"), None),
        P(("dp", "seq"), None),
        P(("dp", "seq"), None),
        P(("dp", "seq"), None),
        P(("dp", "seq"), None),
        P(("dp", "seq")),
        P(None, ("dp", "seq")),
        P(),
    )
    return jax.shard_map(
        on_device, mesh=mesh, in_specs=in_specs, out_specs=out_specs, check_vma=False
    )
```
